32 devices in a mesh: tm: 8 (over z, y), batch: 4 (over x, core).
Axes of the slice: x: 2, y: 2, z: 4, core: 2. Of those that a mesh axis runs over, the one named last changes fastest.
Arguments:
- audio: float32 [4, 61440], P(None, ('tm', 'batch')), may hold values from -6 to 6
- lengths: int32 [4], replicated, may hold values from 15360 to 61440
- kernel0: float32 [10, 512], replicated, may hold values from -2 to 2
- kernel1: bfloat16 [1536, 512], replicated, may hold values from -0.15625 to 0.15625
- kernel2: bfloat16 [1536, 512], replicated, may hold values from -0.15625 to 0.15625
- conv_bias: float32 [3, 512], replicated, may hold values from -3 to 3
- norm_gain: float32 [3, 512], replicated, may hold values from 0.25 to 1.75
- norm_shift: float32 [3, 512], replicated, may hold values from -2 to 2
- cotangent: bfloat16 [4, 3072, 512], P('batch', 'tm'), may hold values from -6 to 6
- left_prev: float32 [64, 192, 192], P('tm'), may hold values from -0.4 to 2.4, as said below
- right_prev: float32 [64, 128, 128], P('tm'), may hold values from -0.4 to 2.4, as said below
Outputs:
- frames: bfloat16 [4, 3072, 512], P('batch', 'tm')
- left_stat: float32 [64, 192, 192], P('tm')
- right_stat: float32 [64, 128, 128], P('tm')
The draws below stay inside these ranges and needn't reach their ends.
Inputs may be any that keep to these rules, and one draw needn't show every extreme that they name: `left_prev`: symmetric running statistics of earlier steps. `right_prev`: symmetric running statistics of earlier steps.
All inputs are finite; a program needn't handle non-finite values.
Results may differ from the reference program's by a relative error of at most 0.0048.
The reference program's roundings to bfloat16 on the way count: a program that leaves them out, or rounds other values in their place, can miss the bound.
Values may be sent and summed in bfloat16 or wider, within the bound.
No kernel may reach another device: no remote copies, remote signals or barrier semaphores. Data moves between devices by JAX's collectives and lax.ppermute only.
A program may use at most 64 MiB of HBM per device.

```python
import math
import jax
import jax.numpy as jnp
from jax import lax

C = 512
BR = 192
BC = 128
RECS = 4
NF = 3072
NS = 61440
BLOCKS = 64


def symmetric_stat(key, number, order):
    noise_key, diag_key = jax.random.split(key)
    noise = 0.1 * jnp.clip(jax.random.normal(noise_key, (number, order, order), jnp.float32), -4.0, 4.0)
    symmetric = 0.5 * (noise + jnp.swapaxes(noise, 1, 2))
    diagonal = jnp.exp(jax.random.uniform(diag_key, (number, order), jnp.float32, math.log(0.5), math.log(2.0)))
    return symmetric + diagonal[:, :, None] * jnp.eye(order, dtype=jnp.float32)


def draw_left_prev(key, part):
    return symmetric_stat(jax.random.fold_in(key, 11), BLOCKS, BR)


def draw_right_prev(key, part):
    return symmetric_stat(jax.random.fold_in(key, 23), BLOCKS, BC)


def plant(array, own_key, least, largest):
    longest = array.shape.index(max(array.shape))
    spots = []
    for shift in (0, 1):
        where = [jax.random.randint(jax.random.fold_in(own_key, axis), (), 0, length) for axis, length in enumerate(array.shape)]
        where[longest] = (where[longest] + shift) % array.shape[longest]
        spots.append(tuple(where))
    return array.at[spots[0]].set(least).at[spots[1]].set(largest)


def shard_levels(rng, shape, shards, least, top_value):
    loudness, own = 1.0, jax.random.fold_in(rng, 6)
    for axis_at, parts in shards:
        steps = jnp.exp(jax.random.uniform(jax.random.fold_in(own, axis_at), (parts,), jnp.float32, least / len(shards), top_value / len(shards)))
        loudness = loudness * jnp.repeat(steps, shape[axis_at] // parts).reshape([-1 if axis == axis_at else 1 for axis in range(len(shape))])
    return loudness


def scatter_about(own_key, shape, scale, limit, pieces=(), held_as=jnp.bfloat16):
    loudness = shard_levels(own_key, shape, pieces, -0.22, 0.18) if pieces else 1.0
    array = jax.random.normal(own_key, shape, jnp.float32) * scale * loudness
    return jnp.minimum(jnp.maximum(array, -limit), limit).astype(held_as)


def setup_inputs(seed: int = 0) -> dict:
    streams_of = jax.random.split(jax.random.key(seed), 12)
    audio = scatter_about(streams_of[0], (RECS, NS), 1.0, 6.0, ((1, 32),), jnp.float32)
    lengths = plant(jax.random.randint(streams_of[1], (RECS,), NS // 4, NS + 1), jax.random.fold_in(streams_of[1], 1), NS // 4, NS).astype(jnp.int32)
    kernel0 = scatter_about(streams_of[2], (10, C), 10 ** -0.5, 2.0, (), jnp.float32)
    kernel1 = scatter_about(streams_of[3], (3 * C, C), (3 * C) ** -0.5, 0.15625)
    kernel2 = scatter_about(streams_of[4], (3 * C, C), (3 * C) ** -0.5, 0.15625)
    conv_bias = scatter_about(streams_of[5], (3, C), 0.5, 3.0, (), jnp.float32)
    norm_gain = jnp.clip(1.0 + 0.15 * jax.random.normal(streams_of[6], (3, C), jnp.float32), 0.25, 1.75)
    norm_shift = scatter_about(streams_of[7], (3, C), 0.3, 2.0, (), jnp.float32)
    cotangent = scatter_about(streams_of[8], (RECS, NF, C), 1.0, 6.0, ((0, 4), (1, 8)))
    left_prev = draw_left_prev(jax.random.fold_in(streams_of[11], 71), 0)
    right_prev = draw_right_prev(jax.random.fold_in(streams_of[11], 71), 0)
    return {"audio": audio, "lengths": lengths, "kernel0": kernel0, "kernel1": kernel1, "kernel2": kernel2, "conv_bias": conv_bias, "norm_gain": norm_gain, "norm_shift": norm_shift, "cotangent": cotangent, "left_prev": left_prev, "right_prev": right_prev}


EPS = 1e-05
BETA = 0.95

def norm_act(preact, offset, scaling, moving):
    shifted = preact + offset
    average = lax.optimization_barrier(jnp.mean(shifted, -1, keepdims=True))
    centred = shifted - average
    spread = lax.optimization_barrier(jnp.mean(centred * centred, -1, keepdims=True))
    normalized = centred * lax.rsqrt(spread + EPS)
    return jax.nn.gelu(normalized * scaling + moving, approximate=False)

def sample_taps(samples, rows):
    leading = samples.shape[:-1]
    opening = samples[..., :5 * rows].reshape(leading + (rows, 5))
    second = samples[..., 5:5 * rows + 5].reshape(leading + (rows, 5))
    return jnp.concatenate([opening, second], -1)

def frame_windows(source, rows):
    leading = source.shape[:-2]
    channels = source.shape[-1]
    paired = source[..., :2 * rows, :].reshape(leading + (rows, 2 * channels))
    following = source[..., 2:2 * rows + 1:2, :]
    return jnp.concatenate([paired, following], -1)

def to_blocks(gradient):
    rows_all, cols_all = gradient.shape
    split = gradient.reshape(rows_all // BR, BR, cols_all // BC, BC)
    return jnp.transpose(split, (0, 2, 1, 3)).reshape(-1, BR, BC)

def reference(audio, lengths, kernel0, kernel1, kernel2, conv_bias, norm_gain, norm_shift, cotangent, left_prev, right_prev):
    scale = 1.0 / math.sqrt(NF)
    channels = kernel1.shape[1]

    def layer_map(layer_index):

        def mapping(preact):
            return norm_act(preact, conv_bias[layer_index], norm_gain[layer_index], norm_shift[layer_index])
        return mapping

    def one_recording(inputs):
        samples_row, length, cot_row = inputs
        total = samples_row.shape[0]
        rows_zero = total // 5
        rows_one = rows_zero // 2
        rows_two = rows_one // 2
        positions = jnp.arange(total, dtype=jnp.int32)
        masked = jnp.where(positions < length, samples_row, jnp.zeros_like(samples_row))
        padded = jnp.concatenate([masked, jnp.zeros((5,), masked.dtype)])
        preact0 = jnp.einsum('nt,tc->nc', sample_taps(padded, rows_zero), kernel0, precision=lax.Precision.HIGHEST)
        act_zero = layer_map(0)(preact0).astype(jnp.bfloat16)
        zero_frame = jnp.zeros((1, channels), jnp.bfloat16)
        win_zero = frame_windows(jnp.concatenate([act_zero, zero_frame], 0), rows_one)
        preact1 = jnp.dot(win_zero, kernel1, preferred_element_type=jnp.float32)
        act_one, back_one = jax.vjp(layer_map(1), preact1)
        win_one = frame_windows(jnp.concatenate([act_one.astype(jnp.bfloat16), zero_frame], 0), rows_two)
        preact2 = jnp.dot(win_one, kernel2, preferred_element_type=jnp.float32)
        act_two, back_two = jax.vjp(layer_map(2), preact2)
        valid = (jnp.arange(rows_two, dtype=jnp.int32) < length // 20)[:, None]
        frames_row = jnp.where(valid, act_two, jnp.zeros_like(act_two)).astype(jnp.bfloat16)
        upstream = jnp.where(valid, cot_row.astype(jnp.float32) * scale, jnp.zeros_like(act_two))
        dpre_two = back_two(upstream)[0].astype(jnp.bfloat16)
        grad_two = jnp.dot(win_one.T, dpre_two, preferred_element_type=jnp.float32)
        dwin = jnp.dot(dpre_two, kernel2.T, preferred_element_type=jnp.float32)
        paired = dwin[:, :2 * channels].reshape(rows_two, 2, channels)
        lower = jnp.concatenate([jnp.zeros((1, channels), jnp.float32), dwin[:-1, 2 * channels:]], 0)
        d_one = jnp.stack([paired[:, 0] + lower, paired[:, 1]], 1).reshape(rows_one, channels)
        dpre_one = back_one(d_one)[0].astype(jnp.bfloat16)
        grad_one = jnp.dot(win_zero.T, dpre_one, preferred_element_type=jnp.float32)
        return (frames_row, grad_one, grad_two)
    frames, grads_one, grads_two = lax.map(one_recording, (audio, lengths, cotangent))
    blocks = jnp.concatenate([to_blocks(lax.optimization_barrier(jnp.sum(grads_one, 0))), to_blocks(lax.optimization_barrier(jnp.sum(grads_two, 0)))], 0)
    left_stat = BETA * left_prev + (1.0 - BETA) * jnp.einsum('bik,bjk->bij', blocks, blocks, precision=lax.Precision.HIGHEST)
    right_stat = BETA * right_prev + (1.0 - BETA) * jnp.einsum('bki,bkj->bij', blocks, blocks, precision=lax.Precision.HIGHEST)
    return (frames, left_stat, right_stat)
```

```python
import functools
import math

import jax
import jax.numpy as jnp
from jax import lax
from jax.experimental import pallas as pl
from jax.experimental.pallas import tpu as pltpu
from jax.sharding import PartitionSpec as P

BR = 192
BC = 128
EPS = 1e-05
BETA = 0.95
AXES = ("tm", "batch")
F32 = jnp.float32
BF16 = jnp.bfloat16
VMEM_LIMIT = 50 * 1024 * 1024
CH = 16
TAIL = 16

VM = pl.BlockSpec(memory_space=pltpu.VMEM)
SM = pl.BlockSpec(memory_space=pltpu.SMEM)


def params():
    return pltpu.CompilerParams(vmem_limit_bytes=VMEM_LIMIT)


def cost(flops, nbytes, trans=0):
    return pl.CostEstimate(flops=flops, bytes_accessed=nbytes, transcendentals=trans)


def sds(shape, dtype):
    return jax.ShapeDtypeStruct(shape, dtype)


def normal_cdf(z):
    bell = jnp.exp(z * z * -0.5)
    t = 1.0 / (1.0 + jnp.abs(z) * (0.3275911 / math.sqrt(2.0)))
    poly = t * (0.5 * 1.061405429) + (0.5 * -1.453152027)
    poly = poly * t + (0.5 * 1.421413741)
    poly = poly * t + (0.5 * -0.284496736)
    poly = poly * t + (0.5 * 0.254829592)
    q = poly * t * bell
    return jnp.where(z < 0.0, q, 1.0 - q), bell


INV_SQRT_2PI = 1.0 / math.sqrt(2.0 * math.pi)


def split3(x):
    hi = x.astype(BF16).astype(F32)
    rest = x - hi
    mid = rest.astype(BF16).astype(F32)
    return hi, mid, rest - mid


def prep_kernel(k0_ref, bias_ref, w_ref, wide):
    channels = k0_ref.shape[1]
    k0 = k0_ref[...]
    k0 = k0 - jnp.mean(k0, -1, keepdims=True)
    bias = bias_ref[0:1, :]
    bias = bias - jnp.mean(bias, -1, keepdims=True)
    parts = split3(k0)
    bparts = split3(bias)
    wide[...] = jnp.zeros_like(wide)
    for block, part in enumerate((0, 1, 2, 0, 1, 0)):
        for g in range(4):
            cols = pl.ds(g * channels, channels)
            wide[pl.ds(block * 32 + 5 * g, 10), cols] = parts[part]
            if block < 3:
                wide[pl.ds(block * 32 + 31, 1), cols] = bparts[part]
    w_ref[...] = wide[...].astype(BF16)


def prep(kernel0, conv_bias):
    channels = kernel0.shape[1]
    return pl.pallas_call(
        prep_kernel,
        out_shape=sds((256, 4 * channels), BF16),
        in_specs=[VM, VM],
        out_specs=VM,
        scratch_shapes=[pltpu.VMEM((256, 4 * channels), F32)],
        compiler_params=params(),
        cost_estimate=cost(4 * 256 * 2048, 1 << 20),
        name="prep",
    )(kernel0, conv_bias)


def dot(a, b):
    return lax.dot_general(a, b, (((1,), (0,)), ((), ())), preferred_element_type=F32)


def dot_tn(a, b):
    return lax.dot_general(a, b, (((0,), (0,)), ((), ())), preferred_element_type=F32)


def dot_nt(a, b):
    return lax.dot_general(a, b, (((1,), (1,)), ((), ())), preferred_element_type=F32)


def put_gradient(core, keep_ref, send_ref, pairs, chunk):
    half = keep_ref.shape[-1] * 2
    width = keep_ref.shape[-1]
    for which, out in ((core, keep_ref), (1 - core, send_ref)):
        start = pl.multiple_of(which * half, half)
        for row in range(keep_ref.shape[1]):
            total = None
            for a_ref, offset, d_ref in pairs:
                groups = d_ref.shape[0]
                a = a_ref[0:groups, offset + row * chunk : offset + (row + 1) * chunk]
                piece = dot_tn(a, d_ref[:, pl.ds(start, half)])
                total = piece if total is None else total + piece
            out[0, row] = total[:, :width].astype(out.dtype)
            out[1, row] = total[:, width:].astype(out.dtype)


def forward_kernel(
    groups,
    scale,
    info,
    p0,
    p1,
    p2,
    p3,
    edge_ref,
    w0_ref,
    k1_ref,
    k2_ref,
    bias_ref,
    gain_ref,
    shift_ref,
    cot_ref,
    cotprev_ref,
    frames_ref,
    keep_ref,
    send_ref,
    a0_ref,
    hat_ref,
    slope_ref,
    rstd_ref,
    d2_ref,
    samples,
    pre0,
    pre1,
    pre2,
    a1_ref,
    ahead,
    cotall,
    d2own,
):
    rows = groups + TAIL
    channels = k1_ref.shape[1]
    length = info[0]
    base = info[1]
    total = info[2]
    me = info[3]
    core = info[4]
    count = rows // CH
    is_last = base + groups >= total

    samples[...] = jnp.zeros_like(samples)
    piece_rows = p0.shape[0]
    for k, piece in enumerate((p0, p1, p2, p3)):
        place = pl.multiple_of((me ^ k) * piece_rows, 8)
        samples[pl.ds(place, piece_rows), 0:20] = piece[...]
    samples[groups : groups + 1, 0:20] = edge_ref[0:1, :]
    samples[rows - 1 : rows, 0:20] = edge_ref[1:2, :]
    row = lax.broadcasted_iota(jnp.int32, (rows, 128), 0)
    lane = lax.broadcasted_iota(jnp.int32, (rows, 128), 1)
    group = base + jnp.where(row == rows - 1, -1, row)
    s = jnp.where((group * 20 + lane < length) & (lane < 20), samples[...], 0.0)
    after = pltpu.roll(pltpu.roll(s, rows - 1, 0), 20, 1)
    s = jnp.where(lane < 20, s, jnp.where(lane < 25, after, jnp.where(lane == 31, 1.0, 0.0)))
    hi, mid, low = split3(s)
    first = hi + pltpu.roll(hi, 32, 1) + pltpu.roll(hi, 64, 1) + pltpu.roll(mid, 96, 1)
    second = mid + pltpu.roll(low, 32, 1)
    x6 = jnp.concatenate([first.astype(BF16), second.astype(BF16)], 1)
    pre0[...] = dot(x6, w0_ref[...])

    gain0 = gain_ref[0:1, :]
    shift0 = shift_ref[0:1, :]

    def step0(i, carry):
        at = pl.ds(pl.multiple_of(i * CH, CH), CH)
        for g in range(4):
            cols = pl.ds(g * channels, channels)
            x = pre0[at, cols]
            rstd = lax.rsqrt(jnp.mean(x * x, -1, keepdims=True) + EPS)
            z = x * rstd * gain0 + shift0
            cdf, _ = normal_cdf(z)
            act = z * cdf
            a0_ref[at, cols] = act.astype(BF16)
            if g == 0:
                ahead[at, :] = act
        return carry

    lax.fori_loop(0, count, step0, 0)

    tail_row = lax.broadcasted_iota(jnp.int32, (TAIL, channels), 0)
    drop = (tail_row == 0) & is_last

    def shifted(target, offset):
        ahead[groups:rows, :] = jnp.where(drop, 0.0, ahead[groups:rows, :])
        ahead[rows : rows + 1, :] = ahead[0:1, :]

        def move(i, carry):
            at = pl.multiple_of(i * CH, CH)
            block = ahead[pl.ds(at, CH + 8), :]
            target[pl.ds(at, CH), offset : offset + channels] = block[1 : CH + 1, :].astype(BF16)
            return carry

        lax.fori_loop(0, count, move, 0)

    shifted(a0_ref, 4 * channels)
    for g in range(3):
        cols = pl.ds(g * channels, channels)
        tail = a0_ref[groups:rows, cols].astype(F32)
        a0_ref[groups:rows, cols] = jnp.where(drop, 0.0, tail).astype(BF16)

    for h in range(2):
        pre1[h] = dot(a0_ref[:, 2 * h * channels : (2 * h + 3) * channels], k1_ref[...])
    bias1 = bias_ref[1:2, :]
    gain1 = gain_ref[1:2, :]
    shift1 = shift_ref[1:2, :]

    def step1(i, carry):
        at = pl.ds(pl.multiple_of(i * CH, CH), CH)
        for h in range(2):
            x = pre1[h, at, :] + bias1
            x = x - jnp.mean(x, -1, keepdims=True)
            rstd = lax.rsqrt(jnp.mean(x * x, -1, keepdims=True) + EPS)
            hat = x * rstd
            z = hat * gain1 + shift1
            cdf, bell = normal_cdf(z)
            act = z * cdf
            hat_ref[h, at, :] = hat
            slope_ref[h, at, :] = (cdf + z * bell * INV_SQRT_2PI) * gain1
            rstd_ref[h, at, :] = jnp.broadcast_to(rstd, (CH, 128))
            a1_ref[at, h * channels : (h + 1) * channels] = act.astype(BF16)
            if h == 0:
                ahead[at, :] = act
        return carry

    lax.fori_loop(0, count, step1, 0)
    shifted(a1_ref, 2 * channels)

    pre2[...] = dot(a1_ref[...], k2_ref[...])
    cotall[0:groups, :] = cot_ref[...].astype(F32)
    cotall[groups:rows, :] = jnp.where(
        tail_row == TAIL - 1, cotprev_ref[...].astype(F32), 0.0
    )
    bias2 = bias_ref[2:3, :]
    gain2 = gain_ref[2:3, :]
    shift2 = shift_ref[2:3, :]
    limit = length // 20

    def step2(i, carry):
        start = pl.multiple_of(i * CH, CH)
        at = pl.ds(start, CH)
        x = pre2[at, :] + bias2
        x = x - jnp.mean(x, -1, keepdims=True)
        rstd = lax.rsqrt(jnp.mean(x * x, -1, keepdims=True) + EPS)
        hat = x * rstd
        z = hat * gain2 + shift2
        cdf, bell = normal_cdf(z)
        place = start + lax.broadcasted_iota(jnp.int32, (CH, channels), 0)
        place = base + jnp.where(place == rows - 1, -1, place)
        valid = place < limit
        frames_all = jnp.where(valid, z * cdf, 0.0).astype(BF16)
        up = jnp.where(valid, cotall[at, :] * scale, 0.0)
        dhat = up * ((cdf + z * bell * INV_SQRT_2PI) * gain2)
        mean_d = jnp.mean(dhat, -1, keepdims=True)
        mean_dh = jnp.mean(dhat * hat, -1, keepdims=True)
        d2_ref[at, :] = (rstd * (dhat - mean_d - hat * mean_dh)).astype(BF16)

        @pl.when(i < groups // CH)
        def _():
            frames_ref[at, :] = frames_all

        return carry

    lax.fori_loop(0, count, step2, 0)
    d2own[...] = d2_ref[0:groups, :]
    chunk = keep_ref.shape[2]
    put_gradient(core, keep_ref, send_ref, [(a1_ref, 0, d2own)], chunk)


def forward(info, pieces, edges, w0, kernel1, kernel2, bias, gain, shift, cot, cotprev, scale, chunks):
    groups = cot.shape[0]
    channels = cot.shape[1]
    rows = groups + TAIL
    taps = kernel1.shape[0]
    grad = (2, chunks, taps // chunks, BC)
    return pl.pallas_call(
        functools.partial(forward_kernel, groups, scale),
        out_shape=[
            sds((groups, channels), BF16),
            sds(grad, F32),
            sds(grad, BF16),
            sds((rows, 5 * channels), BF16),
            sds((2, rows, channels), F32),
            sds((2, rows, channels), F32),
            sds((2, rows, 128), F32),
            sds((rows, channels), BF16),
        ],
        in_specs=[SM] + [VM] * 13,
        out_specs=[VM] * 8,
        scratch_shapes=[
            pltpu.VMEM((rows, 128), F32),
            pltpu.VMEM((rows, 4 * channels), F32),
            pltpu.VMEM((2, rows, channels), F32),
            pltpu.VMEM((rows, channels), F32),
            pltpu.VMEM((rows, 3 * channels), BF16),
            pltpu.VMEM((rows + 8, channels), F32),
            pltpu.VMEM((rows, channels), F32),
            pltpu.VMEM((groups, channels), BF16),
        ],
        compiler_params=params(),
        cost_estimate=cost(int(8e9), 10 << 20),
        name="forward",
    )(info, *pieces, edges, w0, kernel1, kernel2, bias, gain, shift, cot, cotprev)


def backward_kernel(
    groups,
    info,
    d2_ref,
    k2_ref,
    a0_ref,
    hat_ref,
    slope_ref,
    rstd_ref,
    keep_ref,
    send_ref,
    dwin,
    behind,
    d1,
):
    rows = groups + TAIL
    channels = d2_ref.shape[1]
    core = info[4]
    d2 = d2_ref[...]
    dwin[0] = dot_nt(d2[0:groups, :], k2_ref[0:channels, :])
    dwin[1] = dot_nt(d2[0:groups, :], k2_ref[channels : 2 * channels, :])
    third = dot_nt(d2, k2_ref[2 * channels : 3 * channels, :])
    behind[8 : 8 + groups, :] = third[0:groups, :]
    behind[7:8, :] = third[rows - 1 : rows, :]

    def step(i, carry):
        start = pl.multiple_of(i * CH, CH)
        at = pl.ds(start, CH)
        for h in range(2):
            d = dwin[h, at, :]
            if h == 0:
                d = d + behind[pl.ds(start, CH + 8), :][7 : 7 + CH, :]
            hat = hat_ref[h, at, :]
            dhat = d * slope_ref[h, at, :]
            mean_d = jnp.mean(dhat, -1, keepdims=True)
            mean_dh = jnp.mean(dhat * hat, -1, keepdims=True)
            rstd = rstd_ref[h, at, 0:1]
            d1[h, at, :] = (rstd * (dhat - mean_d - hat * mean_dh)).astype(BF16)
        return carry

    lax.fori_loop(0, groups // CH, step, 0)
    chunk = keep_ref.shape[2]
    put_gradient(
        core, keep_ref, send_ref, [(a0_ref, 0, d1.at[0]), (a0_ref, 2 * channels, d1.at[1])], chunk
    )


def backward(info, d2, kernel2, a0, hat, slope, rstd, chunks):
    rows, channels = d2.shape
    groups = rows - TAIL
    grad = (2, chunks, kernel2.shape[0] // chunks, BC)
    return pl.pallas_call(
        functools.partial(backward_kernel, groups),
        out_shape=[sds(grad, F32), sds(grad, BF16)],
        in_specs=[SM] + [VM] * 6,
        out_specs=[VM] * 2,
        scratch_shapes=[
            pltpu.VMEM((2, groups, channels), F32),
            pltpu.VMEM((groups + 8, channels), F32),
            pltpu.VMEM((2, groups, channels), BF16),
        ],
        compiler_params=params(),
        cost_estimate=cost(int(5e9), 10 << 20),
        name="backward",
    )(info, d2, kernel2, a0, hat, slope, rstd)


def plane_kernel(info, keep_ref, recv_ref, own_ref, tox_ref, toy_ref, tod_ref):
    x, y = info[5], info[6]
    for dx, dy, out in ((0, 0, own_ref), (1, 0, tox_ref), (0, 1, toy_ref), (1, 1, tod_ref)):
        for zz in range(2):
            at = (x ^ dx, 2 * zz + (y ^ dy))
            out[zz] = (keep_ref[at] + recv_ref[at].astype(F32)).astype(out.dtype)


def plane(info, keep, recv):
    shape = (2,) + keep.shape[2:]
    return pl.pallas_call(
        plane_kernel,
        out_shape=[sds(shape, F32)] + [sds(shape, BF16)] * 3,
        in_specs=[SM, VM, VM],
        out_specs=[VM] * 4,
        compiler_params=params(),
        cost_estimate=cost(1 << 20, 5 << 20),
        name="plane",
    )(info, keep, recv)


def column_kernel(info, *refs):
    ins, outs = refs[:8], refs[8:]
    z = info[7]
    for dz, out in enumerate(outs):
        zz = z ^ dz
        for layer in range(2):

            @pl.when(zz // 2 == layer)
            def _():
                own, rx, ry, rd = ins[4 * layer : 4 * layer + 4]
                at = zz % 2
                total = own[at] + rx[at].astype(F32) + ry[at].astype(F32) + rd[at].astype(F32)
                out[...] = total.astype(out.dtype)


def column(info, first, second):
    shape = first[0].shape[1:]
    return pl.pallas_call(
        column_kernel,
        out_shape=[sds(shape, F32)] + [sds(shape, BF16)] * 3,
        in_specs=[SM] + [VM] * 8,
        out_specs=[VM] * 4,
        compiler_params=params(),
        cost_estimate=cost(1 << 20, 3 << 20),
        name="column",
    )(info, *first, *second)


def final_kernel(own, a, b, c, out):
    total = own[...] + a[...].astype(F32) + b[...].astype(F32) + c[...].astype(F32)
    out[...] = total.astype(out.dtype)


def final(own, a, b, c):
    return pl.pallas_call(
        final_kernel,
        out_shape=sds(own.shape, BF16),
        in_specs=[VM] * 4,
        out_specs=VM,
        compiler_params=params(),
        cost_estimate=cost(1 << 18, 1 << 19),
        name="final",
    )(own, a, b, c)


def stats_kernel(info, own, other, pair, lprev, rprev, left, right):
    core, x = info[4], info[5]
    for piece, v in (
        (own, 2 * core + x),
        (other, 2 * core + 1 - x),
        (pair.at[0], 2 * (1 - core) + x),
        (pair.at[1], 2 * (1 - core) + 1 - x),
    ):
        for u in range(2):
            block = piece[u * BR : (u + 1) * BR, :]
            q = 4 * u + v
            left[q] = BETA * lprev[q] + (1.0 - BETA) * dot_nt(block, block)
            right[q] = BETA * rprev[q] + (1.0 - BETA) * dot_tn(block, block)


def stats(info, own, other, pair, lprev, rprev):
    return pl.pallas_call(
        stats_kernel,
        out_shape=[sds(lprev.shape, F32), sds(rprev.shape, F32)],
        in_specs=[SM] + [VM] * 5,
        out_specs=[VM] * 2,
        compiler_params=params(),
        cost_estimate=cost(int(2e8), 4 << 20),
        name="stats",
    )(info, own, other, pair, lprev, rprev)


def permute(value, route):
    return lax.ppermute(value, AXES, route)


def body(
    audio,
    lengths,
    kernel0,
    kernel1,
    kernel2,
    conv_bias,
    norm_gain,
    norm_shift,
    cotangent,
    left_prev,
    right_prev,
):
    tms, batches = lax.axis_size("tm"), lax.axis_size("batch")
    t, b = lax.axis_index("tm"), lax.axis_index("batch")
    recordings, samples_dev = audio.shape
    piece_rows = samples_dev // 20
    groups = piece_rows * batches
    total = groups * tms
    scale = 1.0 / math.sqrt(total)

    def route(move):
        pairs = []
        for tt in range(tms):
            for bb in range(batches):
                to = move(tt, bb)
                if 0 <= to[0] < tms:
                    pairs.append((tt * batches + bb, to[0] * batches + to[1]))
        return pairs

    info = jnp.stack(
        [
            lax.dynamic_index_in_dim(lengths, b, 0, False),
            t * groups,
            jnp.int32(total),
            b,
            b % 2,
            b // 2,
            t % 2,
            t // 2,
        ]
    ).astype(jnp.int32)

    grouped = audio.reshape(recordings, piece_rows, 20)
    pieces = []
    for k in range(batches):
        piece = lax.dynamic_index_in_dim(grouped, b ^ k, 0, False)
        if k:
            piece = permute(piece, route(lambda tt, bb: (tt, bb ^ k)))
        pieces.append(piece)

    def of_place(place, row):
        chosen = pieces[0][row]
        for k in range(1, batches):
            chosen = jnp.where((b ^ k) == place, pieces[k][row], chosen)
        return chosen[None]

    following = permute(of_place(0, 0), route(lambda tt, bb: (tt - 1, bb)))
    preceding = permute(of_place(batches - 1, piece_rows - 1), route(lambda tt, bb: (tt + 1, bb)))
    edges = jnp.concatenate([following, preceding], 0)
    cot = cotangent[0]
    cotprev = permute(cot[groups - 1 :], route(lambda tt, bb: (tt + 1, bb)))

    w0 = prep(kernel0, conv_bias)
    special = tms == 8 and batches == 4
    chunks = 4
    if not special:
        info = info.at[4].set(0)
    frames, keep2, send2, a0, hat, slope, rstd, d2 = forward(
        info,
        pieces,
        edges,
        w0,
        kernel1,
        kernel2,
        conv_bias,
        norm_gain,
        norm_shift,
        cot,
        cotprev,
        scale,
        chunks,
    )
    keep1, send1 = backward(info, d2, kernel2, a0, hat, slope, rstd, chunks)

    if not special:

        def blocks_of(keep, send):
            both = jnp.stack([keep, send.astype(F32)])
            both = both.reshape(2, 2, -1, BR, BC)
            return jnp.transpose(both, (2, 0, 1, 3, 4)).reshape(-1, BR, BC)

        stacked = jnp.concatenate([blocks_of(keep1, send1), blocks_of(keep2, send2)], 0)
        owned = lax.psum_scatter(stacked, "tm", scatter_dimension=0, tiled=True)
        owned = lax.psum(owned, "batch")
        left = BETA * left_prev + (1.0 - BETA) * jnp.einsum(
            "bik,bjk->bij", owned, owned, precision=lax.Precision.HIGHEST
        )
        right = BETA * right_prev + (1.0 - BETA) * jnp.einsum(
            "bki,bkj->bij", owned, owned, precision=lax.Precision.HIGHEST
        )
        return frames[None], left, right

    by_core = route(lambda tt, bb: (tt, bb ^ 1))
    by_x = route(lambda tt, bb: (tt, bb ^ 2))
    by_y = route(lambda tt, bb: (tt ^ 1, bb))
    by_xy = route(lambda tt, bb: (tt ^ 1, bb ^ 2))
    by_z = [route(lambda tt, bb: (tt ^ (2 * k), bb)) for k in range(1, 4)]

    def plane_sums(keep, send):
        own, tox, toy, tod = plane(info, keep, permute(send, by_core))
        return own, permute(tox, by_x), permute(toy, by_y), permute(tod, by_xy)

    second = plane_sums(keep2, send2)
    first = plane_sums(keep1, send1)
    own, *out = column(info, first, second)
    arrived = [permute(value, way) for value, way in zip(out, by_z)]
    owned = final(own, *arrived)
    other = permute(owned, by_x)
    pair = permute(jnp.stack([owned, other]), by_core)
    left, right = stats(info, owned, other, pair, left_prev, right_prev)
    return frames[None], left, right


def solution(mesh):
    return jax.shard_map(
        body,
        mesh=mesh,
        in_specs=(
            P(None, AXES),
            P(),
            P(),
            P(),
            P(),
            P(),
            P(),
            P(),
            P("batch", "tm", None),
            P("tm", None, None),
            P("tm", None, None),
        ),
        out_specs=(P("batch", "tm", None), P("tm", None, None), P("tm", None, None)),
        check_vma=False,
    )
```

```python
import functools
import math

import jax
import jax.numpy as jnp
from jax import lax
from jax.experimental import pallas as pl
from jax.experimental.pallas import tpu as pltpu
from jax.sharding import PartitionSpec as P

BR = 192
BC = 128
EPS = 1e-05
BETA = 0.95
AXES = ("tm", "batch")
F32 = jnp.float32
BF16 = jnp.bfloat16
MIB = 1024 * 1024
CH = 16
CH0, CH1, CH2, CH3 = 16,16,16,16
UN0, UN1, UN2, UN3 = 4,25,6,6
TAIL = 16

VM = pl.BlockSpec(memory_space=pltpu.VMEM)
SM = pl.BlockSpec(memory_space=pltpu.SMEM)


def params(mib=12):
    return pltpu.CompilerParams(vmem_limit_bytes=mib * MIB)


def cost(flops, nbytes, trans=0):
    return pl.CostEstimate(flops=flops, bytes_accessed=nbytes, transcendentals=trans)


def sds(shape, dtype):
    return jax.ShapeDtypeStruct(shape, dtype)


def normal_cdf(z):
    bell = jnp.exp(z * z * -0.5)
    t = 1.0 / (1.0 + jnp.abs(z) * (0.3275911 / math.sqrt(2.0)))
    poly = t * (0.5 * 1.061405429) + (0.5 * -1.453152027)
    poly = poly * t + (0.5 * 1.421413741)
    poly = poly * t + (0.5 * -0.284496736)
    poly = poly * t + (0.5 * 0.254829592)
    q = poly * t * bell
    return jnp.where(z < 0.0, q, 1.0 - q), bell


INV_SQRT_2PI = 1.0 / math.sqrt(2.0 * math.pi)


def split3(x):
    hi = x.astype(BF16).astype(F32)
    rest = x - hi
    mid = rest.astype(BF16).astype(F32)
    return hi, mid, rest - mid


def prep_kernel(k0_ref, bias_ref, w_ref, wide):
    channels = k0_ref.shape[1]
    k0 = k0_ref[...]
    k0 = k0 - jnp.mean(k0, -1, keepdims=True)
    bias = bias_ref[0:1, :]
    bias = bias - jnp.mean(bias, -1, keepdims=True)
    parts = split3(k0)
    bparts = split3(bias)
    wide[...] = jnp.zeros_like(wide)
    for block, part in enumerate((0, 1, 2, 0, 1, 0)):
        for g in range(4):
            cols = pl.ds(g * channels, channels)
            wide[pl.ds(block * 32 + 5 * g, 10), cols] = parts[part]
            if block < 3:
                wide[pl.ds(block * 32 + 31, 1), cols] = bparts[part]
    w_ref[...] = wide[...].astype(BF16)


def prep(kernel0, conv_bias):
    channels = kernel0.shape[1]
    return pl.pallas_call(
        prep_kernel,
        out_shape=sds((256, 4 * channels), BF16),
        in_specs=[VM, VM],
        out_specs=VM,
        scratch_shapes=[pltpu.VMEM((256, 4 * channels), F32)],
        compiler_params=params(),
        cost_estimate=cost(4 * 256 * 2048, 1 << 20),
        name="prep",
    )(kernel0, conv_bias)


def dot(a, b):
    return lax.dot_general(a, b, (((1,), (0,)), ((), ())), preferred_element_type=F32)


def dot_tn(a, b):
    return lax.dot_general(a, b, (((0,), (0,)), ((), ())), preferred_element_type=F32)


def dot_nt(a, b):
    return lax.dot_general(a, b, (((1,), (1,)), ((), ())), preferred_element_type=F32)


def put_gradient(core, keep_ref, send_ref, pairs, chunk):
    half = keep_ref.shape[-1] * 2
    width = keep_ref.shape[-1]
    for which, out in ((core, keep_ref), (1 - core, send_ref)):
        start = pl.multiple_of(which * half, half)
        for row in range(keep_ref.shape[1]):
            total = None
            for a_ref, offset, d_ref in pairs:
                groups = d_ref.shape[0]
                a = a_ref[0:groups, offset + row * chunk : offset + (row + 1) * chunk]
                piece = dot_tn(a, d_ref[:, pl.ds(start, half)])
                total = piece if total is None else total + piece
            out[0, row] = total[:, :width].astype(out.dtype)
            out[1, row] = total[:, width:].astype(out.dtype)


class Place:
    def __init__(self, special):
        t, b = lax.axis_index("tm"), lax.axis_index("batch")
        self.t, self.b = t, b
        self.core = lax.rem(b, 2) if special else 0
        self.x, self.y, self.z = lax.div(b, 2), lax.rem(t, 2), lax.div(t, 2)


def layer_zero(pre, at, gain0, shift0, channels, g):
    x = pre[at, pl.ds(g * channels, channels)]
    rstd = lax.rsqrt(jnp.mean(x * x, -1, keepdims=True) + EPS)
    z = x * rstd * gain0 + shift0
    cdf, _ = normal_cdf(z)
    return z * cdf


def taps(block, after):
    lane = lax.broadcasted_iota(jnp.int32, block.shape, 1)
    after = pltpu.roll(after, 20, 1)
    s = jnp.where(
        lane < 20, block, jnp.where(lane < 25, after, jnp.where(lane == 31, 1.0, 0.0))
    )
    hi, mid, low = split3(s)
    first = hi + pltpu.roll(hi, 32, 1) + pltpu.roll(hi, 64, 1) + pltpu.roll(mid, 96, 1)
    second = mid + pltpu.roll(low, 32, 1)
    return jnp.concatenate([first.astype(BF16), second.astype(BF16)], 1)


def move_up(source, target, offset, rows):
    channels = source.shape[1]

    def move(i, carry):
        at = pl.multiple_of(i * CH, CH)
        block = source[pl.ds(at, CH + 8), :]
        target[pl.ds(at, CH), offset : offset + channels] = block[1 : CH + 1, :].astype(BF16)
        return carry

    lax.fori_loop(0, rows // CH, move, 0, unroll=2)


def audio_kernel(
    special, lengths, p0, p1, p2, p3, w0_ref, gain_ref, shift_ref, a0_ref, head_ref, keep, samples, pre0, ahead
):
    here = Place(special)
    piece_rows = p0.shape[0]
    groups = 4 * piece_rows
    channels = gain_ref.shape[1]
    length = lengths[here.b]
    base = here.t * groups
    samples[...] = jnp.zeros_like(samples)
    for k, piece in enumerate((p0, p1, p2, p3)):
        place = pl.multiple_of((here.b ^ k) * piece_rows, 8)
        samples[pl.ds(place, piece_rows), 0:20] = piece[...]
    row = lax.broadcasted_iota(jnp.int32, (groups, 128), 0)
    lane = lax.broadcasted_iota(jnp.int32, (groups, 128), 1)
    s = jnp.where(((base + row) * 20 + lane < length) & (lane < 20), samples[...], 0.0)
    keep[0:8, :] = s[0:8]
    keep[8 : 8 + TAIL, :] = s[groups - TAIL :]
    pre0[...] = dot(taps(s, pltpu.roll(s, groups - 1, 0)), w0_ref[...])
    gain0 = gain_ref[0:1, :]
    shift0 = shift_ref[0:1, :]

    def step(i, carry):
        at = pl.ds(pl.multiple_of(i * CH0, CH0), CH0)
        for g in range(4):
            act = layer_zero(pre0, at, gain0, shift0, channels, g)
            a0_ref[at, pl.ds(g * channels, channels)] = act.astype(BF16)
            if g == 0:
                ahead[at, :] = act
        return carry

    lax.fori_loop(0, groups // CH0, step, 0, unroll=UN0)
    head_ref[...] = ahead[0:8, :]
    move_up(ahead, a0_ref, 4 * channels, groups)


def audio_layer(lengths, pieces, w0, gain, shift, special):
    groups = 4 * pieces[0].shape[0]
    channels = gain.shape[1]
    return pl.pallas_call(
        functools.partial(audio_kernel, special),
        out_shape=[
            sds((groups, 5 * channels), BF16),
            sds((8, channels), F32),
            sds((8 + TAIL, 128), F32),
        ],
        in_specs=[SM] + [VM] * 7,
        out_specs=[VM] * 3,
        scratch_shapes=[
            pltpu.VMEM((groups, 128), F32),
            pltpu.VMEM((groups, 4 * channels), F32),
            pltpu.VMEM((groups + 8, channels), F32),
        ],
        compiler_params=params(16),
        cost_estimate=cost(int(3e9), 5 << 20),
        name="audio_layer",
    )(lengths, *pieces, w0, gain, shift)


def forward_kernel(
    special,
    groups,
    scale,
    lengths,
    a0_in,
    head_in,
    kept,
    edge_a,
    edge_b,
    w0_ref,
    k1_ref,
    k2_ref,
    bias_ref,
    gain_ref,
    shift_ref,
    cot_ref,
    a0_ref,
    frames_ref,
    keep_ref,
    send_ref,
    hat_ref,
    slope_ref,
    rstd_ref,
    d2_ref,
    pre0,
    pre1,
    pre2,
    a1_ref,
    ahead,
    d2own,
):
    here = Place(special)
    rows = groups + TAIL
    channels = k1_ref.shape[1]
    length = lengths[here.b]
    base = here.t * groups
    total = groups * lax.axis_size("tm")
    is_last = base + groups >= total
    odd = lax.rem(here.t, 2) == 1

    following = jnp.where(odd, edge_b[...], edge_a[...])
    preceding = jnp.where(odd, edge_a[...], edge_b[...])
    row = lax.broadcasted_iota(jnp.int32, (TAIL, 128), 0)
    lane = lax.broadcasted_iota(jnp.int32, (TAIL, 128), 1)
    group = base + jnp.where(row == TAIL - 1, -1, groups + row)
    tail = jnp.where(row == 0, following[:, :128], jnp.where(row == TAIL - 1, preceding[:, :128], 0.0))
    tail = jnp.where((group * 20 + lane < length) & (lane < 20), tail, 0.0)
    block = jnp.concatenate([kept[8 : 8 + TAIL, :], tail], 0)
    row = lax.broadcasted_iota(jnp.int32, (2 * TAIL, 128), 0)
    after = jnp.where(row == 2 * TAIL - 1, kept[0:1, :], pltpu.roll(block, 2 * TAIL - 1, 0))
    pre0[...] = dot(taps(block, after), w0_ref[...])
    tail_row = lax.broadcasted_iota(jnp.int32, (TAIL, channels), 0)
    drop = (tail_row == 0) & is_last
    gain0 = gain_ref[0:1, :]
    shift0 = shift_ref[0:1, :]
    a0_ref[0:groups, :] = a0_in[...]
    for g in range(4):
        cols = pl.ds(g * channels, channels)
        start = TAIL if g in (1, 2) else 0
        act = layer_zero(pre0, pl.ds(start, 2 * TAIL - start), gain0, shift0, channels, g)
        behind, act = act[: TAIL - start], act[TAIL - start :]
        act = jnp.where(drop, 0.0, act)
        a0_ref[groups:rows, cols] = act.astype(BF16)
        if g == 3:
            a0_ref[groups - TAIL : groups, cols] = behind.astype(BF16)
        if g == 0:
            both = jnp.concatenate([behind, act], 0)
            up_row = lax.broadcasted_iota(jnp.int32, both.shape, 0)
            up = jnp.where(
                up_row == 2 * TAIL - 1, head_in[0:1, :], pltpu.roll(both, 2 * TAIL - 1, 0)
            )
            a0_ref[groups - TAIL : rows, 4 * channels : 5 * channels] = up.astype(BF16)

    for h in range(2):
        pre1[h] = dot(a0_ref[:, 2 * h * channels : (2 * h + 3) * channels], k1_ref[...])
    bias1 = bias_ref[1:2, :]
    gain1 = gain_ref[1:2, :]
    shift1 = shift_ref[1:2, :]

    def step1(i, carry):
        at = pl.ds(pl.multiple_of(i * CH1, CH1), CH1)
        for h in range(2):
            x = pre1[h, at, :] + bias1
            x = x - jnp.mean(x, -1, keepdims=True)
            rstd = lax.rsqrt(jnp.mean(x * x, -1, keepdims=True) + EPS)
            hat = x * rstd
            z = hat * gain1 + shift1
            cdf, bell = normal_cdf(z)
            act = z * cdf
            hat_ref[h, at, :] = hat
            slope_ref[h, at, :] = (cdf + z * bell * INV_SQRT_2PI) * gain1
            rstd_ref[h, at, :] = jnp.broadcast_to(rstd, (CH1, 128))
            a1_ref[at, h * channels : (h + 1) * channels] = act.astype(BF16)
            if h == 0:
                ahead[at, :] = act
        return carry

    lax.fori_loop(0, rows // CH1, step1, 0, unroll=UN1)
    ahead[groups:rows, :] = jnp.where(drop, 0.0, ahead[groups:rows, :])
    ahead[rows : rows + 1, :] = ahead[0:1, :]
    move_up(ahead, a1_ref, 2 * channels, rows)

    pre2[...] = dot(a1_ref[...], k2_ref[...])
    bias2 = bias_ref[2:3, :]
    gain2 = gain_ref[2:3, :]
    shift2 = shift_ref[2:3, :]
    limit = length // 20

    def layer_two(at, place, cot):
        x = pre2[at, :] + bias2
        x = x - jnp.mean(x, -1, keepdims=True)
        rstd = lax.rsqrt(jnp.mean(x * x, -1, keepdims=True) + EPS)
        hat = x * rstd
        z = hat * gain2 + shift2
        cdf, bell = normal_cdf(z)
        valid = place < limit
        up = jnp.where(valid, cot * scale, 0.0)
        dhat = up * ((cdf + z * bell * INV_SQRT_2PI) * gain2)
        mean_d = jnp.mean(dhat, -1, keepdims=True)
        mean_dh = jnp.mean(dhat * hat, -1, keepdims=True)
        d2 = rstd * (dhat - mean_d - hat * mean_dh)
        return jnp.where(valid, z * cdf, 0.0).astype(BF16), d2.astype(BF16)

    def step2(i, carry):
        start = pl.multiple_of(i * CH2, CH2)
        at = pl.ds(start, CH2)
        place = base + start + lax.broadcasted_iota(jnp.int32, (CH2, channels), 0)
        frames, d2 = layer_two(at, place, cot_ref[at, :].astype(F32))
        frames_ref[at, :] = frames
        d2_ref[at, :] = d2
        d2own[at, :] = d2
        return carry

    lax.fori_loop(0, groups // CH2, step2, 0, unroll=UN2)
    cot_tail = jnp.where(tail_row == TAIL - 1, preceding[:, 128:], 0.0)
    place = base + jnp.where(tail_row == TAIL - 1, -1, groups + tail_row)
    _, d2_ref[groups:rows, :] = layer_two(pl.ds(groups, TAIL), place, cot_tail)
    put_gradient(here.core, keep_ref, send_ref, [(a1_ref, 0, d2own)], keep_ref.shape[2])


def forward(
    lengths, a0, head, kept, edges, w0, kernel1, kernel2, bias, gain, shift, cot, scale, chunks, special
):
    groups = cot.shape[0]
    channels = cot.shape[1]
    rows = groups + TAIL
    taps_all = kernel1.shape[0]
    grad = (2, chunks, taps_all // chunks, BC)
    return pl.pallas_call(
        functools.partial(forward_kernel, special, groups, scale),
        out_shape=[
            sds((rows, 5 * channels), BF16),
            sds((groups, channels), BF16),
            sds(grad, F32),
            sds(grad, BF16),
            sds((2, rows, channels), F32),
            sds((2, rows, channels), F32),
            sds((2, rows, 128), F32),
            sds((rows, channels), BF16),
        ],
        in_specs=[SM] + [VM] * 12,
        out_specs=[VM] * 8,
        scratch_shapes=[
            pltpu.VMEM((2 * TAIL, 4 * channels), F32),
            pltpu.VMEM((2, rows, channels), F32),
            pltpu.VMEM((rows, channels), F32),
            pltpu.VMEM((rows, 3 * channels), BF16),
            pltpu.VMEM((rows + 8, channels), F32),
            pltpu.VMEM((groups, channels), BF16),
        ],
        compiler_params=params(26),
        cost_estimate=cost(int(8e9), 10 << 20),
        name="forward",
    )(lengths, a0, head, kept, *edges, w0, kernel1, kernel2, bias, gain, shift, cot)


def window_kernel(d2_ref, k2_ref, dwin, behind):
    groups, channels = dwin.shape[1:]
    rows = groups + TAIL
    d2 = d2_ref[...]
    third = dot_nt(d2, k2_ref[2 * channels : 3 * channels, :])
    behind[8 : 8 + groups, :] = third[0:groups, :]
    behind[7:8, :] = third[rows - 1 : rows, :]
    dwin[0] = dot_nt(d2[0:groups, :], k2_ref[0:channels, :])
    dwin[1] = dot_nt(d2[0:groups, :], k2_ref[channels : 2 * channels, :])


def window(d2, kernel2):
    rows, channels = d2.shape
    groups = rows - TAIL
    return pl.pallas_call(
        window_kernel,
        out_shape=[sds((2, groups, channels), F32), sds((groups + 8, channels), F32)],
        in_specs=[VM] * 2,
        out_specs=[VM] * 2,
        compiler_params=params(),
        cost_estimate=cost(int(1.5e9), 3 << 20),
        name="window",
    )(d2, kernel2)


def backward_kernel(
    special, behind, dwin, a0_ref, hat_ref, slope_ref, rstd_ref, order_ref, keep_ref, send_ref, d1
):
    here = Place(special)
    groups, channels = dwin.shape[1:]

    def step(i, carry):
        start = pl.multiple_of(i * CH3, CH3)
        at = pl.ds(start, CH3)
        for h in range(2):
            d = dwin[h, at, :]
            if h == 0:
                d = d + behind[pl.ds(start, CH3 + 8), :][7 : 7 + CH3, :]
            hat = hat_ref[h, at, :]
            dhat = d * slope_ref[h, at, :]
            mean_d = jnp.mean(dhat, -1, keepdims=True)
            mean_dh = jnp.mean(dhat * hat, -1, keepdims=True)
            rstd = rstd_ref[h, at, 0:1]
            d1[h, at, :] = (rstd * (dhat - mean_d - hat * mean_dh)).astype(BF16)
        return carry

    lax.fori_loop(0, groups // CH3, step, 0, unroll=UN3)
    put_gradient(
        here.core,
        keep_ref,
        send_ref,
        [(a0_ref, 0, d1.at[0]), (a0_ref, 2 * channels, d1.at[1])],
        keep_ref.shape[2],
    )


def backward(behind, dwin, a0, hat, slope, rstd, order, taps_all, chunks, special):
    groups, channels = dwin.shape[1:]
    grad = (2, chunks, taps_all // chunks, BC)
    return pl.pallas_call(
        functools.partial(backward_kernel, special),
        out_shape=[sds(grad, F32), sds(grad, BF16)],
        in_specs=[VM] * 6 + [pl.BlockSpec(memory_space=pl.ANY)],
        out_specs=[VM] * 2,
        scratch_shapes=[
            pltpu.VMEM((2, groups, channels), BF16),
        ],
        compiler_params=params(20),
        cost_estimate=cost(int(4e9), 10 << 20),
        name="backward",
    )(behind, dwin, a0, hat, slope, rstd, order)


def plane_kernel(keep_ref, recv_ref, *outs):
    here = Place(True)
    x, y = here.x, here.y
    for (dx, dy), out in zip(((0, 0), (1, 0), (0, 1), (1, 1)), outs):
        for zz in range(2):
            at = (x ^ dx, 2 * zz + (y ^ dy))
            out[zz] = (keep_ref[at] + recv_ref[at].astype(F32)).astype(out.dtype)


def plane(keep, recv, order):
    shape = (2,) + keep.shape[2:]
    return pl.pallas_call(
        lambda keep_ref, recv_ref, order_ref, *outs: plane_kernel(keep_ref, recv_ref, *outs),
        out_shape=[sds(shape, F32)] + [sds(shape, BF16)] * 3,
        in_specs=[VM] * 2 + [pl.BlockSpec(memory_space=pl.ANY)],
        out_specs=[VM] * 4,
        compiler_params=params(),
        cost_estimate=cost(1 << 20, 5 << 20),
        name="plane",
    )(keep, recv, order)


def collect_kernel(own, rx, ry, rd, out):
    out[...] = own[...] + rx[...].astype(F32) + ry[...].astype(F32) + rd[...].astype(F32)


def collect(own, rx, ry, rd):
    return pl.pallas_call(
        collect_kernel,
        out_shape=sds(own.shape, F32),
        in_specs=[VM] * 4,
        out_specs=VM,
        compiler_params=params(),
        cost_estimate=cost(1 << 20, 8 << 20),
        name="collect",
    )(own, rx, ry, rd)


def column_kernel(own, rx, ry, rd, second, *outs):
    z = Place(True).z
    for dz, out in enumerate(outs):
        zz = z ^ dz
        at = lax.rem(zz, 2)

        @pl.when(zz < 2)
        def _():
            total = own[at] + rx[at].astype(F32) + ry[at].astype(F32) + rd[at].astype(F32)
            out[...] = total.astype(out.dtype)

        @pl.when(zz >= 2)
        def _():
            out[...] = second[at].astype(out.dtype)


def column(first, second):
    shape = second.shape[1:]
    return pl.pallas_call(
        column_kernel,
        out_shape=[sds(shape, F32)] + [sds(shape, BF16)] * 3,
        in_specs=[VM] * 5,
        out_specs=[VM] * 4,
        compiler_params=params(),
        cost_estimate=cost(1 << 20, 3 << 20),
        name="column",
    )(*first, second)


def final_kernel(own, a, b, c, out):
    total = own[...] + a[...].astype(F32) + b[...].astype(F32) + c[...].astype(F32)
    out[...] = total.astype(out.dtype)


def final(own, a, b, c):
    return pl.pallas_call(
        final_kernel,
        out_shape=sds(own.shape, BF16),
        in_specs=[VM] * 4,
        out_specs=VM,
        compiler_params=params(),
        cost_estimate=cost(1 << 18, 1 << 19),
        name="final",
    )(own, a, b, c)


def stats_kernel(own, other, pair, lprev, rprev, left, right):
    here = Place(True)
    core, x = here.core, here.x
    for piece, v in (
        (own, 2 * core + x),
        (other, 2 * core + 1 - x),
        (pair.at[0], 2 * (1 - core) + x),
        (pair.at[1], 2 * (1 - core) + 1 - x),
    ):
        for u in range(2):
            block = piece[u * BR : (u + 1) * BR, :]
            q = 4 * u + v
            left[q] = BETA * lprev[q] + (1.0 - BETA) * dot_nt(block, block)
            right[q] = BETA * rprev[q] + (1.0 - BETA) * dot_tn(block, block)


def stats(own, other, pair, lprev, rprev):
    return pl.pallas_call(
        stats_kernel,
        out_shape=[sds(lprev.shape, F32), sds(rprev.shape, F32)],
        in_specs=[VM] * 5,
        out_specs=[VM] * 2,
        compiler_params=params(),
        cost_estimate=cost(int(2e8), 4 << 20),
        name="stats",
    )(own, other, pair, lprev, rprev)


def permute(value, route):
    return lax.ppermute(value, AXES, route)


def body(
    audio,
    lengths,
    kernel0,
    kernel1,
    kernel2,
    conv_bias,
    norm_gain,
    norm_shift,
    cotangent,
    left_prev,
    right_prev,
):
    tms, batches = lax.axis_size("tm"), lax.axis_size("batch")
    t, b = lax.axis_index("tm"), lax.axis_index("batch")
    recordings, samples_dev = audio.shape
    piece_rows = samples_dev // 20
    groups = piece_rows * batches
    total = groups * tms
    scale = 1.0 / math.sqrt(total)

    def route(move):
        pairs = []
        for tt in range(tms):
            for bb in range(batches):
                to = move(tt, bb)
                if 0 <= to[0] < tms:
                    pairs.append((tt * batches + bb, to[0] * batches + to[1]))
        return pairs

    grouped = audio.reshape(recordings, piece_rows, 20)
    pieces = []
    for k in range(batches):
        piece = lax.dynamic_index_in_dim(grouped, b ^ k, 0, False)
        if k:
            piece = permute(piece, route(lambda tt, bb: (tt, bb ^ k)))
        pieces.append(piece)

    def of_place(place, row):
        chosen = pieces[0][row]
        for k in range(1, batches):
            chosen = jnp.where((b ^ k) == place, pieces[k][row], chosen)
        return chosen[None]

    cot = cotangent[0]
    first_group = jnp.pad(of_place(0, 0), ((0, 0), (0, 108 + cot.shape[1])))
    last_group = jnp.concatenate(
        [
            jnp.pad(of_place(batches - 1, piece_rows - 1), ((0, 0), (0, 108))),
            cot[groups - 1 :].astype(F32),
        ],
        1,
    )
    odd = t % 2 == 1
    edge_a = permute(jnp.where(odd, first_group, last_group), route(lambda tt, bb: (tt ^ 1, bb)))
    edge_b = permute(
        jnp.where(odd, last_group, first_group), route(lambda tt, bb: (tt + 2 * (tt % 2) - 1, bb))
    )

    w0 = prep(kernel0, conv_bias)
    special = tms == 8 and batches == 4
    chunks = 4
    a0, head, kept = audio_layer(lengths, pieces, w0, norm_gain, norm_shift, special)
    a0, frames, keep2, send2, hat, slope, rstd, d2 = forward(
        lengths,
        a0,
        head,
        kept,
        (edge_a, edge_b),
        w0,
        kernel1,
        kernel2,
        conv_bias,
        norm_gain,
        norm_shift,
        cot,
        scale,
        chunks,
        special,
    )
    dwin, behind = window(d2, kernel2)

    def gradient_one(order):
        return backward(behind, dwin, a0, hat, slope, rstd, order, kernel1.shape[0], chunks, special)

    if not special:
        keep1, send1 = gradient_one(keep2)

        def blocks_of(keep, send):
            both = jnp.stack([keep, send.astype(F32)])
            both = both.reshape(2, 2, -1, BR, BC)
            return jnp.transpose(both, (2, 0, 1, 3, 4)).reshape(-1, BR, BC)

        stacked = jnp.concatenate([blocks_of(keep1, send1), blocks_of(keep2, send2)], 0)
        owned = lax.psum_scatter(stacked, "tm", scatter_dimension=0, tiled=True)
        owned = lax.psum(owned, "batch")
        left = BETA * left_prev + (1.0 - BETA) * jnp.einsum(
            "bik,bjk->bij", owned, owned, precision=lax.Precision.HIGHEST
        )
        right = BETA * right_prev + (1.0 - BETA) * jnp.einsum(
            "bki,bkj->bij", owned, owned, precision=lax.Precision.HIGHEST
        )
        return frames[None], left, right

    by_core = route(lambda tt, bb: (tt, bb ^ 1))
    by_x = route(lambda tt, bb: (tt, bb ^ 2))
    by_y = route(lambda tt, bb: (tt ^ 1, bb))
    by_xy = route(lambda tt, bb: (tt ^ 1, bb ^ 2))
    by_z = [route(lambda tt, bb: (tt ^ (2 * k), bb)) for k in range(1, 4)]

    def to_plane(tox, toy, tod):
        return permute(tox, by_x), permute(toy, by_y), permute(tod, by_xy)

    own2, *out = plane(keep2, permute(send2, by_core), keep2)
    second = collect(own2, *to_plane(*out))
    keep1, send1 = gradient_one(own2)
    own1, *out = plane(keep1, permute(send1, by_core), second)
    own, *out = column((own1, *to_plane(*out)), second)
    arrived = [permute(value, way) for value, way in zip(out, by_z)]
    owned = final(own, *arrived)
    other = permute(owned, by_x)
    pair = permute(jnp.stack([owned, other]), by_core)
    left, right = stats(owned, other, pair, left_prev, right_prev)
    return frames[None], left, right


def solution(mesh):
    return jax.shard_map(
        body,
        mesh=mesh,
        in_specs=(
            P(None, AXES),
            P(),
            P(),
            P(),
            P(),
            P(),
            P(),
            P(),
            P("batch", "tm", None),
            P("tm", None, None),
            P("tm", None, None),
        ),
        out_specs=(P("batch", "tm", None), P("tm", None, None), P("tm", None, None)),
        check_vma=False,
    )
```

```python
import functools
import math

import jax
import jax.numpy as jnp
from jax import lax
from jax.experimental import pallas as pl
from jax.experimental.pallas import tpu as pltpu
from jax.sharding import PartitionSpec as P

BR = 192
BC = 128
EPS = 1e-05
BETA = 0.95
AXES = ("tm", "batch")
F32 = jnp.float32
BF16 = jnp.bfloat16
MIB = 1024 * 1024
CH = 16
PACK = 6
CH0, CH1, CH2, CH3 = 16,16,16,16
UN0, UN1, UN2, UN3 = 4,25,6,6
TAIL = 16

VM = pl.BlockSpec(memory_space=pltpu.VMEM)
SM = pl.BlockSpec(memory_space=pltpu.SMEM)


def params(mib=12):
    return pltpu.CompilerParams(vmem_limit_bytes=mib * MIB)


def cost(flops, nbytes, trans=0):
    return pl.CostEstimate(flops=flops, bytes_accessed=nbytes, transcendentals=trans)


def sds(shape, dtype):
    return jax.ShapeDtypeStruct(shape, dtype)


def normal_cdf(z):
    bell = jnp.exp(z * z * -0.5)
    t = 1.0 / (1.0 + jnp.abs(z) * (0.3275911 / math.sqrt(2.0)))
    poly = t * (0.5 * 1.061405429) + (0.5 * -1.453152027)
    poly = poly * t + (0.5 * 1.421413741)
    poly = poly * t + (0.5 * -0.284496736)
    poly = poly * t + (0.5 * 0.254829592)
    q = poly * t * bell
    return jnp.where(z < 0.0, q, 1.0 - q), bell


INV_SQRT_2PI = 1.0 / math.sqrt(2.0 * math.pi)


def split3(x):
    hi = x.astype(BF16).astype(F32)
    rest = x - hi
    mid = rest.astype(BF16).astype(F32)
    return hi, mid, rest - mid


def prep_kernel(k0_ref, bias_ref, w_ref, wide):
    channels = k0_ref.shape[1]
    k0 = k0_ref[...]
    k0 = k0 - jnp.mean(k0, -1, keepdims=True)
    bias = bias_ref[0:1, :]
    bias = bias - jnp.mean(bias, -1, keepdims=True)
    parts = split3(k0)
    bparts = split3(bias)
    wide[...] = jnp.zeros_like(wide)
    for block, part in enumerate((0, 1, 2, 0, 1, 0)):
        for g in range(4):
            cols = pl.ds(g * channels, channels)
            wide[pl.ds(block * 32 + 5 * g, 10), cols] = parts[part]
            if block < 3:
                wide[pl.ds(block * 32 + 31, 1), cols] = bparts[part]
    w_ref[...] = wide[...].astype(BF16)


def prep(kernel0, conv_bias):
    channels = kernel0.shape[1]
    return pl.pallas_call(
        prep_kernel,
        out_shape=sds((256, 4 * channels), BF16),
        in_specs=[VM, VM],
        out_specs=VM,
        scratch_shapes=[pltpu.VMEM((256, 4 * channels), F32)],
        compiler_params=params(),
        cost_estimate=cost(4 * 256 * 2048, 1 << 20),
        name="prep",
    )(kernel0, conv_bias)


def dot(a, b):
    return lax.dot_general(a, b, (((1,), (0,)), ((), ())), preferred_element_type=F32)


def dot_tn(a, b):
    return lax.dot_general(a, b, (((0,), (0,)), ((), ())), preferred_element_type=F32)


def dot_nt(a, b):
    return lax.dot_general(a, b, (((1,), (1,)), ((), ())), preferred_element_type=F32)


def put_gradient(core, keep_ref, send_ref, pairs, chunk):
    half = keep_ref.shape[-1] * 2
    width = keep_ref.shape[-1]
    for which, out in ((core, keep_ref), (1 - core, send_ref)):
        start = pl.multiple_of(which * half, half)
        for row in range(keep_ref.shape[1]):
            total = None
            for a_ref, offset, d_ref in pairs:
                groups = d_ref.shape[0]
                a = a_ref[0:groups, offset + row * chunk : offset + (row + 1) * chunk]
                piece = dot_tn(a, d_ref[:, pl.ds(start, half)])
                total = piece if total is None else total + piece
            out[0, row] = total[:, :width].astype(out.dtype)
            out[1, row] = total[:, width:].astype(out.dtype)


class Place:
    def __init__(self, special):
        t, b = lax.axis_index("tm"), lax.axis_index("batch")
        self.t, self.b = t, b
        self.core = lax.rem(b, 2) if special else 0
        self.x, self.y, self.z = lax.div(b, 2), lax.rem(t, 2), lax.div(t, 2)


def layer_zero(pre, at, gain0, shift0, channels, g):
    x = pre[at, pl.ds(g * channels, channels)]
    rstd = lax.rsqrt(jnp.mean(x * x, -1, keepdims=True) + EPS)
    z = x * rstd * gain0 + shift0
    cdf, _ = normal_cdf(z)
    return z * cdf


def taps(block, after):
    lane = lax.broadcasted_iota(jnp.int32, block.shape, 1)
    after = pltpu.roll(after, 20, 1)
    s = jnp.where(
        lane < 20, block, jnp.where(lane < 25, after, jnp.where(lane == 31, 1.0, 0.0))
    )
    hi, mid, low = split3(s)
    first = hi + pltpu.roll(hi, 32, 1) + pltpu.roll(hi, 64, 1) + pltpu.roll(mid, 96, 1)
    second = mid + pltpu.roll(low, 32, 1)
    return jnp.concatenate([first.astype(BF16), second.astype(BF16)], 1)


def move_up(source, target, offset, rows):
    channels = source.shape[1]

    def move(i, carry):
        at = pl.multiple_of(i * CH, CH)
        block = source[pl.ds(at, CH + 8), :]
        target[pl.ds(at, CH), offset : offset + channels] = block[1 : CH + 1, :].astype(BF16)
        return carry

    lax.fori_loop(0, rows // CH, move, 0, unroll=2)


def pack_kernel(grouped, *outs):
    b = lax.axis_index("batch")
    piece_rows = grouped.shape[1]
    part = piece_rows // PACK
    lane = lax.broadcasted_iota(jnp.int32, (part, 128), 1)
    for k, out in enumerate(outs):
        total = None
        for q in range(PACK):
            block = grouped[b ^ k, q * part : (q + 1) * part, :]
            block = jnp.concatenate([block, jnp.zeros((part, 108), F32)], 1)
            block = pltpu.roll(block, 20 * q, 1) if q else block
            total = block if total is None else total + block
        out[...] = total


def pack(grouped):
    recordings, piece_rows, _ = grouped.shape
    return pl.pallas_call(
        pack_kernel,
        out_shape=[sds((piece_rows // PACK, 128), F32)] * recordings,
        in_specs=[VM],
        out_specs=[VM] * recordings,
        compiler_params=params(),
        cost_estimate=cost(1 << 16, 1 << 17),
        name="pack",
    )(grouped)


def audio_kernel(
    special, lengths, p0, p1, p2, p3, w0_ref, gain_ref, shift_ref, a0_ref, head_ref, keep, samples, pre0, ahead
):
    here = Place(special)
    part = p0.shape[0]
    piece_rows = PACK * part
    groups = 4 * piece_rows
    channels = gain_ref.shape[1]
    length = lengths[here.b]
    base = here.t * groups
    for k, piece in enumerate((p0, p1, p2, p3)):
        for q in range(PACK):
            place = pl.multiple_of((here.b ^ k) * piece_rows + q * part, 8)
            block = piece[...]
            samples[pl.ds(place, part), :] = pltpu.roll(block, 128 - 20 * q, 1) if q else block
    row = lax.broadcasted_iota(jnp.int32, (groups, 128), 0)
    lane = lax.broadcasted_iota(jnp.int32, (groups, 128), 1)
    s = jnp.where(((base + row) * 20 + lane < length) & (lane < 20), samples[...], 0.0)
    keep[0:8, :] = s[0:8]
    keep[8 : 8 + TAIL, :] = s[groups - TAIL :]
    pre0[...] = dot(taps(s, pltpu.roll(s, groups - 1, 0)), w0_ref[...])
    gain0 = gain_ref[0:1, :]
    shift0 = shift_ref[0:1, :]

    def step(i, carry):
        at = pl.ds(pl.multiple_of(i * CH0, CH0), CH0)
        for g in range(4):
            act = layer_zero(pre0, at, gain0, shift0, channels, g)
            a0_ref[at, pl.ds(g * channels, channels)] = act.astype(BF16)
            if g == 0:
                ahead[at, :] = act
        return carry

    lax.fori_loop(0, groups // CH0, step, 0, unroll=UN0)
    head_ref[...] = ahead[0:8, :]
    move_up(ahead, a0_ref, 4 * channels, groups)


def audio_layer(lengths, pieces, w0, gain, shift, special):
    groups = 4 * PACK * pieces[0].shape[0]
    channels = gain.shape[1]
    return pl.pallas_call(
        functools.partial(audio_kernel, special),
        out_shape=[
            sds((groups, 5 * channels), BF16),
            sds((8, channels), F32),
            sds((8 + TAIL, 128), F32),
        ],
        in_specs=[SM] + [VM] * 7,
        out_specs=[VM] * 3,
        scratch_shapes=[
            pltpu.VMEM((groups, 128), F32),
            pltpu.VMEM((groups, 4 * channels), F32),
            pltpu.VMEM((groups + 8, channels), F32),
        ],
        compiler_params=params(16),
        cost_estimate=cost(int(3e9), 5 << 20),
        name="audio_layer",
    )(lengths, *pieces, w0, gain, shift)


def forward_kernel(
    special,
    groups,
    scale,
    lengths,
    a0_in,
    head_in,
    kept,
    edge_a,
    edge_b,
    w0_ref,
    k1_ref,
    k2_ref,
    bias_ref,
    gain_ref,
    shift_ref,
    cot_ref,
    a0_ref,
    frames_ref,
    keep_ref,
    send_ref,
    hat_ref,
    slope_ref,
    rstd_ref,
    d2_ref,
    pre0,
    pre1,
    pre2,
    a1_ref,
    ahead,
    d2own,
):
    here = Place(special)
    rows = groups + TAIL
    channels = k1_ref.shape[1]
    length = lengths[here.b]
    base = here.t * groups
    total = groups * lax.axis_size("tm")
    is_last = base + groups >= total
    odd = lax.rem(here.t, 2) == 1

    following = jnp.where(odd, edge_b[...], edge_a[...])
    preceding = jnp.where(odd, edge_a[...], edge_b[...])
    row = lax.broadcasted_iota(jnp.int32, (TAIL, 128), 0)
    lane = lax.broadcasted_iota(jnp.int32, (TAIL, 128), 1)
    group = base + jnp.where(row == TAIL - 1, -1, groups + row)
    tail = jnp.where(row == 0, following[:, :128], jnp.where(row == TAIL - 1, preceding[:, :128], 0.0))
    tail = jnp.where((group * 20 + lane < length) & (lane < 20), tail, 0.0)
    block = jnp.concatenate([kept[8 : 8 + TAIL, :], tail], 0)
    row = lax.broadcasted_iota(jnp.int32, (2 * TAIL, 128), 0)
    after = jnp.where(row == 2 * TAIL - 1, kept[0:1, :], pltpu.roll(block, 2 * TAIL - 1, 0))
    pre0[...] = dot(taps(block, after), w0_ref[...])
    tail_row = lax.broadcasted_iota(jnp.int32, (TAIL, channels), 0)
    drop = (tail_row == 0) & is_last
    gain0 = gain_ref[0:1, :]
    shift0 = shift_ref[0:1, :]
    a0_ref[0:groups, :] = a0_in[...]
    for g in range(4):
        cols = pl.ds(g * channels, channels)
        start = TAIL if g in (1, 2) else 0
        act = layer_zero(pre0, pl.ds(start, 2 * TAIL - start), gain0, shift0, channels, g)
        behind, act = act[: TAIL - start], act[TAIL - start :]
        act = jnp.where(drop, 0.0, act)
        a0_ref[groups:rows, cols] = act.astype(BF16)
        if g == 3:
            a0_ref[groups - TAIL : groups, cols] = behind.astype(BF16)
        if g == 0:
            both = jnp.concatenate([behind, act], 0)
            up_row = lax.broadcasted_iota(jnp.int32, both.shape, 0)
            up = jnp.where(
                up_row == 2 * TAIL - 1, head_in[0:1, :], pltpu.roll(both, 2 * TAIL - 1, 0)
            )
            a0_ref[groups - TAIL : rows, 4 * channels : 5 * channels] = up.astype(BF16)

    for h in range(2):
        pre1[h] = dot(a0_ref[:, 2 * h * channels : (2 * h + 3) * channels], k1_ref[...])
    bias1 = bias_ref[1:2, :]
    gain1 = gain_ref[1:2, :]
    shift1 = shift_ref[1:2, :]

    def step1(i, carry):
        at = pl.ds(pl.multiple_of(i * CH1, CH1), CH1)
        for h in range(2):
            x = pre1[h, at, :] + bias1
            x = x - jnp.mean(x, -1, keepdims=True)
            rstd = lax.rsqrt(jnp.mean(x * x, -1, keepdims=True) + EPS)
            hat = x * rstd
            z = hat * gain1 + shift1
            cdf, bell = normal_cdf(z)
            act = z * cdf
            hat_ref[h, at, :] = hat
            slope_ref[h, at, :] = (cdf + z * bell * INV_SQRT_2PI) * gain1
            rstd_ref[h, at, :] = jnp.broadcast_to(rstd, (CH1, 128))
            a1_ref[at, h * channels : (h + 1) * channels] = act.astype(BF16)
            if h == 0:
                ahead[at, :] = act
        return carry

    lax.fori_loop(0, rows // CH1, step1, 0, unroll=UN1)
    ahead[groups:rows, :] = jnp.where(drop, 0.0, ahead[groups:rows, :])
    ahead[rows : rows + 1, :] = ahead[0:1, :]
    move_up(ahead, a1_ref, 2 * channels, rows)

    pre2[...] = dot(a1_ref[...], k2_ref[...])
    bias2 = bias_ref[2:3, :]
    gain2 = gain_ref[2:3, :]
    shift2 = shift_ref[2:3, :]
    limit = length // 20

    def layer_two(at, place, cot):
        x = pre2[at, :] + bias2
        x = x - jnp.mean(x, -1, keepdims=True)
        rstd = lax.rsqrt(jnp.mean(x * x, -1, keepdims=True) + EPS)
        hat = x * rstd
        z = hat * gain2 + shift2
        cdf, bell = normal_cdf(z)
        valid = place < limit
        up = jnp.where(valid, cot * scale, 0.0)
        dhat = up * ((cdf + z * bell * INV_SQRT_2PI) * gain2)
        mean_d = jnp.mean(dhat, -1, keepdims=True)
        mean_dh = jnp.mean(dhat * hat, -1, keepdims=True)
        d2 = rstd * (dhat - mean_d - hat * mean_dh)
        return jnp.where(valid, z * cdf, 0.0).astype(BF16), d2.astype(BF16)

    def step2(i, carry):
        start = pl.multiple_of(i * CH2, CH2)
        at = pl.ds(start, CH2)
        place = base + start + lax.broadcasted_iota(jnp.int32, (CH2, channels), 0)
        frames, d2 = layer_two(at, place, cot_ref[at, :].astype(F32))
        frames_ref[at, :] = frames
        d2_ref[at, :] = d2
        d2own[at, :] = d2
        return carry

    lax.fori_loop(0, groups // CH2, step2, 0, unroll=UN2)
    cot_tail = jnp.where(tail_row == TAIL - 1, preceding[:, 128:], 0.0)
    place = base + jnp.where(tail_row == TAIL - 1, -1, groups + tail_row)
    _, d2_ref[groups:rows, :] = layer_two(pl.ds(groups, TAIL), place, cot_tail)
    put_gradient(here.core, keep_ref, send_ref, [(a1_ref, 0, d2own)], keep_ref.shape[2])


def forward(
    lengths, a0, head, kept, edges, w0, kernel1, kernel2, bias, gain, shift, cot, scale, chunks, special
):
    groups = cot.shape[0]
    channels = cot.shape[1]
    rows = groups + TAIL
    taps_all = kernel1.shape[0]
    grad = (2, chunks, taps_all // chunks, BC)
    return pl.pallas_call(
        functools.partial(forward_kernel, special, groups, scale),
        out_shape=[
            sds((rows, 5 * channels), BF16),
            sds((groups, channels), BF16),
            sds(grad, F32),
            sds(grad, BF16),
            sds((2, rows, channels), F32),
            sds((2, rows, channels), F32),
            sds((2, rows, 128), F32),
            sds((rows, channels), BF16),
        ],
        in_specs=[SM] + [VM] * 12,
        out_specs=[VM] * 8,
        scratch_shapes=[
            pltpu.VMEM((2 * TAIL, 4 * channels), F32),
            pltpu.VMEM((2, rows, channels), F32),
            pltpu.VMEM((rows, channels), F32),
            pltpu.VMEM((rows, 3 * channels), BF16),
            pltpu.VMEM((rows + 8, channels), F32),
            pltpu.VMEM((groups, channels), BF16),
        ],
        compiler_params=params(26),
        cost_estimate=cost(int(8e9), 10 << 20),
        name="forward",
    )(lengths, a0, head, kept, *edges, w0, kernel1, kernel2, bias, gain, shift, cot)


def window_kernel(d2_ref, k2_ref, hat_ref, slope_ref, rstd_ref, d1, dwin, behind):
    groups, channels = dwin.shape[1:]
    rows = groups + TAIL
    d2 = d2_ref[...]
    third = dot_nt(d2, k2_ref[2 * channels : 3 * channels, :])
    behind[8 : 8 + groups, :] = third[0:groups, :]
    behind[7:8, :] = third[rows - 1 : rows, :]
    dwin[0] = dot_nt(d2[0:groups, :], k2_ref[0:channels, :])
    dwin[1] = dot_nt(d2[0:groups, :], k2_ref[channels : 2 * channels, :])

    def step(i, carry):
        start = pl.multiple_of(i * CH3, CH3)
        at = pl.ds(start, CH3)
        for h in range(2):
            d = dwin[h, at, :]
            if h == 0:
                d = d + behind[pl.ds(start, CH3 + 8), :][7 : 7 + CH3, :]
            hat = hat_ref[h, at, :]
            dhat = d * slope_ref[h, at, :]
            mean_d = jnp.mean(dhat, -1, keepdims=True)
            mean_dh = jnp.mean(dhat * hat, -1, keepdims=True)
            rstd = rstd_ref[h, at, 0:1]
            d1[h, at, :] = (rstd * (dhat - mean_d - hat * mean_dh)).astype(BF16)
        return carry

    lax.fori_loop(0, groups // CH3, step, 0, unroll=UN3)


def window(d2, kernel2, hat, slope, rstd):
    rows, channels = d2.shape
    groups = rows - TAIL
    return pl.pallas_call(
        window_kernel,
        out_shape=sds((2, groups, channels), BF16),
        in_specs=[VM] * 5,
        out_specs=VM,
        scratch_shapes=[
            pltpu.VMEM((2, groups, channels), F32),
            pltpu.VMEM((groups + 8, channels), F32),
        ],
        compiler_params=params(16),
        cost_estimate=cost(int(1.5e9), 3 << 20),
        name="window",
    )(d2, kernel2, hat, slope, rstd)


def backward_kernel(special, d1, a0_ref, order_ref, keep_ref, send_ref):
    here = Place(special)
    channels = d1.shape[2]
    put_gradient(
        here.core,
        keep_ref,
        send_ref,
        [(a0_ref, 0, d1.at[0]), (a0_ref, 2 * channels, d1.at[1])],
        keep_ref.shape[2],
    )


def backward(d1, a0, order, taps_all, chunks, special):
    grad = (2, chunks, taps_all // chunks, BC)
    return pl.pallas_call(
        functools.partial(backward_kernel, special),
        out_shape=[sds(grad, F32), sds(grad, BF16)],
        in_specs=[VM] * 2 + [pl.BlockSpec(memory_space=pl.ANY)],
        out_specs=[VM] * 2,
        compiler_params=params(16),
        cost_estimate=cost(int(4e9), 10 << 20),
        name="backward",
    )(d1, a0, order)


def plane_kernel(keep_ref, recv_ref, *outs):
    here = Place(True)
    x, y = here.x, here.y
    for (dx, dy), out in zip(((0, 0), (1, 0), (0, 1), (1, 1)), outs):
        for zz in range(2):
            at = (x ^ dx, 2 * zz + (y ^ dy))
            out[zz] = (keep_ref[at] + recv_ref[at].astype(F32)).astype(out.dtype)


def plane(keep, recv, order):
    shape = (2,) + keep.shape[2:]
    return pl.pallas_call(
        lambda keep_ref, recv_ref, order_ref, *outs: plane_kernel(keep_ref, recv_ref, *outs),
        out_shape=[sds(shape, F32)] + [sds(shape, BF16)] * 3,
        in_specs=[VM] * 2 + [pl.BlockSpec(memory_space=pl.ANY)],
        out_specs=[VM] * 4,
        compiler_params=params(),
        cost_estimate=cost(1 << 20, 5 << 20),
        name="plane",
    )(keep, recv, order)


def collect_kernel(own, rx, ry, rd, out):
    out[...] = own[...] + rx[...].astype(F32) + ry[...].astype(F32) + rd[...].astype(F32)


def collect(own, rx, ry, rd):
    return pl.pallas_call(
        collect_kernel,
        out_shape=sds(own.shape, F32),
        in_specs=[VM] * 4,
        out_specs=VM,
        compiler_params=params(),
        cost_estimate=cost(int(1e10), 8 << 20),
        name="collect",
    )(own, rx, ry, rd)


def column_kernel(own, rx, ry, rd, second, *outs):
    z = Place(True).z
    for dz, out in enumerate(outs):
        zz = z ^ dz
        at = lax.rem(zz, 2)

        @pl.when(zz < 2)
        def _():
            total = own[at] + rx[at].astype(F32) + ry[at].astype(F32) + rd[at].astype(F32)
            out[...] = total.astype(out.dtype)

        @pl.when(zz >= 2)
        def _():
            out[...] = second[at].astype(out.dtype)


def column(first, second):
    shape = second.shape[1:]
    return pl.pallas_call(
        column_kernel,
        out_shape=[sds(shape, F32)] + [sds(shape, BF16)] * 3,
        in_specs=[VM] * 5,
        out_specs=[VM] * 4,
        compiler_params=params(),
        cost_estimate=cost(1 << 20, 3 << 20),
        name="column",
    )(*first, second)


def final_kernel(own, a, b, c, out):
    total = own[...] + a[...].astype(F32) + b[...].astype(F32) + c[...].astype(F32)
    out[...] = total.astype(out.dtype)


def final(own, a, b, c):
    return pl.pallas_call(
        final_kernel,
        out_shape=sds(own.shape, BF16),
        in_specs=[VM] * 4,
        out_specs=VM,
        compiler_params=params(),
        cost_estimate=cost(1 << 18, 1 << 19),
        name="final",
    )(own, a, b, c)


def stats_kernel(own, other, pair, lprev, rprev, left, right):
    here = Place(True)
    core, x = here.core, here.x
    for piece, v in (
        (own, 2 * core + x),
        (other, 2 * core + 1 - x),
        (pair.at[0], 2 * (1 - core) + x),
        (pair.at[1], 2 * (1 - core) + 1 - x),
    ):
        for u in range(2):
            block = piece[u * BR : (u + 1) * BR, :]
            q = 4 * u + v
            left[q] = BETA * lprev[q] + (1.0 - BETA) * dot_nt(block, block)
            right[q] = BETA * rprev[q] + (1.0 - BETA) * dot_tn(block, block)


def stats(own, other, pair, lprev, rprev):
    return pl.pallas_call(
        stats_kernel,
        out_shape=[sds(lprev.shape, F32), sds(rprev.shape, F32)],
        in_specs=[VM] * 5,
        out_specs=[VM] * 2,
        compiler_params=params(),
        cost_estimate=cost(int(2e8), 4 << 20),
        name="stats",
    )(own, other, pair, lprev, rprev)


def permute(value, route):
    return lax.ppermute(value, AXES, route)


def body(
    audio,
    lengths,
    kernel0,
    kernel1,
    kernel2,
    conv_bias,
    norm_gain,
    norm_shift,
    cotangent,
    left_prev,
    right_prev,
):
    tms, batches = lax.axis_size("tm"), lax.axis_size("batch")
    t, b = lax.axis_index("tm"), lax.axis_index("batch")
    recordings, samples_dev = audio.shape
    piece_rows = samples_dev // 20
    groups = piece_rows * batches
    total = groups * tms
    scale = 1.0 / math.sqrt(total)

    def route(move):
        pairs = []
        for tt in range(tms):
            for bb in range(batches):
                to = move(tt, bb)
                if 0 <= to[0] < tms:
                    pairs.append((tt * batches + bb, to[0] * batches + to[1]))
        return pairs

    pieces = list(pack(audio.reshape(recordings, piece_rows, 20)))
    for k in range(1, batches):
        pieces[k] = permute(pieces[k], route(lambda tt, bb: (tt, bb ^ k)))

    def of_place(place, row, lane):
        chosen = pieces[0][row, lane : lane + 20]
        for k in range(1, batches):
            chosen = jnp.where((b ^ k) == place, pieces[k][row, lane : lane + 20], chosen)
        return chosen[None]

    cot = cotangent[0]
    first_group = jnp.pad(of_place(0, 0, 0), ((0, 0), (0, 108 + cot.shape[1])))
    last_group = jnp.concatenate(
        [
            jnp.pad(of_place(batches - 1, -1, 20 * (PACK - 1)), ((0, 0), (0, 108))),
            cot[groups - 1 :].astype(F32),
        ],
        1,
    )
    odd = t % 2 == 1
    edge_a = permute(jnp.where(odd, first_group, last_group), route(lambda tt, bb: (tt ^ 1, bb)))
    edge_b = permute(
        jnp.where(odd, last_group, first_group), route(lambda tt, bb: (tt + 2 * (tt % 2) - 1, bb))
    )

    w0 = prep(kernel0, conv_bias)
    special = tms == 8 and batches == 4
    chunks = 4
    a0, head, kept = audio_layer(lengths, pieces, w0, norm_gain, norm_shift, special)
    a0, frames, keep2, send2, hat, slope, rstd, d2 = forward(
        lengths,
        a0,
        head,
        kept,
        (edge_a, edge_b),
        w0,
        kernel1,
        kernel2,
        conv_bias,
        norm_gain,
        norm_shift,
        cot,
        scale,
        chunks,
        special,
    )
    d1 = window(d2, kernel2, hat, slope, rstd)

    def gradient_one(order):
        return backward(d1, a0, order, kernel1.shape[0], chunks, special)

    if not special:
        keep1, send1 = gradient_one(keep2)

        def blocks_of(keep, send):
            both = jnp.stack([keep, send.astype(F32)])
            both = both.reshape(2, 2, -1, BR, BC)
            return jnp.transpose(both, (2, 0, 1, 3, 4)).reshape(-1, BR, BC)

        stacked = jnp.concatenate([blocks_of(keep1, send1), blocks_of(keep2, send2)], 0)
        owned = lax.psum_scatter(stacked, "tm", scatter_dimension=0, tiled=True)
        owned = lax.psum(owned, "batch")
        left = BETA * left_prev + (1.0 - BETA) * jnp.einsum(
            "bik,bjk->bij", owned, owned, precision=lax.Precision.HIGHEST
        )
        right = BETA * right_prev + (1.0 - BETA) * jnp.einsum(
            "bki,bkj->bij", owned, owned, precision=lax.Precision.HIGHEST
        )
        return frames[None], left, right

    by_core = route(lambda tt, bb: (tt, bb ^ 1))
    by_x = route(lambda tt, bb: (tt, bb ^ 2))
    by_y = route(lambda tt, bb: (tt ^ 1, bb))
    by_xy = route(lambda tt, bb: (tt ^ 1, bb ^ 2))
    by_z = [route(lambda tt, bb: (tt ^ (2 * k), bb)) for k in range(1, 4)]

    def to_plane(tox, toy, tod):
        return permute(tox, by_x), permute(toy, by_y), permute(tod, by_xy)

    own2, *out = plane(keep2, permute(send2, by_core), keep2)
    second = collect(own2, *to_plane(*out))
    keep1, send1 = gradient_one(own2)
    own1, *out = plane(keep1, permute(send1, by_core), second)
    own, *out = column((own1, *to_plane(*out)), second)
    arrived = [permute(value, way) for value, way in zip(out, by_z)]
    owned = final(own, *arrived)
    other = permute(owned, by_x)
    pair = permute(jnp.stack([owned, other]), by_core)
    left, right = stats(owned, other, pair, left_prev, right_prev)
    return frames[None], left, right


def solution(mesh):
    return jax.shard_map(
        body,
        mesh=mesh,
        in_specs=(
            P(None, AXES),
            P(),
            P(),
            P(),
            P(),
            P(),
            P(),
            P(),
            P("batch", "tm", None),
            P("tm", None, None),
            P("tm", None, None),
        ),
        out_specs=(P("batch", "tm", None), P("tm", None, None), P("tm", None, None)),
        check_vma=False,
    )
```

```python
import functools
import math

import jax
import jax.numpy as jnp
from jax import lax
from jax.experimental import pallas as pl
from jax.experimental.pallas import tpu as pltpu
from jax.sharding import PartitionSpec as P

BR = 192
BC = 128
EPS = 1e-05
BETA = 0.95
AXES = ("tm", "batch")
F32 = jnp.float32
BF16 = jnp.bfloat16
MIB = 1024 * 1024
CH = 16
PACK = 6
CH0, CH1, CH2, CH3 = 16,16,16,16
UN0, UN1, UN2, UN3 = 12, 25, 24, 24
TAIL = 16

VM = pl.BlockSpec(memory_space=pltpu.VMEM)
SM = pl.BlockSpec(memory_space=pltpu.SMEM)


def params(mib=12):
    return pltpu.CompilerParams(vmem_limit_bytes=mib * MIB)


def cost(flops, nbytes, trans=0):
    return pl.CostEstimate(flops=flops, bytes_accessed=nbytes, transcendentals=trans)


def sds(shape, dtype):
    return jax.ShapeDtypeStruct(shape, dtype)


def normal_cdf(z):
    bell = jnp.exp2(z * z * (-0.5 * math.log2(math.e)))
    return 0.5 + 0.5 * lax.erf(z * math.sqrt(0.5)), bell


INV_SQRT_2PI = 1.0 / math.sqrt(2.0 * math.pi)


def split3(x):
    hi = x.astype(BF16).astype(F32)
    rest = x - hi
    mid = rest.astype(BF16).astype(F32)
    return hi, mid, rest - mid


def prep_kernel(table_ref, w_ref, meta_ref, wide):
    channels = table_ref.shape[1]
    b = lax.axis_index("batch")
    lane = lax.broadcasted_iota(jnp.int32, (1, channels), 1)
    length = jnp.sum(jnp.where(lane == b, table_ref[20:21, :], 0.0), -1, keepdims=True)
    length = jnp.broadcast_to(length.astype(jnp.int32), meta_ref.shape)
    meta_row = lax.broadcasted_iota(jnp.int32, meta_ref.shape, 0)
    meta_ref[...] = jnp.where(meta_row == 0, length, lax.div(length, 20))
    wide[...] = jnp.zeros_like(wide)
    k0 = table_ref[0:10, :]
    k0 = k0 - jnp.mean(k0, -1, keepdims=True)
    bias = table_ref[10:11, :]
    bias = bias - jnp.mean(bias, -1, keepdims=True)
    parts = split3(k0)
    bparts = split3(bias)
    for block, part in enumerate((0, 1, 2, 0, 1, 0)):
        for g in range(4):
            cols = pl.ds(g * channels, channels)
            wide[pl.ds(block * 32 + 5 * g, 10), cols] = parts[part]
            if block < 3:
                wide[pl.ds(block * 32 + 31, 1), cols] = bparts[part]
    w_ref[...] = wide[...].astype(BF16)


def prep(table):
    channels = table.shape[1]
    return pl.pallas_call(
        prep_kernel,
        out_shape=[sds((256, 4 * channels), BF16), sds((8, channels), jnp.int32)],
        in_specs=[VM],
        out_specs=[VM] * 2,
        scratch_shapes=[pltpu.VMEM((256, 4 * channels), F32)],
        compiler_params=params(),
        cost_estimate=cost(4 * 256 * 2048, 1 << 20),
        name="prep",
    )(table)


def dot(a, b):
    return lax.dot_general(a, b, (((1,), (0,)), ((), ())), preferred_element_type=F32)


def dot_tn(a, b):
    return lax.dot_general(a, b, (((0,), (0,)), ((), ())), preferred_element_type=F32)


def dot_nt(a, b):
    return lax.dot_general(a, b, (((1,), (1,)), ((), ())), preferred_element_type=F32)


def put_gradient(core, keep_ref, send_ref, pairs, chunk):
    half = keep_ref.shape[-1] * 2
    width = keep_ref.shape[-1]
    for which, out in ((core, keep_ref), (1 - core, send_ref)):
        start = pl.multiple_of(which * half, half)
        for row in range(keep_ref.shape[1]):
            total = None
            for a_ref, offset, d_ref in pairs:
                groups = d_ref.shape[0]
                a = a_ref[0:groups, offset + row * chunk : offset + (row + 1) * chunk]
                piece = dot_tn(a, d_ref[:, pl.ds(start, half)])
                total = piece if total is None else total + piece
            out[0, row] = total[:, :width].astype(out.dtype)
            out[1, row] = total[:, width:].astype(out.dtype)


class Place:
    def __init__(self, special):
        t, b = lax.axis_index("tm"), lax.axis_index("batch")
        self.t, self.b = t, b
        self.core = lax.rem(b, 2) if special else 0
        self.x, self.y, self.z = lax.div(b, 2), lax.rem(t, 2), lax.div(t, 2)


def layer_zero(pre, at, gain0, shift0, channels, g):
    x = pre[at, pl.ds(g * channels, channels)]
    rstd = lax.rsqrt(jnp.mean(x * x, -1, keepdims=True) + EPS)
    z = x * rstd * gain0 + shift0
    cdf, _ = normal_cdf(z)
    return z * cdf


def taps(block, after):
    lane = lax.broadcasted_iota(jnp.int32, block.shape, 1)
    after = pltpu.roll(after, 20, 1)
    s = jnp.where(
        lane < 20, block, jnp.where(lane < 25, after, jnp.where(lane == 31, 1.0, 0.0))
    )
    hi, mid, low = split3(s)
    first = hi + pltpu.roll(hi, 32, 1) + pltpu.roll(hi, 64, 1) + pltpu.roll(mid, 96, 1)
    second = mid + pltpu.roll(low, 32, 1)
    return jnp.concatenate([first.astype(BF16), second.astype(BF16)], 1)


def move_up(source, target, offset, rows):
    channels = source.shape[1]

    def move(i, carry):
        at = pl.multiple_of(i * CH, CH)
        block = source[pl.ds(at, CH + 8), :]
        target[pl.ds(at, CH), offset : offset + channels] = block[1 : CH + 1, :].astype(BF16)
        return carry

    lax.fori_loop(0, rows // CH, move, 0, unroll=2)


def pack_kernel(audio, *refs):
    outs, (local, packed) = refs[:-2], refs[-2:]
    b = lax.axis_index("batch")
    recordings, samples = audio.shape
    part = samples // 20 // PACK
    pltpu.sync_copy(audio, local)
    x = local[...]
    blank = jnp.zeros((recordings, 128 - 20 * PACK), F32)
    for r in range(part):
        starts = [20 * (part * q + r) for q in range(PACK)]
        packed[:, r, :] = jnp.concatenate([x[:, at : at + 20] for at in starts] + [blank], 1)
    for k, out in enumerate(outs):
        out[...] = packed[b ^ k]


def pack(audio):
    recordings, samples = audio.shape
    part = samples // 20 // PACK
    return pl.pallas_call(
        pack_kernel,
        out_shape=[sds((part, 128), F32)] * recordings,
        in_specs=[pl.BlockSpec(memory_space=pltpu.HBM)],
        out_specs=[VM] * recordings,
        scratch_shapes=[
            pltpu.VMEM(audio.shape, F32),
            pltpu.VMEM((recordings, part, 128), F32),
        ],
        compiler_params=params(),
        cost_estimate=cost(1 << 16, 1 << 17),
        name="pack",
    )(audio)


def audio_kernel(
    special, p0, p1, p2, p3, w0_ref, rows_ref, meta_ref, a0_ref, head_ref, keep, samples, pre0, ahead
):
    here = Place(special)
    part = p0.shape[0]
    piece_rows = PACK * part
    groups = 4 * piece_rows
    channels = rows_ref.shape[1]
    length = meta_ref[0:1, 0:128]
    base = here.t * groups
    for k, piece in enumerate((p0, p1, p2, p3)):
        for q in range(PACK):
            place = pl.multiple_of((here.b ^ k) * piece_rows + q * part, 8)
            block = piece[...]
            samples[pl.ds(place, part), :] = pltpu.roll(block, 128 - 20 * q, 1) if q else block
    row = lax.broadcasted_iota(jnp.int32, (groups, 128), 0)
    lane = lax.broadcasted_iota(jnp.int32, (groups, 128), 1)
    s = jnp.where(((base + row) * 20 + lane < length) & (lane < 20), samples[...], 0.0)
    keep[0:8, :] = s[0:8]
    keep[8 : 8 + TAIL, :] = s[groups - TAIL :]
    pre0[...] = dot(taps(s, pltpu.roll(s, groups - 1, 0)), w0_ref[...])
    gain0 = rows_ref[13:14, :]
    shift0 = rows_ref[16:17, :]

    def step(i, carry):
        at = pl.ds(pl.multiple_of(i * CH0, CH0), CH0)
        for g in range(4):
            act = layer_zero(pre0, at, gain0, shift0, channels, g)
            a0_ref[at, pl.ds(g * channels, channels)] = act.astype(BF16)
            if g == 0:
                ahead[at, :] = act
        return carry

    lax.fori_loop(0, groups // CH0, step, 0, unroll=UN0)
    head_ref[...] = ahead[0:8, :]
    move_up(ahead, a0_ref, 4 * channels, groups)


def audio_layer(pieces, w0, table, meta, special):
    groups = 4 * PACK * pieces[0].shape[0]
    channels = table.shape[1]
    return pl.pallas_call(
        functools.partial(audio_kernel, special),
        out_shape=[
            sds((groups, 5 * channels), BF16),
            sds((8, channels), F32),
            sds((8 + TAIL, 128), F32),
        ],
        in_specs=[VM] * 7,
        out_specs=[VM] * 3,
        scratch_shapes=[
            pltpu.VMEM((groups, 128), F32),
            pltpu.VMEM((groups, 4 * channels), F32),
            pltpu.VMEM((groups + 8, channels), F32),
        ],
        compiler_params=params(16),
        cost_estimate=cost(int(3e9), 5 << 20),
        name="audio_layer",
    )(*pieces, w0, table, meta)


def forward_kernel(
    special,
    groups,
    scale,
    a0_in,
    head_in,
    kept,
    edge_a,
    edge_b,
    w0_ref,
    k1_ref,
    k2_ref,
    rows_ref,
    meta_ref,
    cot_ref,
    a0_ref,
    frames_ref,
    keep_ref,
    send_ref,
    hat_ref,
    slope_ref,
    rstd_ref,
    d2_ref,
    pre0,
    pre1,
    pre2,
    a1_ref,
    ahead,
    d2own,
):
    here = Place(special)
    rows = groups + TAIL
    channels = k1_ref.shape[1]
    length = meta_ref[0:1, 0:128]
    base = here.t * groups
    total = groups * lax.axis_size("tm")
    is_last = base + groups >= total
    odd = lax.rem(here.t, 2) == 1

    following = jnp.where(odd, edge_b[...], edge_a[...])
    preceding = jnp.where(odd, edge_a[...], edge_b[...])
    row = lax.broadcasted_iota(jnp.int32, (TAIL, 128), 0)
    lane = lax.broadcasted_iota(jnp.int32, (TAIL, 128), 1)
    group = base + jnp.where(row == TAIL - 1, -1, groups + row)
    tail = jnp.where(row == 0, following[:, :128], jnp.where(row == TAIL - 1, preceding[:, :128], 0.0))
    tail = jnp.where((group * 20 + lane < length) & (lane < 20), tail, 0.0)
    block = jnp.concatenate([kept[8 : 8 + TAIL, :], tail], 0)
    row = lax.broadcasted_iota(jnp.int32, (2 * TAIL, 128), 0)
    after = jnp.where(row == 2 * TAIL - 1, kept[0:1, :], pltpu.roll(block, 2 * TAIL - 1, 0))
    pre0[...] = dot(taps(block, after), w0_ref[...])
    tail_row = lax.broadcasted_iota(jnp.int32, (TAIL, channels), 0)
    drop = (tail_row == 0) & is_last
    gain0 = rows_ref[13:14, :]
    shift0 = rows_ref[16:17, :]
    a0_ref[0:groups, :] = a0_in[...]
    for g in range(4):
        cols = pl.ds(g * channels, channels)
        start = TAIL if g in (1, 2) else 0
        act = layer_zero(pre0, pl.ds(start, 2 * TAIL - start), gain0, shift0, channels, g)
        behind, act = act[: TAIL - start], act[TAIL - start :]
        act = jnp.where(drop, 0.0, act)
        a0_ref[groups:rows, cols] = act.astype(BF16)
        if g == 3:
            a0_ref[groups - TAIL : groups, cols] = behind.astype(BF16)
        if g == 0:
            both = jnp.concatenate([behind, act], 0)
            up_row = lax.broadcasted_iota(jnp.int32, both.shape, 0)
            up = jnp.where(
                up_row == 2 * TAIL - 1, head_in[0:1, :], pltpu.roll(both, 2 * TAIL - 1, 0)
            )
            a0_ref[groups - TAIL : rows, 4 * channels : 5 * channels] = up.astype(BF16)

    for h in range(2):
        pre1[h] = dot(a0_ref[:, 2 * h * channels : (2 * h + 3) * channels], k1_ref[...])
    bias1 = rows_ref[11:12, :]
    gain1 = rows_ref[14:15, :]
    shift1 = rows_ref[17:18, :]

    def step1(i, carry):
        at = pl.ds(pl.multiple_of(i * CH1, CH1), CH1)
        for h in range(2):
            x = pre1[h, at, :] + bias1
            x = x - jnp.mean(x, -1, keepdims=True)
            rstd = lax.rsqrt(jnp.mean(x * x, -1, keepdims=True) + EPS)
            hat = x * rstd
            z = hat * gain1 + shift1
            cdf, bell = normal_cdf(z)
            act = z * cdf
            hat_ref[h, at, :] = hat
            slope_ref[h, at, :] = (cdf + z * bell * INV_SQRT_2PI) * gain1
            rstd_ref[h, at, :] = jnp.broadcast_to(rstd, (CH1, 128))
            a1_ref[at, h * channels : (h + 1) * channels] = act.astype(BF16)
            if h == 0:
                ahead[at, :] = act
        return carry

    lax.fori_loop(0, rows // CH1, step1, 0, unroll=UN1)
    ahead[groups:rows, :] = jnp.where(drop, 0.0, ahead[groups:rows, :])
    ahead[rows : rows + 1, :] = ahead[0:1, :]
    move_up(ahead, a1_ref, 2 * channels, rows)

    pre2[...] = dot(a1_ref[...], k2_ref[...])
    bias2 = rows_ref[12:13, :]
    gain2 = rows_ref[15:16, :]
    shift2 = rows_ref[18:19, :]
    limit = meta_ref[1:2, :]

    def layer_two(at, place, cot):
        x = pre2[at, :] + bias2
        x = x - jnp.mean(x, -1, keepdims=True)
        rstd = lax.rsqrt(jnp.mean(x * x, -1, keepdims=True) + EPS)
        hat = x * rstd
        z = hat * gain2 + shift2
        cdf, bell = normal_cdf(z)
        valid = place < limit
        up = jnp.where(valid, cot * scale, 0.0)
        dhat = up * ((cdf + z * bell * INV_SQRT_2PI) * gain2)
        mean_d = jnp.mean(dhat, -1, keepdims=True)
        mean_dh = jnp.mean(dhat * hat, -1, keepdims=True)
        d2 = rstd * (dhat - mean_d - hat * mean_dh)
        return jnp.where(valid, z * cdf, 0.0).astype(BF16), d2.astype(BF16)

    def step2(i, carry):
        start = pl.multiple_of(i * CH2, CH2)
        at = pl.ds(start, CH2)
        place = base + start + lax.broadcasted_iota(jnp.int32, (CH2, channels), 0)
        frames, d2 = layer_two(at, place, cot_ref[at, :].astype(F32))
        frames_ref[at, :] = frames
        d2_ref[at, :] = d2
        d2own[at, :] = d2
        return carry

    lax.fori_loop(0, groups // CH2, step2, 0, unroll=UN2)
    cot_tail = jnp.where(tail_row == TAIL - 1, preceding[:, 128:], 0.0)
    place = base + jnp.where(tail_row == TAIL - 1, -1, groups + tail_row)
    _, d2_ref[groups:rows, :] = layer_two(pl.ds(groups, TAIL), place, cot_tail)
    put_gradient(here.core, keep_ref, send_ref, [(a1_ref, 0, d2own)], keep_ref.shape[2])


def forward(
    a0, head, kept, edges, w0, kernel1, kernel2, table, meta, cot, scale, chunks, special
):
    groups = cot.shape[0]
    channels = cot.shape[1]
    rows = groups + TAIL
    taps_all = kernel1.shape[0]
    grad = (2, chunks, taps_all // chunks, BC)
    return pl.pallas_call(
        functools.partial(forward_kernel, special, groups, scale),
        out_shape=[
            sds((rows, 5 * channels), BF16),
            sds((groups, channels), BF16),
            sds(grad, F32),
            sds(grad, BF16),
            sds((2, rows, channels), F32),
            sds((2, rows, channels), F32),
            sds((2, rows, 128), F32),
            sds((rows, channels), BF16),
        ],
        in_specs=[VM] * 11,
        out_specs=[VM] * 8,
        scratch_shapes=[
            pltpu.VMEM((2 * TAIL, 4 * channels), F32),
            pltpu.VMEM((2, rows, channels), F32),
            pltpu.VMEM((rows, channels), F32),
            pltpu.VMEM((rows, 3 * channels), BF16),
            pltpu.VMEM((rows + 8, channels), F32),
            pltpu.VMEM((groups, channels), BF16),
        ],
        compiler_params=params(26),
        cost_estimate=cost(int(8e9), 10 << 20),
        name="forward",
    )(a0, head, kept, *edges, w0, kernel1, kernel2, table, meta, cot)


def window_kernel(d2_ref, k2_ref, hat_ref, slope_ref, rstd_ref, d1, dwin, behind):
    groups, channels = dwin.shape[1:]
    rows = groups + TAIL
    d2 = d2_ref[...]
    third = dot_nt(d2, k2_ref[2 * channels : 3 * channels, :])
    behind[8 : 8 + groups, :] = third[0:groups, :]
    behind[7:8, :] = third[rows - 1 : rows, :]
    dwin[0] = dot_nt(d2[0:groups, :], k2_ref[0:channels, :])
    dwin[1] = dot_nt(d2[0:groups, :], k2_ref[channels : 2 * channels, :])

    def step(i, carry):
        start = pl.multiple_of(i * CH3, CH3)
        at = pl.ds(start, CH3)
        for h in range(2):
            d = dwin[h, at, :]
            if h == 0:
                d = d + behind[pl.ds(start, CH3 + 8), :][7 : 7 + CH3, :]
            hat = hat_ref[h, at, :]
            dhat = d * slope_ref[h, at, :]
            mean_d = jnp.mean(dhat, -1, keepdims=True)
            mean_dh = jnp.mean(dhat * hat, -1, keepdims=True)
            rstd = rstd_ref[h, at, 0:1]
            d1[h, at, :] = (rstd * (dhat - mean_d - hat * mean_dh)).astype(BF16)
        return carry

    lax.fori_loop(0, groups // CH3, step, 0, unroll=UN3)


def window(d2, kernel2, hat, slope, rstd):
    rows, channels = d2.shape
    groups = rows - TAIL
    return pl.pallas_call(
        window_kernel,
        out_shape=sds((2, groups, channels), BF16),
        in_specs=[VM] * 5,
        out_specs=VM,
        scratch_shapes=[
            pltpu.VMEM((2, groups, channels), F32),
            pltpu.VMEM((groups + 8, channels), F32),
        ],
        compiler_params=params(16),
        cost_estimate=cost(int(1.5e9), 3 << 20),
        name="window",
    )(d2, kernel2, hat, slope, rstd)


def backward_kernel(special, d1, a0_ref, keep_ref, send_ref):
    here = Place(special)
    channels = d1.shape[2]
    put_gradient(
        here.core,
        keep_ref,
        send_ref,
        [(a0_ref, 0, d1.at[0]), (a0_ref, 2 * channels, d1.at[1])],
        keep_ref.shape[2],
    )


def backward(d1, a0, taps_all, chunks, special):
    grad = (2, chunks, taps_all // chunks, BC)
    return pl.pallas_call(
        functools.partial(backward_kernel, special),
        out_shape=[sds(grad, F32), sds(grad, BF16)],
        in_specs=[VM] * 2,
        out_specs=[VM] * 2,
        compiler_params=params(16),
        cost_estimate=cost(int(4e9), 10 << 20),
        name="backward",
    )(d1, a0)


def plane_kernel(keep_ref, recv_ref, *outs):
    here = Place(True)
    x, y = here.x, here.y
    for (dx, dy), out in zip(((0, 0), (1, 0), (0, 1), (1, 1)), outs):
        for zz in range(2):
            at = (x ^ dx, 2 * zz + (y ^ dy))
            out[zz] = (keep_ref[at] + recv_ref[at].astype(F32)).astype(out.dtype)


def plane(keep, recv, flops=1 << 20):
    shape = (2,) + keep.shape[2:]
    return pl.pallas_call(
        plane_kernel,
        out_shape=[sds(shape, F32)] + [sds(shape, BF16)] * 3,
        in_specs=[VM] * 2,
        out_specs=[VM] * 4,
        compiler_params=params(),
        cost_estimate=cost(flops, 5 << 20),
        name="plane",
    )(keep, recv)


def column_kernel(*refs):
    layers, outs = (refs[0:4], refs[4:8]), refs[8:]
    z = Place(True).z
    for dz, out in enumerate(outs):
        zz = z ^ dz
        at = lax.rem(zz, 2)
        for layer, (own, rx, ry, rd) in enumerate(layers):

            @pl.when(lax.div(zz, 2) == layer)
            def _():
                total = own[at] + rx[at].astype(F32) + ry[at].astype(F32) + rd[at].astype(F32)
                out[...] = total.astype(out.dtype)


def column(first, second):
    shape = first[0].shape[1:]
    return pl.pallas_call(
        column_kernel,
        out_shape=[sds(shape, F32)] + [sds(shape, BF16)] * 3,
        in_specs=[VM] * 8,
        out_specs=[VM] * 4,
        compiler_params=params(),
        cost_estimate=cost(1 << 20, 3 << 20),
        name="column",
    )(*first, *second)


def final_kernel(own, a, b, c, out):
    total = own[...] + a[...].astype(F32) + b[...].astype(F32) + c[...].astype(F32)
    out[...] = total.astype(out.dtype)


def final(own, a, b, c):
    return pl.pallas_call(
        final_kernel,
        out_shape=sds(own.shape, BF16),
        in_specs=[VM] * 4,
        out_specs=VM,
        compiler_params=params(),
        cost_estimate=cost(1 << 18, 1 << 19),
        name="final",
    )(own, a, b, c)


def stats_kernel(flips, count, *refs):
    pieces, (lprev, rprev), (left, right, lbuf, rbuf, sems) = refs[:count], refs[count : count + 2], refs[-5:]
    here = Place(True)
    copies = []
    for i, (piece, (dcore, dx)) in enumerate(zip(pieces, flips)):
        v = 2 * (here.core ^ dcore) + (here.x ^ dx)
        for u in range(2):
            slot = 2 * i + u
            q = 4 * u + v
            block = piece[u * BR : (u + 1) * BR, :]
            lbuf[slot] = BETA * lprev[q] + (1.0 - BETA) * dot_nt(block, block)
            rbuf[slot] = BETA * rprev[q] + (1.0 - BETA) * dot_tn(block, block)
            for buf, out, which in ((lbuf, left, 0), (rbuf, right, 1)):
                copy = pltpu.make_async_copy(buf.at[slot], out.at[q], sems.at[which, slot])
                copy.start()
                copies.append(copy)
    for copy in copies:
        copy.wait()


def stats(pieces, flips, lprev, rprev, begun=()):
    count = len(pieces)
    slots = 2 * count
    hbm = pl.BlockSpec(memory_space=pl.ANY)
    return pl.pallas_call(
        functools.partial(stats_kernel, flips, count),
        out_shape=[sds(lprev.shape, F32), sds(rprev.shape, F32)],
        in_specs=[VM] * (count + 2) + [hbm] * len(begun),
        out_specs=[hbm] * 2,
        input_output_aliases={count + 2 + i: i for i in range(len(begun))},
        scratch_shapes=[
            pltpu.VMEM((slots,) + lprev.shape[1:], F32),
            pltpu.VMEM((slots,) + rprev.shape[1:], F32),
            pltpu.SemaphoreType.DMA((2, slots)),
        ],
        compiler_params=params(),
        cost_estimate=cost(slots * int(2e7), slots << 18),
        name="stats",
    )(*pieces, lprev, rprev, *begun)


def permute(value, route):
    return lax.ppermute(value, AXES, route)


def body(
    audio,
    lengths,
    kernel0,
    kernel1,
    kernel2,
    conv_bias,
    norm_gain,
    norm_shift,
    cotangent,
    left_prev,
    right_prev,
):
    tms, batches = lax.axis_size("tm"), lax.axis_size("batch")
    t, b = lax.axis_index("tm"), lax.axis_index("batch")
    recordings, samples_dev = audio.shape
    piece_rows = samples_dev // 20
    groups = piece_rows * batches
    total = groups * tms
    scale = 1.0 / math.sqrt(total)

    def route(move):
        pairs = []
        for tt in range(tms):
            for bb in range(batches):
                to = move(tt, bb)
                if 0 <= to[0] < tms:
                    pairs.append((tt * batches + bb, to[0] * batches + to[1]))
        return pairs

    pieces = list(pack(audio))
    for k in range(1, batches):
        pieces[k] = permute(pieces[k], route(lambda tt, bb: (tt, bb ^ k)))

    def of_place(place, row, lane):
        chosen = pieces[0][row, lane : lane + 20]
        for k in range(1, batches):
            chosen = jnp.where((b ^ k) == place, pieces[k][row, lane : lane + 20], chosen)
        return chosen[None]

    cot = cotangent[0]
    last_row = cot[groups - 1 :].astype(F32)
    lengths_row = jnp.pad(lengths.astype(F32), (0, cot.shape[1] - recordings))[None]
    table, at = 0.0, 0
    for part in (kernel0, conv_bias, norm_gain, norm_shift, last_row, lengths_row):
        table += jnp.pad(part, ((at, 24 - at - part.shape[0]), (0, 0)))
        at += part.shape[0]
    w0, meta = prep(table)
    first_group = jnp.pad(of_place(0, 0, 0), ((0, 0), (0, 108 + cot.shape[1])))
    last_group = jnp.concatenate(
        [
            jnp.pad(of_place(batches - 1, -1, 20 * (PACK - 1)), ((0, 0), (0, 108))),
            table[19:20],
        ],
        1,
    )
    odd = t % 2 == 1
    edge_a = permute(jnp.where(odd, first_group, last_group), route(lambda tt, bb: (tt ^ 1, bb)))
    edge_b = permute(
        jnp.where(odd, last_group, first_group), route(lambda tt, bb: (tt + 2 * (tt % 2) - 1, bb))
    )

    special = tms == 8 and batches == 4
    chunks = 4
    a0, head, kept = audio_layer(pieces, w0, table, meta, special)
    a0, frames, keep2, send2, hat, slope, rstd, d2 = forward(
        a0,
        head,
        kept,
        (edge_a, edge_b),
        w0,
        kernel1,
        kernel2,
        table,
        meta,
        cot,
        scale,
        chunks,
        special,
    )
    d1 = window(d2, kernel2, hat, slope, rstd)

    def gradient_one():
        return backward(d1, a0, kernel1.shape[0], chunks, special)

    if not special:
        keep1, send1 = gradient_one()

        def blocks_of(keep, send):
            both = jnp.stack([keep, send.astype(F32)])
            both = both.reshape(2, 2, -1, BR, BC)
            return jnp.transpose(both, (2, 0, 1, 3, 4)).reshape(-1, BR, BC)

        stacked = jnp.concatenate([blocks_of(keep1, send1), blocks_of(keep2, send2)], 0)
        owned = lax.psum_scatter(stacked, "tm", scatter_dimension=0, tiled=True)
        owned = lax.psum(owned, "batch")
        left = BETA * left_prev + (1.0 - BETA) * jnp.einsum(
            "bik,bjk->bij", owned, owned, precision=lax.Precision.HIGHEST
        )
        right = BETA * right_prev + (1.0 - BETA) * jnp.einsum(
            "bki,bkj->bij", owned, owned, precision=lax.Precision.HIGHEST
        )
        return frames[None], left, right

    by_core = route(lambda tt, bb: (tt, bb ^ 1))
    by_x = route(lambda tt, bb: (tt, bb ^ 2))
    by_y = route(lambda tt, bb: (tt ^ 1, bb))
    by_xy = route(lambda tt, bb: (tt ^ 1, bb ^ 2))
    by_z = [route(lambda tt, bb: (tt ^ (2 * k), bb)) for k in range(1, 4)]

    def to_plane(tox, toy, tod):
        return permute(tox, by_x), permute(toy, by_y), permute(tod, by_xy)

    own2, *out = plane(keep2, permute(send2, by_core), int(1e10))
    second = (own2, *to_plane(*out))
    keep1, send1 = gradient_one()
    own1, *out = plane(keep1, permute(send1, by_core))
    own, *out = column((own1, *to_plane(*out)), second)
    arrived = [permute(value, way) for value, way in zip(out, by_z)]
    owned = final(own, *arrived)
    other = permute(owned, by_x)
    far = permute(owned, by_core), permute(other, by_core)
    begun = stats((owned, other), ((0, 0), (0, 1)), left_prev, right_prev)
    left, right = stats(far, ((1, 0), (1, 1)), left_prev, right_prev, begun)
    return frames[None], left, right


def solution(mesh):
    return jax.shard_map(
        body,
        mesh=mesh,
        in_specs=(
            P(None, AXES),
            P(),
            P(),
            P(),
            P(),
            P(),
            P(),
            P(),
            P("batch", "tm", None),
            P("tm", None, None),
            P("tm", None, None),
        ),
        out_specs=(P("batch", "tm", None), P("tm", None, None), P("tm", None, None)),
        check_vma=False,
    )
```

```python
import functools
import math

import jax
import jax.numpy as jnp
from jax import lax
from jax.experimental import pallas as pl
from jax.experimental.pallas import tpu as pltpu
from jax.sharding import PartitionSpec as P

BR = 192
BC = 128
EPS = 1e-05
BETA = 0.95
AXES = ("tm", "batch")
F32 = jnp.float32
BF16 = jnp.bfloat16
MIB = 1024 * 1024
CH = 16
PACK = 6
CH0, CH1, CH2, CH3 = 16,16,16,16
UN0, UN1, UN2, UN3 = 12, 25, 24, 24
TAIL = 16

VM = pl.BlockSpec(memory_space=pltpu.VMEM)
SM = pl.BlockSpec(memory_space=pltpu.SMEM)


def params(mib=12):
    return pltpu.CompilerParams(vmem_limit_bytes=mib * MIB)


def cost(flops, nbytes, trans=0):
    return pl.CostEstimate(flops=flops, bytes_accessed=nbytes, transcendentals=trans)


def sds(shape, dtype):
    return jax.ShapeDtypeStruct(shape, dtype)


def normal_cdf(z):
    bell = jnp.exp2(z * z * (-0.5 * math.log2(math.e)))
    return 0.5 + 0.5 * lax.erf(z * math.sqrt(0.5)), bell


INV_SQRT_2PI = 1.0 / math.sqrt(2.0 * math.pi)


def split3(x):
    hi = x.astype(BF16).astype(F32)
    rest = x - hi
    mid = rest.astype(BF16).astype(F32)
    return hi, mid, rest - mid


def prep_kernel(table_ref, w_ref, meta_ref, wide):
    channels = table_ref.shape[1]
    b = lax.axis_index("batch")
    lane = lax.broadcasted_iota(jnp.int32, (1, channels), 1)
    length = jnp.sum(jnp.where(lane == b, table_ref[20:21, :], 0.0), -1, keepdims=True)
    length = jnp.broadcast_to(length.astype(jnp.int32), meta_ref.shape)
    meta_row = lax.broadcasted_iota(jnp.int32, meta_ref.shape, 0)
    meta_ref[...] = jnp.where(meta_row == 0, length, lax.div(length, 20))
    wide[...] = jnp.zeros_like(wide)
    k0 = table_ref[0:10, :]
    k0 = k0 - jnp.mean(k0, -1, keepdims=True)
    bias = table_ref[10:11, :]
    bias = bias - jnp.mean(bias, -1, keepdims=True)
    parts = split3(k0)
    bparts = split3(bias)
    for block, part in enumerate((0, 1, 2, 0, 1, 0)):
        for g in range(4):
            cols = pl.ds(g * channels, channels)
            wide[pl.ds(block * 32 + 5 * g, 10), cols] = parts[part]
            if block < 3:
                wide[pl.ds(block * 32 + 31, 1), cols] = bparts[part]
    w_ref[...] = wide[...].astype(BF16)


def prep(table):
    channels = table.shape[1]
    return pl.pallas_call(
        prep_kernel,
        out_shape=[sds((256, 4 * channels), BF16), sds((8, channels), jnp.int32)],
        in_specs=[VM],
        out_specs=[VM] * 2,
        scratch_shapes=[pltpu.VMEM((256, 4 * channels), F32)],
        compiler_params=params(),
        cost_estimate=cost(4 * 256 * 2048, 1 << 20),
        name="prep",
    )(table)


def dot(a, b):
    return lax.dot_general(a, b, (((1,), (0,)), ((), ())), preferred_element_type=F32)


def dot_tn(a, b):
    return lax.dot_general(a, b, (((0,), (0,)), ((), ())), preferred_element_type=F32)


def dot_nt(a, b):
    return lax.dot_general(a, b, (((1,), (1,)), ((), ())), preferred_element_type=F32)


def put_gradient(halves, pairs):
    for which, out in halves:
        width, chunk = out.shape[-1], out.shape[2]
        half = 2 * width
        start = pl.multiple_of(which * half, half)
        for row in range(out.shape[1]):
            total = None
            for a_ref, offset, d_ref in pairs:
                groups = d_ref.shape[0]
                a = a_ref[0:groups, offset + row * chunk : offset + (row + 1) * chunk]
                piece = dot_tn(a, d_ref[:, pl.ds(start, half)])
                total = piece if total is None else total + piece
            out[0, row] = total[:, :width].astype(out.dtype)
            out[1, row] = total[:, width:].astype(out.dtype)


class Place:
    def __init__(self, special):
        t, b = lax.axis_index("tm"), lax.axis_index("batch")
        self.t, self.b = t, b
        self.core = lax.rem(b, 2) if special else 0
        self.x, self.y, self.z = lax.div(b, 2), lax.rem(t, 2), lax.div(t, 2)


def layer_zero(pre, at, gain0, shift0, channels, g):
    x = pre[at, pl.ds(g * channels, channels)]
    rstd = lax.rsqrt(jnp.mean(x * x, -1, keepdims=True) + EPS)
    z = x * rstd * gain0 + shift0
    cdf, _ = normal_cdf(z)
    return z * cdf


def taps(block, after):
    lane = lax.broadcasted_iota(jnp.int32, block.shape, 1)
    after = pltpu.roll(after, 20, 1)
    s = jnp.where(
        lane < 20, block, jnp.where(lane < 25, after, jnp.where(lane == 31, 1.0, 0.0))
    )
    hi, mid, low = split3(s)
    first = hi + pltpu.roll(hi, 32, 1) + pltpu.roll(hi, 64, 1) + pltpu.roll(mid, 96, 1)
    second = mid + pltpu.roll(low, 32, 1)
    return jnp.concatenate([first.astype(BF16), second.astype(BF16)], 1)


def move_up(source, target, offset, rows):
    channels = source.shape[1]

    def move(i, carry):
        at = pl.multiple_of(i * CH, CH)
        block = source[pl.ds(at, CH + 8), :]
        target[pl.ds(at, CH), offset : offset + channels] = block[1 : CH + 1, :].astype(BF16)
        return carry

    lax.fori_loop(0, rows // CH, move, 0, unroll=2)


def pack_kernel(audio, *refs):
    outs, (local, packed) = refs[:-2], refs[-2:]
    b = lax.axis_index("batch")
    recordings, samples = audio.shape
    part = samples // 20 // PACK
    pltpu.sync_copy(audio, local)
    x = local[...]
    blank = jnp.zeros((recordings, 128 - 20 * PACK), F32)
    for r in range(part):
        starts = [20 * (part * q + r) for q in range(PACK)]
        packed[:, r, :] = jnp.concatenate([x[:, at : at + 20] for at in starts] + [blank], 1)
    for k, out in enumerate(outs):
        out[...] = packed[b ^ k]


def pack(audio):
    recordings, samples = audio.shape
    part = samples // 20 // PACK
    return pl.pallas_call(
        pack_kernel,
        out_shape=[sds((part, 128), F32)] * recordings,
        in_specs=[pl.BlockSpec(memory_space=pltpu.HBM)],
        out_specs=[VM] * recordings,
        scratch_shapes=[
            pltpu.VMEM(audio.shape, F32),
            pltpu.VMEM((recordings, part, 128), F32),
        ],
        compiler_params=params(),
        cost_estimate=cost(1 << 16, 1 << 17),
        name="pack",
    )(audio)


def audio_kernel(
    special, p0, p1, p2, p3, w0_ref, rows_ref, meta_ref, a0_ref, head_ref, keep, samples, pre0, ahead
):
    here = Place(special)
    part = p0.shape[0]
    piece_rows = PACK * part
    groups = 4 * piece_rows
    channels = rows_ref.shape[1]
    length = meta_ref[0:1, 0:128]
    base = here.t * groups
    for k, piece in enumerate((p0, p1, p2, p3)):
        for q in range(PACK):
            place = pl.multiple_of((here.b ^ k) * piece_rows + q * part, 8)
            block = piece[...]
            samples[pl.ds(place, part), :] = pltpu.roll(block, 128 - 20 * q, 1) if q else block
    row = lax.broadcasted_iota(jnp.int32, (groups, 128), 0)
    lane = lax.broadcasted_iota(jnp.int32, (groups, 128), 1)
    s = jnp.where(((base + row) * 20 + lane < length) & (lane < 20), samples[...], 0.0)
    keep[0:8, :] = s[0:8]
    keep[8 : 8 + TAIL, :] = s[groups - TAIL :]
    pre0[...] = dot(taps(s, pltpu.roll(s, groups - 1, 0)), w0_ref[...])
    gain0 = rows_ref[13:14, :]
    shift0 = rows_ref[16:17, :]

    def step(i, carry):
        at = pl.ds(pl.multiple_of(i * CH0, CH0), CH0)
        for g in range(4):
            act = layer_zero(pre0, at, gain0, shift0, channels, g)
            a0_ref[at, pl.ds(g * channels, channels)] = act.astype(BF16)
            if g == 0:
                ahead[at, :] = act
        return carry

    lax.fori_loop(0, groups // CH0, step, 0, unroll=UN0)
    head_ref[...] = ahead[0:8, :]
    move_up(ahead, a0_ref, 4 * channels, groups)


def audio_layer(pieces, w0, table, meta, special):
    groups = 4 * PACK * pieces[0].shape[0]
    channels = table.shape[1]
    return pl.pallas_call(
        functools.partial(audio_kernel, special),
        out_shape=[
            sds((groups, 5 * channels), BF16),
            sds((8, channels), F32),
            sds((8 + TAIL, 128), F32),
        ],
        in_specs=[VM] * 7,
        out_specs=[VM] * 3,
        scratch_shapes=[
            pltpu.VMEM((groups, 128), F32),
            pltpu.VMEM((groups, 4 * channels), F32),
            pltpu.VMEM((groups + 8, channels), F32),
        ],
        compiler_params=params(16),
        cost_estimate=cost(int(3e9), 5 << 20),
        name="audio_layer",
    )(*pieces, w0, table, meta)


def forward_kernel(
    special,
    groups,
    scale,
    a0_in,
    head_in,
    kept,
    edge_a,
    edge_b,
    w0_ref,
    k1_ref,
    k2_ref,
    rows_ref,
    meta_ref,
    cot_ref,
    a0_ref,
    frames_ref,
    keep_ref,
    send_ref,
    hat_ref,
    slope_ref,
    rstd_ref,
    d2_ref,
    pre0,
    pre1,
    pre2,
    a1_ref,
    ahead,
    d2own,
):
    here = Place(special)
    rows = groups + TAIL
    channels = k1_ref.shape[1]
    length = meta_ref[0:1, 0:128]
    base = here.t * groups
    total = groups * lax.axis_size("tm")
    is_last = base + groups >= total
    odd = lax.rem(here.t, 2) == 1

    following = jnp.where(odd, edge_b[...], edge_a[...])
    preceding = jnp.where(odd, edge_a[...], edge_b[...])
    row = lax.broadcasted_iota(jnp.int32, (TAIL, 128), 0)
    lane = lax.broadcasted_iota(jnp.int32, (TAIL, 128), 1)
    group = base + jnp.where(row == TAIL - 1, -1, groups + row)
    tail = jnp.where(row == 0, following[:, :128], jnp.where(row == TAIL - 1, preceding[:, :128], 0.0))
    tail = jnp.where((group * 20 + lane < length) & (lane < 20), tail, 0.0)
    block = jnp.concatenate([kept[8 : 8 + TAIL, :], tail], 0)
    row = lax.broadcasted_iota(jnp.int32, (2 * TAIL, 128), 0)
    after = jnp.where(row == 2 * TAIL - 1, kept[0:1, :], pltpu.roll(block, 2 * TAIL - 1, 0))
    pre0[...] = dot(taps(block, after), w0_ref[...])
    tail_row = lax.broadcasted_iota(jnp.int32, (TAIL, channels), 0)
    drop = (tail_row == 0) & is_last
    gain0 = rows_ref[13:14, :]
    shift0 = rows_ref[16:17, :]
    a0_ref[0:groups, :] = a0_in[...]
    for g in range(4):
        cols = pl.ds(g * channels, channels)
        start = TAIL if g in (1, 2) else 0
        act = layer_zero(pre0, pl.ds(start, 2 * TAIL - start), gain0, shift0, channels, g)
        behind, act = act[: TAIL - start], act[TAIL - start :]
        act = jnp.where(drop, 0.0, act)
        a0_ref[groups:rows, cols] = act.astype(BF16)
        if g == 3:
            a0_ref[groups - TAIL : groups, cols] = behind.astype(BF16)
        if g == 0:
            both = jnp.concatenate([behind, act], 0)
            up_row = lax.broadcasted_iota(jnp.int32, both.shape, 0)
            up = jnp.where(
                up_row == 2 * TAIL - 1, head_in[0:1, :], pltpu.roll(both, 2 * TAIL - 1, 0)
            )
            a0_ref[groups - TAIL : rows, 4 * channels : 5 * channels] = up.astype(BF16)

    for h in range(2):
        pre1[h] = dot(a0_ref[:, 2 * h * channels : (2 * h + 3) * channels], k1_ref[...])
    bias1 = rows_ref[11:12, :]
    gain1 = rows_ref[14:15, :]
    shift1 = rows_ref[17:18, :]

    def step1(i, carry):
        at = pl.ds(pl.multiple_of(i * CH1, CH1), CH1)
        for h in range(2):
            x = pre1[h, at, :] + bias1
            x = x - jnp.mean(x, -1, keepdims=True)
            rstd = lax.rsqrt(jnp.mean(x * x, -1, keepdims=True) + EPS)
            hat = x * rstd
            z = hat * gain1 + shift1
            cdf, bell = normal_cdf(z)
            act = z * cdf
            hat_ref[h, at, :] = hat
            slope_ref[h, at, :] = (cdf + z * bell * INV_SQRT_2PI) * gain1
            rstd_ref[h, at, :] = jnp.broadcast_to(rstd, (CH1, 128))
            a1_ref[at, h * channels : (h + 1) * channels] = act.astype(BF16)
            if h == 0:
                ahead[at, :] = act
        return carry

    lax.fori_loop(0, rows // CH1, step1, 0, unroll=UN1)
    ahead[groups:rows, :] = jnp.where(drop, 0.0, ahead[groups:rows, :])
    ahead[rows : rows + 1, :] = ahead[0:1, :]
    move_up(ahead, a1_ref, 2 * channels, rows)

    pre2[...] = dot(a1_ref[...], k2_ref[...])
    bias2 = rows_ref[12:13, :]
    gain2 = rows_ref[15:16, :]
    shift2 = rows_ref[18:19, :]
    limit = meta_ref[1:2, :]

    def layer_two(at, place, cot):
        x = pre2[at, :] + bias2
        x = x - jnp.mean(x, -1, keepdims=True)
        rstd = lax.rsqrt(jnp.mean(x * x, -1, keepdims=True) + EPS)
        hat = x * rstd
        z = hat * gain2 + shift2
        cdf, bell = normal_cdf(z)
        valid = place < limit
        up = jnp.where(valid, cot * scale, 0.0)
        dhat = up * ((cdf + z * bell * INV_SQRT_2PI) * gain2)
        mean_d = jnp.mean(dhat, -1, keepdims=True)
        mean_dh = jnp.mean(dhat * hat, -1, keepdims=True)
        d2 = rstd * (dhat - mean_d - hat * mean_dh)
        return jnp.where(valid, z * cdf, 0.0).astype(BF16), d2.astype(BF16)

    def step2(i, carry):
        start = pl.multiple_of(i * CH2, CH2)
        at = pl.ds(start, CH2)
        place = base + start + lax.broadcasted_iota(jnp.int32, (CH2, channels), 0)
        frames, d2 = layer_two(at, place, cot_ref[at, :].astype(F32))
        frames_ref[at, :] = frames
        d2_ref[at, :] = d2
        d2own[at, :] = d2
        return carry

    lax.fori_loop(0, groups // CH2, step2, 0, unroll=UN2)
    cot_tail = jnp.where(tail_row == TAIL - 1, preceding[:, 128:], 0.0)
    place = base + jnp.where(tail_row == TAIL - 1, -1, groups + tail_row)
    _, d2_ref[groups:rows, :] = layer_two(pl.ds(groups, TAIL), place, cot_tail)
    put_gradient(((here.core, keep_ref), (1 - here.core, send_ref)), [(a1_ref, 0, d2own)])


def forward(
    a0, head, kept, edges, w0, kernel1, kernel2, table, meta, cot, scale, chunks, special
):
    groups = cot.shape[0]
    channels = cot.shape[1]
    rows = groups + TAIL
    taps_all = kernel1.shape[0]
    grad = (2, chunks, taps_all // chunks, BC)
    return pl.pallas_call(
        functools.partial(forward_kernel, special, groups, scale),
        out_shape=[
            sds((rows, 5 * channels), BF16),
            sds((groups, channels), BF16),
            sds(grad, F32),
            sds(grad, BF16),
            sds((2, rows, channels), F32),
            sds((2, rows, channels), F32),
            sds((2, rows, 128), F32),
            sds((rows, channels), BF16),
        ],
        in_specs=[VM] * 11,
        out_specs=[VM] * 8,
        scratch_shapes=[
            pltpu.VMEM((2 * TAIL, 4 * channels), F32),
            pltpu.VMEM((2, rows, channels), F32),
            pltpu.VMEM((rows, channels), F32),
            pltpu.VMEM((rows, 3 * channels), BF16),
            pltpu.VMEM((rows + 8, channels), F32),
            pltpu.VMEM((groups, channels), BF16),
        ],
        compiler_params=params(26),
        cost_estimate=cost(int(8e9), 10 << 20),
        name="forward",
    )(a0, head, kept, *edges, w0, kernel1, kernel2, table, meta, cot)


def window_kernel(special, d2_ref, k2_ref, hat_ref, slope_ref, rstd_ref, a0_ref, d1, keep_ref, dwin, behind):
    groups, channels = dwin.shape[1:]
    rows = groups + TAIL
    d2 = d2_ref[...]
    third = dot_nt(d2, k2_ref[2 * channels : 3 * channels, :])
    behind[8 : 8 + groups, :] = third[0:groups, :]
    behind[7:8, :] = third[rows - 1 : rows, :]
    dwin[0] = dot_nt(d2[0:groups, :], k2_ref[0:channels, :])
    dwin[1] = dot_nt(d2[0:groups, :], k2_ref[channels : 2 * channels, :])

    def step(i, carry):
        start = pl.multiple_of(i * CH3, CH3)
        at = pl.ds(start, CH3)
        for h in range(2):
            d = dwin[h, at, :]
            if h == 0:
                d = d + behind[pl.ds(start, CH3 + 8), :][7 : 7 + CH3, :]
            hat = hat_ref[h, at, :]
            dhat = d * slope_ref[h, at, :]
            mean_d = jnp.mean(dhat, -1, keepdims=True)
            mean_dh = jnp.mean(dhat * hat, -1, keepdims=True)
            rstd = rstd_ref[h, at, 0:1]
            d1[h, at, :] = (rstd * (dhat - mean_d - hat * mean_dh)).astype(BF16)
        return carry

    lax.fori_loop(0, groups // CH3, step, 0, unroll=UN3)
    put_gradient(((Place(special).core, keep_ref),), both_taps(a0_ref, d1))


def both_taps(a0_ref, d1):
    return [(a0_ref, 0, d1.at[0]), (a0_ref, 2 * d1.shape[2], d1.at[1])]


def window(d2, kernel2, hat, slope, rstd, a0, chunks, special):
    rows, channels = d2.shape
    groups = rows - TAIL
    return pl.pallas_call(
        functools.partial(window_kernel, special),
        out_shape=[
            sds((2, groups, channels), BF16),
            sds((2, chunks, kernel2.shape[0] // chunks, BC), F32),
        ],
        in_specs=[VM] * 6,
        out_specs=[VM] * 2,
        scratch_shapes=[
            pltpu.VMEM((2, groups, channels), F32),
            pltpu.VMEM((groups + 8, channels), F32),
        ],
        compiler_params=params(16),
        cost_estimate=cost(int(2.5e9), 3 << 20),
        name="window",
    )(d2, kernel2, hat, slope, rstd, a0)


def backward_kernel(special, d1, a0_ref, order_ref, send_ref):
    put_gradient(((1 - Place(special).core, send_ref),), both_taps(a0_ref, d1))


def backward(d1, a0, order, shape, special):
    return pl.pallas_call(
        functools.partial(backward_kernel, special),
        out_shape=sds(shape, BF16),
        in_specs=[VM] * 2 + [pl.BlockSpec(memory_space=pl.ANY)],
        out_specs=VM,
        compiler_params=params(16),
        cost_estimate=cost(int(2e9), 5 << 20),
        name="backward",
    )(d1, a0, order)


def plane_kernel(keep_ref, recv_ref, *outs):
    here = Place(True)
    x, y = here.x, here.y
    for (dx, dy), out in zip(((0, 0), (1, 0), (0, 1), (1, 1)), outs):
        for zz in range(2):
            at = (x ^ dx, 2 * zz + (y ^ dy))
            out[zz] = (keep_ref[at] + recv_ref[at].astype(F32)).astype(out.dtype)


def plane(keep, recv, flops=1 << 20):
    shape = (2,) + keep.shape[2:]
    return pl.pallas_call(
        plane_kernel,
        out_shape=[sds(shape, F32)] + [sds(shape, BF16)] * 3,
        in_specs=[VM] * 2,
        out_specs=[VM] * 4,
        compiler_params=params(),
        cost_estimate=cost(flops, 5 << 20),
        name="plane",
    )(keep, recv)


def column_kernel(*refs):
    layers, outs = (refs[0:4], refs[4:8]), refs[8:]
    z = Place(True).z
    for dz, out in zip((0, 2, 3, 1), outs):
        zz = z ^ dz
        at = lax.rem(zz, 2)
        for layer, (own, rx, ry, rd) in enumerate(layers):

            @pl.when(lax.div(zz, 2) == layer)
            def _():
                total = own[at] + rx[at].astype(F32) + ry[at].astype(F32) + rd[at].astype(F32)
                out[...] = total.astype(out.dtype)


def column(first, second):
    shape = first[0].shape[1:]
    return pl.pallas_call(
        column_kernel,
        out_shape=[sds(shape, F32)] + [sds(shape, BF16)] * 3,
        in_specs=[VM] * 8,
        out_specs=[VM] * 4,
        compiler_params=params(),
        cost_estimate=cost(1 << 20, 3 << 20),
        name="column",
    )(*first, *second)


def final_kernel(own, a, b, c, out):
    total = own[...] + a[...].astype(F32) + b[...].astype(F32) + c[...].astype(F32)
    out[...] = total.astype(out.dtype)


def final(own, a, b, c):
    return pl.pallas_call(
        final_kernel,
        out_shape=sds(own.shape, BF16),
        in_specs=[VM] * 4,
        out_specs=VM,
        compiler_params=params(),
        cost_estimate=cost(1 << 18, 1 << 19),
        name="final",
    )(own, a, b, c)


def stats_kernel(flips, count, *refs):
    pieces, (lprev, rprev), (left, right, lbuf, rbuf, sems) = refs[:count], refs[count : count + 2], refs[-5:]
    here = Place(True)
    copies = []
    for i, (piece, (dcore, dx)) in enumerate(zip(pieces, flips)):
        v = 2 * (here.core ^ dcore) + (here.x ^ dx)
        for u in range(2):
            slot = 2 * i + u
            q = 4 * u + v
            block = piece[u * BR : (u + 1) * BR, :]
            lbuf[slot] = BETA * lprev[q] + (1.0 - BETA) * dot_nt(block, block)
            rbuf[slot] = BETA * rprev[q] + (1.0 - BETA) * dot_tn(block, block)
            for buf, out, which in ((lbuf, left, 0), (rbuf, right, 1)):
                copy = pltpu.make_async_copy(buf.at[slot], out.at[q], sems.at[which, slot])
                copy.start()
                copies.append(copy)
    for copy in copies:
        copy.wait()


def stats(pieces, flips, lprev, rprev, begun=()):
    count = len(pieces)
    slots = 2 * count
    hbm = pl.BlockSpec(memory_space=pl.ANY)
    return pl.pallas_call(
        functools.partial(stats_kernel, flips, count),
        out_shape=[sds(lprev.shape, F32), sds(rprev.shape, F32)],
        in_specs=[VM] * (count + 2) + [hbm] * len(begun),
        out_specs=[hbm] * 2,
        input_output_aliases={count + 2 + i: i for i in range(len(begun))},
        scratch_shapes=[
            pltpu.VMEM((slots,) + lprev.shape[1:], F32),
            pltpu.VMEM((slots,) + rprev.shape[1:], F32),
            pltpu.SemaphoreType.DMA((2, slots)),
        ],
        compiler_params=params(),
        cost_estimate=cost(slots * int(2e7), slots << 18),
        name="stats",
    )(*pieces, lprev, rprev, *begun)


def permute(value, route):
    return lax.ppermute(value, AXES, route)


def body(
    audio,
    lengths,
    kernel0,
    kernel1,
    kernel2,
    conv_bias,
    norm_gain,
    norm_shift,
    cotangent,
    left_prev,
    right_prev,
):
    tms, batches = lax.axis_size("tm"), lax.axis_size("batch")
    t, b = lax.axis_index("tm"), lax.axis_index("batch")
    recordings, samples_dev = audio.shape
    piece_rows = samples_dev // 20
    groups = piece_rows * batches
    total = groups * tms
    scale = 1.0 / math.sqrt(total)

    def route(move):
        pairs = []
        for tt in range(tms):
            for bb in range(batches):
                to = move(tt, bb)
                if 0 <= to[0] < tms:
                    pairs.append((tt * batches + bb, to[0] * batches + to[1]))
        return pairs

    pieces = list(pack(audio))
    for k in range(1, batches):
        pieces[k] = permute(pieces[k], route(lambda tt, bb: (tt, bb ^ k)))

    def of_place(place, row, lane):
        chosen = pieces[0][row, lane : lane + 20]
        for k in range(1, batches):
            chosen = jnp.where((b ^ k) == place, pieces[k][row, lane : lane + 20], chosen)
        return chosen[None]

    cot = cotangent[0]
    last_row = cot[groups - 1 :].astype(F32)
    lengths_row = jnp.pad(lengths.astype(F32), (0, cot.shape[1] - recordings))[None]
    table, at = 0.0, 0
    for part in (kernel0, conv_bias, norm_gain, norm_shift, last_row, lengths_row):
        table += jnp.pad(part, ((at, 24 - at - part.shape[0]), (0, 0)))
        at += part.shape[0]
    w0, meta = prep(table)
    first_group = jnp.pad(of_place(0, 0, 0), ((0, 0), (0, 108 + cot.shape[1])))
    last_group = jnp.concatenate(
        [
            jnp.pad(of_place(batches - 1, -1, 20 * (PACK - 1)), ((0, 0), (0, 108))),
            table[19:20],
        ],
        1,
    )
    odd = t % 2 == 1
    edge_a = permute(jnp.where(odd, first_group, last_group), route(lambda tt, bb: (tt ^ 1, bb)))
    edge_b = permute(
        jnp.where(odd, last_group, first_group), route(lambda tt, bb: (tt + 2 * (tt % 2) - 1, bb))
    )

    special = tms == 8 and batches == 4
    chunks = 4
    a0, head, kept = audio_layer(pieces, w0, table, meta, special)
    a0, frames, keep2, send2, hat, slope, rstd, d2 = forward(
        a0,
        head,
        kept,
        (edge_a, edge_b),
        w0,
        kernel1,
        kernel2,
        table,
        meta,
        cot,
        scale,
        chunks,
        special,
    )
    d1, keep1 = window(d2, kernel2, hat, slope, rstd, a0, chunks, special)

    if not special:
        send1 = backward(d1, a0, keep2, keep1.shape, special)

        def blocks_of(keep, send):
            both = jnp.stack([keep, send.astype(F32)])
            both = both.reshape(2, 2, -1, BR, BC)
            return jnp.transpose(both, (2, 0, 1, 3, 4)).reshape(-1, BR, BC)

        stacked = jnp.concatenate([blocks_of(keep1, send1), blocks_of(keep2, send2)], 0)
        owned = lax.psum_scatter(stacked, "tm", scatter_dimension=0, tiled=True)
        owned = lax.psum(owned, "batch")
        left = BETA * left_prev + (1.0 - BETA) * jnp.einsum(
            "bik,bjk->bij", owned, owned, precision=lax.Precision.HIGHEST
        )
        right = BETA * right_prev + (1.0 - BETA) * jnp.einsum(
            "bki,bkj->bij", owned, owned, precision=lax.Precision.HIGHEST
        )
        return frames[None], left, right

    by_core = route(lambda tt, bb: (tt, bb ^ 1))
    by_x = route(lambda tt, bb: (tt, bb ^ 2))
    by_y = route(lambda tt, bb: (tt ^ 1, bb))
    by_xy = route(lambda tt, bb: (tt ^ 1, bb ^ 2))
    by_z = [route(lambda tt, bb: (tt ^ (2 * k), bb)) for k in (2, 3, 1)]

    def to_plane(tox, toy, tod):
        return permute(tox, by_x), permute(toy, by_y), permute(tod, by_xy)

    own2, *out = plane(keep2, permute(send2, by_core), int(1e10))
    second = (own2, *to_plane(*out))
    send1 = backward(d1, a0, own2, keep1.shape, special)
    own1, *out = plane(keep1, permute(send1, by_core))
    own, *out = column((own1, *to_plane(*out)), second)
    arrived = [permute(value, way) for value, way in zip(out, by_z)]
    owned = final(own, *arrived)
    other = permute(owned, by_x)
    far = permute(owned, by_core), permute(other, by_core)
    begun = stats((owned, other), ((0, 0), (0, 1)), left_prev, right_prev)
    left, right = stats(far, ((1, 0), (1, 1)), left_prev, right_prev, begun)
    return frames[None], left, right


def solution(mesh):
    return jax.shard_map(
        body,
        mesh=mesh,
        in_specs=(
            P(None, AXES),
            P(),
            P(),
            P(),
            P(),
            P(),
            P(),
            P(),
            P("batch", "tm", None),
            P("tm", None, None),
            P("tm", None, None),
        ),
        out_specs=(P("batch", "tm", None), P("tm", None, None), P("tm", None, None)),
        check_vma=False,
    )
```

```python
import functools
import math

import jax
import jax.numpy as jnp
from jax import lax
from jax.experimental import pallas as pl
from jax.experimental.pallas import tpu as pltpu
from jax.sharding import PartitionSpec as P

BR = 192
BC = 128
EPS = 1e-05
BETA = 0.95
AXES = ("tm", "batch")
F32 = jnp.float32
BF16 = jnp.bfloat16
MIB = 1024 * 1024
CH = 16
PACK = 6
CH0, CH1, CH2, CH3 = 16,16,16,16
UN0, UN1, UN2, UN3 = 24, 25, 24, 24
TAIL = 16

VM = pl.BlockSpec(memory_space=pltpu.VMEM)
SM = pl.BlockSpec(memory_space=pltpu.SMEM)


def params(mib=12):
    return pltpu.CompilerParams(vmem_limit_bytes=mib * MIB)


def cost(flops, nbytes, trans=0):
    return pl.CostEstimate(flops=flops, bytes_accessed=nbytes, transcendentals=trans)


def sds(shape, dtype):
    return jax.ShapeDtypeStruct(shape, dtype)


def normal_cdf(z):
    bell = jnp.exp2(z * z * (-0.5 * math.log2(math.e)))
    return 0.5 + 0.5 * lax.erf(z * math.sqrt(0.5)), bell


INV_SQRT_2PI = 1.0 / math.sqrt(2.0 * math.pi)


def split3(x):
    hi = x.astype(BF16).astype(F32)
    rest = x - hi
    mid = rest.astype(BF16).astype(F32)
    return hi, mid, rest - mid


def prep_kernel(table_ref, w_ref, meta_ref, wide):
    channels = table_ref.shape[1]
    b = lax.axis_index("batch")
    lane = lax.broadcasted_iota(jnp.int32, (1, channels), 1)
    length = jnp.sum(jnp.where(lane == b, table_ref[20:21, :], 0.0), -1, keepdims=True)
    length = jnp.broadcast_to(length.astype(jnp.int32), meta_ref.shape)
    meta_row = lax.broadcasted_iota(jnp.int32, meta_ref.shape, 0)
    meta_ref[...] = jnp.where(meta_row == 0, length, lax.div(length, 20))
    wide[...] = jnp.zeros_like(wide)
    k0 = table_ref[0:10, :]
    k0 = k0 - jnp.mean(k0, -1, keepdims=True)
    bias = table_ref[10:11, :]
    bias = bias - jnp.mean(bias, -1, keepdims=True)
    parts = split3(k0)
    bparts = split3(bias)
    for block, part in enumerate((0, 1, 2, 0, 1, 0)):
        for g in range(4):
            cols = pl.ds(g * channels, channels)
            wide[pl.ds(block * 32 + 5 * g, 10), cols] = parts[part]
            if block < 3:
                wide[pl.ds(block * 32 + 31, 1), cols] = bparts[part]
    w_ref[...] = wide[...].astype(BF16)


def prep(table):
    channels = table.shape[1]
    return pl.pallas_call(
        prep_kernel,
        out_shape=[sds((256, 4 * channels), BF16), sds((8, channels), jnp.int32)],
        in_specs=[VM],
        out_specs=[VM] * 2,
        scratch_shapes=[pltpu.VMEM((256, 4 * channels), F32)],
        compiler_params=params(),
        cost_estimate=cost(4 * 256 * 2048, 1 << 20),
        name="prep",
    )(table)


def dot(a, b):
    return lax.dot_general(a, b, (((1,), (0,)), ((), ())), preferred_element_type=F32)


def dot_tn(a, b):
    return lax.dot_general(a, b, (((0,), (0,)), ((), ())), preferred_element_type=F32)


def dot_nt(a, b):
    return lax.dot_general(a, b, (((1,), (1,)), ((), ())), preferred_element_type=F32)


def put_gradient(halves, pairs):
    for which, out in halves:
        width, chunk = out.shape[-1], out.shape[2]
        half = 2 * width
        start = pl.multiple_of(which * half, half)
        for row in range(out.shape[1]):
            total = None
            for a_ref, offset, d_ref in pairs:
                groups = d_ref.shape[0]
                a = a_ref[0:groups, offset + row * chunk : offset + (row + 1) * chunk]
                piece = dot_tn(a, d_ref[:, pl.ds(start, half)])
                total = piece if total is None else total + piece
            out[0, row] = total[:, :width].astype(out.dtype)
            out[1, row] = total[:, width:].astype(out.dtype)


class Place:
    def __init__(self, special):
        t, b = lax.axis_index("tm"), lax.axis_index("batch")
        self.t, self.b = t, b
        self.core = lax.rem(b, 2) if special else 0
        self.x, self.y, self.z = lax.div(b, 2), lax.rem(t, 2), lax.div(t, 2)


def layer_zero(pre, at, gain0, shift0, channels, g):
    x = pre[at, pl.ds(g * channels, channels)]
    rstd = lax.rsqrt(jnp.mean(x * x, -1, keepdims=True) + EPS)
    z = x * rstd * gain0 + shift0
    cdf, _ = normal_cdf(z)
    return z * cdf


def taps(block, after):
    lane = lax.broadcasted_iota(jnp.int32, block.shape, 1)
    after = pltpu.roll(after, 20, 1)
    s = jnp.where(
        lane < 20, block, jnp.where(lane < 25, after, jnp.where(lane == 31, 1.0, 0.0))
    )
    hi, mid, low = split3(s)
    first = hi + pltpu.roll(hi, 32, 1) + pltpu.roll(hi, 64, 1) + pltpu.roll(mid, 96, 1)
    second = mid + pltpu.roll(low, 32, 1)
    return jnp.concatenate([first.astype(BF16), second.astype(BF16)], 1)


def move_up(source, target, offset, rows):
    channels = source.shape[1]

    def move(i, carry):
        at = pl.multiple_of(i * CH, CH)
        block = source[pl.ds(at, CH + 8), :]
        target[pl.ds(at, CH), offset : offset + channels] = block[1 : CH + 1, :].astype(BF16)
        return carry

    lax.fori_loop(0, rows // CH, move, 0, unroll=2)


def pack_kernel(audio, *refs):
    outs, (local, packed) = refs[:-2], refs[-2:]
    b = lax.axis_index("batch")
    recordings, samples = audio.shape
    part = samples // 20 // PACK
    pltpu.sync_copy(audio, local)
    x = local[...]
    blank = jnp.zeros((recordings, 128 - 20 * PACK), F32)
    for r in range(part):
        starts = [20 * (part * q + r) for q in range(PACK)]
        packed[:, r, :] = jnp.concatenate([x[:, at : at + 20] for at in starts] + [blank], 1)
    for k, out in enumerate(outs):
        out[...] = packed[b ^ k]


def pack(audio):
    recordings, samples = audio.shape
    part = samples // 20 // PACK
    return pl.pallas_call(
        pack_kernel,
        out_shape=[sds((part, 128), F32)] * recordings,
        in_specs=[pl.BlockSpec(memory_space=pltpu.HBM)],
        out_specs=[VM] * recordings,
        scratch_shapes=[
            pltpu.VMEM(audio.shape, F32),
            pltpu.VMEM((recordings, part, 128), F32),
        ],
        compiler_params=params(),
        cost_estimate=cost(1 << 16, 1 << 17),
        name="pack",
    )(audio)


def audio_kernel(
    special, p0, p1, p2, p3, w0_ref, rows_ref, meta_ref, a0_ref, head_ref, keep, samples, pre0, ahead
):
    here = Place(special)
    part = p0.shape[0]
    piece_rows = PACK * part
    groups = 4 * piece_rows
    channels = rows_ref.shape[1]
    length = meta_ref[0:1, 0:128]
    base = here.t * groups
    for k, piece in enumerate((p0, p1, p2, p3)):
        for q in range(PACK):
            place = pl.multiple_of((here.b ^ k) * piece_rows + q * part, 8)
            block = piece[...]
            samples[pl.ds(place, part), :] = pltpu.roll(block, 128 - 20 * q, 1) if q else block
    row = lax.broadcasted_iota(jnp.int32, (groups, 128), 0)
    lane = lax.broadcasted_iota(jnp.int32, (groups, 128), 1)
    s = jnp.where(((base + row) * 20 + lane < length) & (lane < 20), samples[...], 0.0)
    keep[0:8, :] = s[0:8]
    keep[8 : 8 + TAIL, :] = s[groups - TAIL :]
    pre0[...] = dot(taps(s, pltpu.roll(s, groups - 1, 0)), w0_ref[...])
    gain0 = rows_ref[13:14, :]
    shift0 = rows_ref[16:17, :]

    def step(i, carry):
        at = pl.ds(pl.multiple_of(i * CH0, CH0), CH0)
        for g in range(4):
            act = layer_zero(pre0, at, gain0, shift0, channels, g)
            a0_ref[at, pl.ds(g * channels, channels)] = act.astype(BF16)
            if g == 0:
                ahead[at, :] = act
        return carry

    lax.fori_loop(0, groups // CH0, step, 0, unroll=UN0)
    head_ref[...] = ahead[0:8, :]
    move_up(ahead, a0_ref, 4 * channels, groups)


def audio_layer(pieces, w0, table, meta, special):
    groups = 4 * PACK * pieces[0].shape[0]
    channels = table.shape[1]
    return pl.pallas_call(
        functools.partial(audio_kernel, special),
        out_shape=[
            sds((groups, 5 * channels), BF16),
            sds((8, channels), F32),
            sds((8 + TAIL, 128), F32),
        ],
        in_specs=[VM] * 7,
        out_specs=[VM] * 3,
        scratch_shapes=[
            pltpu.VMEM((groups, 128), F32),
            pltpu.VMEM((groups, 4 * channels), F32),
            pltpu.VMEM((groups + 8, channels), F32),
        ],
        compiler_params=params(16),
        cost_estimate=cost(int(3e9), 5 << 20),
        name="audio_layer",
    )(*pieces, w0, table, meta)


def forward_kernel(
    special,
    groups,
    scale,
    a0_in,
    head_in,
    kept,
    edge_a,
    edge_b,
    w0_ref,
    k1_ref,
    k2_ref,
    rows_ref,
    meta_ref,
    cot_ref,
    a0_ref,
    frames_ref,
    keep_ref,
    send_ref,
    hat_ref,
    slope_ref,
    rstd_ref,
    d2_ref,
    pre0,
    pre1,
    pre2,
    a1_ref,
    ahead,
    d2own,
):
    here = Place(special)
    rows = groups + TAIL
    channels = k1_ref.shape[1]
    length = meta_ref[0:1, 0:128]
    base = here.t * groups
    total = groups * lax.axis_size("tm")
    is_last = base + groups >= total
    odd = lax.rem(here.t, 2) == 1

    following = jnp.where(odd, edge_b[...], edge_a[...])
    preceding = jnp.where(odd, edge_a[...], edge_b[...])
    row = lax.broadcasted_iota(jnp.int32, (TAIL, 128), 0)
    lane = lax.broadcasted_iota(jnp.int32, (TAIL, 128), 1)
    group = base + jnp.where(row == TAIL - 1, -1, groups + row)
    tail = jnp.where(row == 0, following[:, :128], jnp.where(row == TAIL - 1, preceding[:, :128], 0.0))
    tail = jnp.where((group * 20 + lane < length) & (lane < 20), tail, 0.0)
    block = jnp.concatenate([kept[8 : 8 + TAIL, :], tail], 0)
    row = lax.broadcasted_iota(jnp.int32, (2 * TAIL, 128), 0)
    after = jnp.where(row == 2 * TAIL - 1, kept[0:1, :], pltpu.roll(block, 2 * TAIL - 1, 0))
    pre0[...] = dot(taps(block, after), w0_ref[...])
    tail_row = lax.broadcasted_iota(jnp.int32, (TAIL, channels), 0)
    drop = (tail_row == 0) & is_last
    gain0 = rows_ref[13:14, :]
    shift0 = rows_ref[16:17, :]
    a0_ref[0:groups, :] = a0_in[...]
    for g in range(4):
        cols = pl.ds(g * channels, channels)
        start = TAIL if g in (1, 2) else 0
        act = layer_zero(pre0, pl.ds(start, 2 * TAIL - start), gain0, shift0, channels, g)
        behind, act = act[: TAIL - start], act[TAIL - start :]
        act = jnp.where(drop, 0.0, act)
        a0_ref[groups:rows, cols] = act.astype(BF16)
        if g == 3:
            a0_ref[groups - TAIL : groups, cols] = behind.astype(BF16)
        if g == 0:
            both = jnp.concatenate([behind, act], 0)
            up_row = lax.broadcasted_iota(jnp.int32, both.shape, 0)
            up = jnp.where(
                up_row == 2 * TAIL - 1, head_in[0:1, :], pltpu.roll(both, 2 * TAIL - 1, 0)
            )
            a0_ref[groups - TAIL : rows, 4 * channels : 5 * channels] = up.astype(BF16)

    for h in range(2):
        pre1[h] = dot(a0_ref[:, 2 * h * channels : (2 * h + 3) * channels], k1_ref[...])
    bias1 = rows_ref[11:12, :]
    gain1 = rows_ref[14:15, :]
    shift1 = rows_ref[17:18, :]

    def step1(i, carry):
        at = pl.ds(pl.multiple_of(i * CH1, CH1), CH1)
        for h in range(2):
            x = pre1[h, at, :] + bias1
            x = x - jnp.mean(x, -1, keepdims=True)
            rstd = lax.rsqrt(jnp.mean(x * x, -1, keepdims=True) + EPS)
            hat = x * rstd
            z = hat * gain1 + shift1
            cdf, bell = normal_cdf(z)
            act = z * cdf
            hat_ref[h, at, :] = hat
            slope_ref[h, at, :] = (cdf + z * bell * INV_SQRT_2PI) * gain1
            rstd_ref[h, at, :] = jnp.broadcast_to(rstd, (CH1, 128))
            a1_ref[at, h * channels : (h + 1) * channels] = act.astype(BF16)
            if h == 0:
                ahead[at, :] = act
        return carry

    lax.fori_loop(0, rows // CH1, step1, 0, unroll=UN1)
    ahead[groups:rows, :] = jnp.where(drop, 0.0, ahead[groups:rows, :])
    ahead[rows : rows + 1, :] = ahead[0:1, :]
    move_up(ahead, a1_ref, 2 * channels, rows)

    pre2[...] = dot(a1_ref[...], k2_ref[...])
    bias2 = rows_ref[12:13, :]
    gain2 = rows_ref[15:16, :]
    shift2 = rows_ref[18:19, :]
    limit = meta_ref[1:2, :]

    def layer_two(at, place, cot):
        x = pre2[at, :] + bias2
        x = x - jnp.mean(x, -1, keepdims=True)
        rstd = lax.rsqrt(jnp.mean(x * x, -1, keepdims=True) + EPS)
        hat = x * rstd
        z = hat * gain2 + shift2
        cdf, bell = normal_cdf(z)
        valid = place < limit
        up = jnp.where(valid, cot * scale, 0.0)
        dhat = up * ((cdf + z * bell * INV_SQRT_2PI) * gain2)
        mean_d = jnp.mean(dhat, -1, keepdims=True)
        mean_dh = jnp.mean(dhat * hat, -1, keepdims=True)
        d2 = rstd * (dhat - mean_d - hat * mean_dh)
        return jnp.where(valid, z * cdf, 0.0).astype(BF16), d2.astype(BF16)

    def step2(i, carry):
        start = pl.multiple_of(i * CH2, CH2)
        at = pl.ds(start, CH2)
        place = base + start + lax.broadcasted_iota(jnp.int32, (CH2, channels), 0)
        frames, d2 = layer_two(at, place, cot_ref[at, :].astype(F32))
        frames_ref[at, :] = frames
        d2_ref[at, :] = d2
        d2own[at, :] = d2
        return carry

    lax.fori_loop(0, groups // CH2, step2, 0, unroll=UN2)
    cot_tail = jnp.where(tail_row == TAIL - 1, preceding[:, 128:], 0.0)
    place = base + jnp.where(tail_row == TAIL - 1, -1, groups + tail_row)
    _, d2_ref[groups:rows, :] = layer_two(pl.ds(groups, TAIL), place, cot_tail)
    put_gradient(((here.core, keep_ref), (1 - here.core, send_ref)), [(a1_ref, 0, d2own)])


def forward(
    a0, head, kept, edges, w0, kernel1, kernel2, table, meta, cot, scale, chunks, special
):
    groups = cot.shape[0]
    channels = cot.shape[1]
    rows = groups + TAIL
    taps_all = kernel1.shape[0]
    grad = (2, chunks, taps_all // chunks, BC)
    return pl.pallas_call(
        functools.partial(forward_kernel, special, groups, scale),
        out_shape=[
            sds((rows, 5 * channels), BF16),
            sds((groups, channels), BF16),
            sds(grad, F32),
            sds(grad, BF16),
            sds((2, rows, channels), F32),
            sds((2, rows, channels), F32),
            sds((2, rows, 128), F32),
            sds((rows, channels), BF16),
        ],
        in_specs=[VM] * 11,
        out_specs=[VM] * 8,
        scratch_shapes=[
            pltpu.VMEM((2 * TAIL, 4 * channels), F32),
            pltpu.VMEM((2, rows, channels), F32),
            pltpu.VMEM((rows, channels), F32),
            pltpu.VMEM((rows, 3 * channels), BF16),
            pltpu.VMEM((rows + 8, channels), F32),
            pltpu.VMEM((groups, channels), BF16),
        ],
        compiler_params=params(26),
        cost_estimate=cost(int(8e9), 10 << 20),
        name="forward",
    )(a0, head, kept, *edges, w0, kernel1, kernel2, table, meta, cot)


def window_kernel(special, d2_ref, k2_ref, hat_ref, slope_ref, rstd_ref, a0_ref, d1, keep_ref, dwin, behind):
    groups, channels = dwin.shape[1:]
    rows = groups + TAIL
    d2 = d2_ref[...]
    third = dot_nt(d2, k2_ref[2 * channels : 3 * channels, :])
    behind[8 : 8 + groups, :] = third[0:groups, :]
    behind[7:8, :] = third[rows - 1 : rows, :]
    dwin[0] = dot_nt(d2[0:groups, :], k2_ref[0:channels, :])
    dwin[1] = dot_nt(d2[0:groups, :], k2_ref[channels : 2 * channels, :])

    def step(i, carry):
        start = pl.multiple_of(i * CH3, CH3)
        at = pl.ds(start, CH3)
        for h in range(2):
            d = dwin[h, at, :]
            if h == 0:
                d = d + behind[pl.ds(start, CH3 + 8), :][7 : 7 + CH3, :]
            hat = hat_ref[h, at, :]
            dhat = d * slope_ref[h, at, :]
            mean_d = jnp.mean(dhat, -1, keepdims=True)
            mean_dh = jnp.mean(dhat * hat, -1, keepdims=True)
            rstd = rstd_ref[h, at, 0:1]
            d1[h, at, :] = (rstd * (dhat - mean_d - hat * mean_dh)).astype(BF16)
        return carry

    lax.fori_loop(0, groups // CH3, step, 0, unroll=UN3)
    put_gradient(((Place(special).core, keep_ref),), both_taps(a0_ref, d1))


def both_taps(a0_ref, d1):
    return [(a0_ref, 0, d1.at[0]), (a0_ref, 2 * d1.shape[2], d1.at[1])]


def window(d2, kernel2, hat, slope, rstd, a0, chunks, special):
    rows, channels = d2.shape
    groups = rows - TAIL
    return pl.pallas_call(
        functools.partial(window_kernel, special),
        out_shape=[
            sds((2, groups, channels), BF16),
            sds((2, chunks, kernel2.shape[0] // chunks, BC), F32),
        ],
        in_specs=[VM] * 6,
        out_specs=[VM] * 2,
        scratch_shapes=[
            pltpu.VMEM((2, groups, channels), F32),
            pltpu.VMEM((groups + 8, channels), F32),
        ],
        compiler_params=params(16),
        cost_estimate=cost(int(2.5e9), 3 << 20),
        name="window",
    )(d2, kernel2, hat, slope, rstd, a0)


def backward_kernel(special, d1, a0_ref, order_ref, send_ref):
    put_gradient(((1 - Place(special).core, send_ref),), both_taps(a0_ref, d1))


def backward(d1, a0, order, shape, special):
    return pl.pallas_call(
        functools.partial(backward_kernel, special),
        out_shape=sds(shape, BF16),
        in_specs=[VM] * 2 + [pl.BlockSpec(memory_space=pl.ANY)],
        out_specs=VM,
        compiler_params=params(16),
        cost_estimate=cost(int(2e9), 5 << 20),
        name="backward",
    )(d1, a0, order)


def plane_kernel(keep_ref, recv_ref, *outs):
    here = Place(True)
    x, y = here.x, here.y
    for (dx, dy), out in zip(((0, 0), (1, 0), (0, 1), (1, 1)), outs):
        for zz in range(2):
            at = (x ^ dx, 2 * zz + (y ^ dy))
            out[zz] = (keep_ref[at] + recv_ref[at].astype(F32)).astype(out.dtype)


def plane(keep, recv, flops=1 << 20):
    shape = (2,) + keep.shape[2:]
    return pl.pallas_call(
        plane_kernel,
        out_shape=[sds(shape, F32)] + [sds(shape, BF16)] * 3,
        in_specs=[VM] * 2,
        out_specs=[VM] * 4,
        compiler_params=params(),
        cost_estimate=cost(flops, 5 << 20),
        name="plane",
    )(keep, recv)


def column_kernel(*refs):
    layers, outs = (refs[0:4], refs[4:8]), refs[8:]
    z = Place(True).z
    for dz, out in zip((0, 2, 3, 1), outs):
        zz = z ^ dz
        at = lax.rem(zz, 2)
        for layer, (own, rx, ry, rd) in enumerate(layers):

            @pl.when(lax.div(zz, 2) == layer)
            def _():
                total = own[at] + rx[at].astype(F32) + ry[at].astype(F32) + rd[at].astype(F32)
                out[...] = total.astype(out.dtype)


def column(first, second):
    shape = first[0].shape[1:]
    return pl.pallas_call(
        column_kernel,
        out_shape=[sds(shape, F32)] + [sds(shape, BF16)] * 3,
        in_specs=[VM] * 8,
        out_specs=[VM] * 4,
        compiler_params=params(),
        cost_estimate=cost(1 << 20, 3 << 20),
        name="column",
    )(*first, *second)


def final_kernel(own, a, b, c, out):
    total = own[...] + a[...].astype(F32) + b[...].astype(F32) + c[...].astype(F32)
    out[...] = total.astype(out.dtype)


def final(own, a, b, c):
    return pl.pallas_call(
        final_kernel,
        out_shape=sds(own.shape, BF16),
        in_specs=[VM] * 4,
        out_specs=VM,
        compiler_params=params(),
        cost_estimate=cost(1 << 18, 1 << 19),
        name="final",
    )(own, a, b, c)


def stats_kernel(flips, count, *refs):
    pieces, (lprev, rprev), (left, right, lbuf, rbuf, sems) = refs[:count], refs[count : count + 2], refs[-5:]
    here = Place(True)
    copies = []
    for i, (piece, (dcore, dx)) in enumerate(zip(pieces, flips)):
        v = 2 * (here.core ^ dcore) + (here.x ^ dx)
        for u in range(2):
            slot = 2 * i + u
            q = 4 * u + v
            block = piece[u * BR : (u + 1) * BR, :]
            lbuf[slot] = BETA * lprev[q] + (1.0 - BETA) * dot_nt(block, block)
            rbuf[slot] = BETA * rprev[q] + (1.0 - BETA) * dot_tn(block, block)
            for buf, out, which in ((lbuf, left, 0), (rbuf, right, 1)):
                copy = pltpu.make_async_copy(buf.at[slot], out.at[q], sems.at[which, slot])
                copy.start()
                copies.append(copy)
    for copy in copies:
        copy.wait()


def stats(pieces, flips, lprev, rprev, begun=()):
    count = len(pieces)
    slots = 2 * count
    hbm = pl.BlockSpec(memory_space=pl.ANY)
    return pl.pallas_call(
        functools.partial(stats_kernel, flips, count),
        out_shape=[sds(lprev.shape, F32), sds(rprev.shape, F32)],
        in_specs=[VM] * (count + 2) + [hbm] * len(begun),
        out_specs=[hbm] * 2,
        input_output_aliases={count + 2 + i: i for i in range(len(begun))},
        scratch_shapes=[
            pltpu.VMEM((slots,) + lprev.shape[1:], F32),
            pltpu.VMEM((slots,) + rprev.shape[1:], F32),
            pltpu.SemaphoreType.DMA((2, slots)),
        ],
        compiler_params=params(),
        cost_estimate=cost(slots * int(2e7), slots << 18),
        name="stats",
    )(*pieces, lprev, rprev, *begun)


def permute(value, route):
    return lax.ppermute(value, AXES, route)


def body(
    audio,
    lengths,
    kernel0,
    kernel1,
    kernel2,
    conv_bias,
    norm_gain,
    norm_shift,
    cotangent,
    left_prev,
    right_prev,
):
    tms, batches = lax.axis_size("tm"), lax.axis_size("batch")
    t, b = lax.axis_index("tm"), lax.axis_index("batch")
    recordings, samples_dev = audio.shape
    piece_rows = samples_dev // 20
    groups = piece_rows * batches
    total = groups * tms
    scale = 1.0 / math.sqrt(total)

    def route(move):
        pairs = []
        for tt in range(tms):
            for bb in range(batches):
                to = move(tt, bb)
                if 0 <= to[0] < tms:
                    pairs.append((tt * batches + bb, to[0] * batches + to[1]))
        return pairs

    pieces = list(pack(audio))
    for k in range(1, batches):
        pieces[k] = permute(pieces[k], route(lambda tt, bb: (tt, bb ^ k)))

    def of_place(place, row, lane):
        chosen = pieces[0][row, lane : lane + 20]
        for k in range(1, batches):
            chosen = jnp.where((b ^ k) == place, pieces[k][row, lane : lane + 20], chosen)
        return chosen[None]

    cot = cotangent[0]
    last_row = cot[groups - 1 :].astype(F32)
    lengths_row = jnp.pad(lengths.astype(F32), (0, cot.shape[1] - recordings))[None]
    table, at = 0.0, 0
    for part in (kernel0, conv_bias, norm_gain, norm_shift, last_row, lengths_row):
        table += jnp.pad(part, ((at, 24 - at - part.shape[0]), (0, 0)))
        at += part.shape[0]
    w0, meta = prep(table)
    first_group = jnp.pad(of_place(0, 0, 0), ((0, 0), (0, 108 + cot.shape[1])))
    last_group = jnp.concatenate(
        [
            jnp.pad(of_place(batches - 1, -1, 20 * (PACK - 1)), ((0, 0), (0, 108))),
            table[19:20],
        ],
        1,
    )
    odd = t % 2 == 1
    edge_a = permute(jnp.where(odd, first_group, last_group), route(lambda tt, bb: (tt ^ 1, bb)))
    edge_b = permute(
        jnp.where(odd, last_group, first_group), route(lambda tt, bb: (tt + 2 * (tt % 2) - 1, bb))
    )

    special = tms == 8 and batches == 4
    chunks = 4
    a0, head, kept = audio_layer(pieces, w0, table, meta, special)
    a0, frames, keep2, send2, hat, slope, rstd, d2 = forward(
        a0,
        head,
        kept,
        (edge_a, edge_b),
        w0,
        kernel1,
        kernel2,
        table,
        meta,
        cot,
        scale,
        chunks,
        special,
    )
    d1, keep1 = window(d2, kernel2, hat, slope, rstd, a0, chunks, special)

    if not special:
        send1 = backward(d1, a0, keep2, keep1.shape, special)

        def blocks_of(keep, send):
            both = jnp.stack([keep, send.astype(F32)])
            both = both.reshape(2, 2, -1, BR, BC)
            return jnp.transpose(both, (2, 0, 1, 3, 4)).reshape(-1, BR, BC)

        stacked = jnp.concatenate([blocks_of(keep1, send1), blocks_of(keep2, send2)], 0)
        owned = lax.psum_scatter(stacked, "tm", scatter_dimension=0, tiled=True)
        owned = lax.psum(owned, "batch")
        left = BETA * left_prev + (1.0 - BETA) * jnp.einsum(
            "bik,bjk->bij", owned, owned, precision=lax.Precision.HIGHEST
        )
        right = BETA * right_prev + (1.0 - BETA) * jnp.einsum(
            "bki,bkj->bij", owned, owned, precision=lax.Precision.HIGHEST
        )
        return frames[None], left, right

    by_core = route(lambda tt, bb: (tt, bb ^ 1))
    by_x = route(lambda tt, bb: (tt, bb ^ 2))
    by_y = route(lambda tt, bb: (tt ^ 1, bb))
    by_xy = route(lambda tt, bb: (tt ^ 1, bb ^ 2))
    by_z = [route(lambda tt, bb: (tt ^ (2 * k), bb)) for k in (2, 3, 1)]

    def to_plane(tox, toy, tod):
        return permute(tox, by_x), permute(toy, by_y), permute(tod, by_xy)

    own2, *out = plane(keep2, permute(send2, by_core), int(1e10))
    second = (own2, *to_plane(*out))
    send1 = backward(d1, a0, own2, keep1.shape, special)
    own1, *out = plane(keep1, permute(send1, by_core))
    tox, toy, tod = out
    first = (own1, permute(toy, by_y), permute(tod, by_xy), permute(tox, by_x))
    own, *out = column(first, second)
    arrived = [permute(value, way) for value, way in zip(out, by_z)]
    owned = final(own, *arrived)
    other = permute(owned, by_x)
    far = permute(owned, by_core), permute(other, by_core)
    begun = stats((owned, other), ((0, 0), (0, 1)), left_prev, right_prev)
    left, right = stats(far, ((1, 0), (1, 1)), left_prev, right_prev, begun)
    return frames[None], left, right


def solution(mesh):
    return jax.shard_map(
        body,
        mesh=mesh,
        in_specs=(
            P(None, AXES),
            P(),
            P(),
            P(),
            P(),
            P(),
            P(),
            P(),
            P("batch", "tm", None),
            P("tm", None, None),
            P("tm", None, None),
        ),
        out_specs=(P("batch", "tm", None), P("tm", None, None), P("tm", None, None)),
        check_vma=False,
    )
```

```python
import functools
import math

import jax
import jax.numpy as jnp
from jax import lax
from jax.experimental import pallas as pl
from jax.experimental.pallas import tpu as pltpu
from jax.sharding import PartitionSpec as P

BR = 192
BC = 128
EPS = 1e-05
BETA = 0.95
AXES = ("tm", "batch")
F32 = jnp.float32
BF16 = jnp.bfloat16
MIB = 1024 * 1024
CH = 16
PACK = 6
CH0, CH1, CH2, CH3 = 16,16,16,16
UN0, UN1, UN2, UN3 = 24, 25, 24, 24
TAIL = 16

VM = pl.BlockSpec(memory_space=pltpu.VMEM)
SM = pl.BlockSpec(memory_space=pltpu.SMEM)


def params(mib=12):
    return pltpu.CompilerParams(vmem_limit_bytes=mib * MIB)


def cost(flops, nbytes, trans=0):
    return pl.CostEstimate(flops=flops, bytes_accessed=nbytes, transcendentals=trans)


def sds(shape, dtype):
    return jax.ShapeDtypeStruct(shape, dtype)


def normal_cdf(z):
    bell = jnp.exp2(z * z * (-0.5 * math.log2(math.e)))
    return 0.5 + 0.5 * lax.erf(z * math.sqrt(0.5)), bell


INV_SQRT_2PI = 1.0 / math.sqrt(2.0 * math.pi)


def split3(x):
    hi = x.astype(BF16).astype(F32)
    rest = x - hi
    mid = rest.astype(BF16).astype(F32)
    return hi, mid, rest - mid


def prep_kernel(table_ref, w_ref, meta_ref, wide):
    channels = table_ref.shape[1]
    b = lax.axis_index("batch")
    lane = lax.broadcasted_iota(jnp.int32, (1, channels), 1)
    length = jnp.sum(jnp.where(lane == b, table_ref[20:21, :], 0.0), -1, keepdims=True)
    length = jnp.broadcast_to(length.astype(jnp.int32), meta_ref.shape)
    meta_row = lax.broadcasted_iota(jnp.int32, meta_ref.shape, 0)
    meta_ref[...] = jnp.where(meta_row == 0, length, lax.div(length, 20))
    wide[...] = jnp.zeros_like(wide)
    k0 = table_ref[0:10, :]
    k0 = k0 - jnp.mean(k0, -1, keepdims=True)
    bias = table_ref[10:11, :]
    bias = bias - jnp.mean(bias, -1, keepdims=True)
    parts = split3(k0)
    bparts = split3(bias)
    for block, part in enumerate((0, 1, 2, 0, 1, 0)):
        for g in range(4):
            cols = pl.ds(g * channels, channels)
            wide[pl.ds(block * 32 + 5 * g, 10), cols] = parts[part]
            if block < 3:
                wide[pl.ds(block * 32 + 31, 1), cols] = bparts[part]
    w_ref[...] = wide[...].astype(BF16)


def prep(table):
    channels = table.shape[1]
    return pl.pallas_call(
        prep_kernel,
        out_shape=[sds((256, 4 * channels), BF16), sds((8, channels), jnp.int32)],
        in_specs=[VM],
        out_specs=[VM] * 2,
        scratch_shapes=[pltpu.VMEM((256, 4 * channels), F32)],
        compiler_params=params(),
        cost_estimate=cost(4 * 256 * 2048, 1 << 20),
        name="prep",
    )(table)


def dot(a, b):
    return lax.dot_general(a, b, (((1,), (0,)), ((), ())), preferred_element_type=F32)


def dot_tn(a, b):
    return lax.dot_general(a, b, (((0,), (0,)), ((), ())), preferred_element_type=F32)


def dot_nt(a, b):
    return lax.dot_general(a, b, (((1,), (1,)), ((), ())), preferred_element_type=F32)


def put_gradient(halves, pairs):
    for which, out in halves:
        width, chunk = out.shape[-1], out.shape[2]
        half = 2 * width
        start = pl.multiple_of(which * half, half)
        for row in range(out.shape[1]):
            total = None
            for a_ref, offset, d_ref in pairs:
                groups = d_ref.shape[0]
                a = a_ref[0:groups, offset + row * chunk : offset + (row + 1) * chunk]
                piece = dot_tn(a, d_ref[:, pl.ds(start, half)])
                total = piece if total is None else total + piece
            out[0, row] = total[:, :width].astype(out.dtype)
            out[1, row] = total[:, width:].astype(out.dtype)


class Place:
    def __init__(self, special):
        t, b = lax.axis_index("tm"), lax.axis_index("batch")
        self.t, self.b = t, b
        self.core = lax.rem(b, 2) if special else 0
        self.x, self.y, self.z = lax.div(b, 2), lax.rem(t, 2), lax.div(t, 2)


def layer_zero(pre, at, gain0, shift0, channels, g):
    x = pre[at, pl.ds(g * channels, channels)]
    rstd = lax.rsqrt(jnp.mean(x * x, -1, keepdims=True) + EPS)
    z = x * rstd * gain0 + shift0
    cdf, _ = normal_cdf(z)
    return z * cdf


def taps(block, after):
    lane = lax.broadcasted_iota(jnp.int32, block.shape, 1)
    after = pltpu.roll(after, 20, 1)
    s = jnp.where(
        lane < 20, block, jnp.where(lane < 25, after, jnp.where(lane == 31, 1.0, 0.0))
    )
    hi, mid, low = split3(s)
    first = hi + pltpu.roll(hi, 32, 1) + pltpu.roll(hi, 64, 1) + pltpu.roll(mid, 96, 1)
    second = mid + pltpu.roll(low, 32, 1)
    return jnp.concatenate([first.astype(BF16), second.astype(BF16)], 1)


def move_up(source, target, offset, rows):
    channels = source.shape[1]

    def move(i, carry):
        at = pl.multiple_of(i * CH, CH)
        block = source[pl.ds(at, CH + 8), :]
        target[pl.ds(at, CH), offset : offset + channels] = block[1 : CH + 1, :].astype(BF16)
        return carry

    lax.fori_loop(0, rows // CH, move, 0, unroll=2)


def pack_kernel(audio, *refs):
    outs, (local, packed) = refs[:-2], refs[-2:]
    b = lax.axis_index("batch")
    recordings, samples = audio.shape
    part = samples // 20 // PACK
    pltpu.sync_copy(audio, local)
    x = local[...]
    blank = jnp.zeros((recordings, 128 - 20 * PACK), F32)
    for r in range(part):
        starts = [20 * (part * q + r) for q in range(PACK)]
        packed[:, r, :] = jnp.concatenate([x[:, at : at + 20] for at in starts] + [blank], 1)
    for k, out in enumerate(outs):
        out[...] = packed[b ^ k]


def pack(audio):
    recordings, samples = audio.shape
    part = samples // 20 // PACK
    return pl.pallas_call(
        pack_kernel,
        out_shape=[sds((part, 128), F32)] * recordings,
        in_specs=[pl.BlockSpec(memory_space=pltpu.HBM)],
        out_specs=[VM] * recordings,
        scratch_shapes=[
            pltpu.VMEM(audio.shape, F32),
            pltpu.VMEM((recordings, part, 128), F32),
        ],
        compiler_params=params(),
        cost_estimate=cost(1 << 16, 1 << 17),
        name="pack",
    )(audio)


def audio_kernel(
    special, p0, p1, p2, p3, w0_ref, rows_ref, meta_ref, a0_ref, head_ref, keep, samples, pre0, ahead
):
    here = Place(special)
    part = p0.shape[0]
    piece_rows = PACK * part
    groups = 4 * piece_rows
    channels = rows_ref.shape[1]
    length = meta_ref[0:1, 0:128]
    base = here.t * groups
    for k, piece in enumerate((p0, p1, p2, p3)):
        for q in range(PACK):
            place = pl.multiple_of((here.b ^ k) * piece_rows + q * part, 8)
            block = piece[...]
            samples[pl.ds(place, part), :] = pltpu.roll(block, 128 - 20 * q, 1) if q else block
    row = lax.broadcasted_iota(jnp.int32, (groups, 128), 0)
    lane = lax.broadcasted_iota(jnp.int32, (groups, 128), 1)
    s = jnp.where(((base + row) * 20 + lane < length) & (lane < 20), samples[...], 0.0)
    keep[0:8, :] = s[0:8]
    keep[8 : 8 + TAIL, :] = s[groups - TAIL :]
    pre0[...] = dot(taps(s, pltpu.roll(s, groups - 1, 0)), w0_ref[...])
    gain0 = rows_ref[13:14, :]
    shift0 = rows_ref[16:17, :]

    def step(i, carry):
        at = pl.ds(pl.multiple_of(i * CH0, CH0), CH0)
        for g in range(4):
            act = layer_zero(pre0, at, gain0, shift0, channels, g)
            a0_ref[at, pl.ds(g * channels, channels)] = act.astype(BF16)
            if g == 0:
                ahead[at, :] = act
        return carry

    lax.fori_loop(0, groups // CH0, step, 0, unroll=UN0)
    head_ref[...] = ahead[0:8, :]
    move_up(ahead, a0_ref, 4 * channels, groups)


def audio_layer(pieces, w0, table, meta, special):
    groups = 4 * PACK * pieces[0].shape[0]
    channels = table.shape[1]
    return pl.pallas_call(
        functools.partial(audio_kernel, special),
        out_shape=[
            sds((groups, 5 * channels), BF16),
            sds((8, channels), F32),
            sds((8 + TAIL, 128), F32),
        ],
        in_specs=[VM] * 7,
        out_specs=[VM] * 3,
        scratch_shapes=[
            pltpu.VMEM((groups, 128), F32),
            pltpu.VMEM((groups, 4 * channels), F32),
            pltpu.VMEM((groups + 8, channels), F32),
        ],
        compiler_params=params(16),
        cost_estimate=cost(int(3e9), 5 << 20),
        name="audio_layer",
    )(*pieces, w0, table, meta)


def forward_kernel(
    special,
    groups,
    scale,
    a0_in,
    head_in,
    kept,
    edge_a,
    edge_b,
    w0_ref,
    k1_ref,
    k2_ref,
    rows_ref,
    meta_ref,
    cot_ref,
    a0_ref,
    frames_ref,
    keep_ref,
    send_ref,
    hat_ref,
    slope_ref,
    rstd_ref,
    d2_ref,
    pre0,
    pre1,
    pre2,
    a1_ref,
    ahead,
    d2own,
):
    here = Place(special)
    rows = groups + TAIL
    channels = k1_ref.shape[1]
    length = meta_ref[0:1, 0:128]
    base = here.t * groups
    total = groups * lax.axis_size("tm")
    is_last = base + groups >= total
    odd = lax.rem(here.t, 2) == 1

    following = jnp.where(odd, edge_b[...], edge_a[...])
    preceding = jnp.where(odd, edge_a[...], edge_b[...])
    row = lax.broadcasted_iota(jnp.int32, (TAIL, 128), 0)
    lane = lax.broadcasted_iota(jnp.int32, (TAIL, 128), 1)
    group = base + jnp.where(row == TAIL - 1, -1, groups + row)
    tail = jnp.where(row == 0, following[:, :128], jnp.where(row == TAIL - 1, preceding[:, :128], 0.0))
    tail = jnp.where((group * 20 + lane < length) & (lane < 20), tail, 0.0)
    block = jnp.concatenate([kept[8 : 8 + TAIL, :], tail], 0)
    row = lax.broadcasted_iota(jnp.int32, (2 * TAIL, 128), 0)
    after = jnp.where(row == 2 * TAIL - 1, kept[0:1, :], pltpu.roll(block, 2 * TAIL - 1, 0))
    pre0[...] = dot(taps(block, after), w0_ref[...])
    tail_row = lax.broadcasted_iota(jnp.int32, (TAIL, channels), 0)
    drop = (tail_row == 0) & is_last
    gain0 = rows_ref[13:14, :]
    shift0 = rows_ref[16:17, :]
    a0_ref[0:groups, :] = a0_in[...]
    for g in range(4):
        cols = pl.ds(g * channels, channels)
        start = TAIL if g in (1, 2) else 0
        act = layer_zero(pre0, pl.ds(start, 2 * TAIL - start), gain0, shift0, channels, g)
        behind, act = act[: TAIL - start], act[TAIL - start :]
        act = jnp.where(drop, 0.0, act)
        a0_ref[groups:rows, cols] = act.astype(BF16)
        if g == 3:
            a0_ref[groups - TAIL : groups, cols] = behind.astype(BF16)
        if g == 0:
            both = jnp.concatenate([behind, act], 0)
            up_row = lax.broadcasted_iota(jnp.int32, both.shape, 0)
            up = jnp.where(
                up_row == 2 * TAIL - 1, head_in[0:1, :], pltpu.roll(both, 2 * TAIL - 1, 0)
            )
            a0_ref[groups - TAIL : rows, 4 * channels : 5 * channels] = up.astype(BF16)

    for h in range(2):
        pre1[h] = dot(a0_ref[:, 2 * h * channels : (2 * h + 3) * channels], k1_ref[...])
    bias1 = rows_ref[11:12, :]
    gain1 = rows_ref[14:15, :]
    shift1 = rows_ref[17:18, :]

    def step1(i, carry):
        at = pl.ds(pl.multiple_of(i * CH1, CH1), CH1)
        for h in range(2):
            x = pre1[h, at, :] + bias1
            x = x - jnp.mean(x, -1, keepdims=True)
            rstd = lax.rsqrt(jnp.mean(x * x, -1, keepdims=True) + EPS)
            hat = x * rstd
            z = hat * gain1 + shift1
            cdf, bell = normal_cdf(z)
            act = z * cdf
            hat_ref[h, at, :] = hat
            slope_ref[h, at, :] = (cdf + z * bell * INV_SQRT_2PI) * gain1
            rstd_ref[h, at, :] = jnp.broadcast_to(rstd, (CH1, 128))
            a1_ref[at, h * channels : (h + 1) * channels] = act.astype(BF16)
            if h == 0:
                ahead[at, :] = act
        return carry

    lax.fori_loop(0, rows // CH1, step1, 0, unroll=UN1)
    ahead[groups:rows, :] = jnp.where(drop, 0.0, ahead[groups:rows, :])
    ahead[rows : rows + 1, :] = ahead[0:1, :]
    move_up(ahead, a1_ref, 2 * channels, rows)

    pre2[...] = dot(a1_ref[...], k2_ref[...])
    bias2 = rows_ref[12:13, :]
    gain2 = rows_ref[15:16, :]
    shift2 = rows_ref[18:19, :]
    limit = meta_ref[1:2, :]

    def layer_two(at, place, cot):
        x = pre2[at, :] + bias2
        x = x - jnp.mean(x, -1, keepdims=True)
        rstd = lax.rsqrt(jnp.mean(x * x, -1, keepdims=True) + EPS)
        hat = x * rstd
        z = hat * gain2 + shift2
        cdf, bell = normal_cdf(z)
        valid = place < limit
        up = jnp.where(valid, cot * scale, 0.0)
        dhat = up * ((cdf + z * bell * INV_SQRT_2PI) * gain2)
        mean_d = jnp.mean(dhat, -1, keepdims=True)
        mean_dh = jnp.mean(dhat * hat, -1, keepdims=True)
        d2 = rstd * (dhat - mean_d - hat * mean_dh)
        return jnp.where(valid, z * cdf, 0.0).astype(BF16), d2.astype(BF16)

    def step2(i, carry):
        start = pl.multiple_of(i * CH2, CH2)
        at = pl.ds(start, CH2)
        place = base + start + lax.broadcasted_iota(jnp.int32, (CH2, channels), 0)
        frames, d2 = layer_two(at, place, cot_ref[at, :].astype(F32))
        frames_ref[at, :] = frames
        d2_ref[at, :] = d2
        d2own[at, :] = d2
        return carry

    lax.fori_loop(0, groups // CH2, step2, 0, unroll=UN2)
    cot_tail = jnp.where(tail_row == TAIL - 1, preceding[:, 128:], 0.0)
    place = base + jnp.where(tail_row == TAIL - 1, -1, groups + tail_row)
    _, d2_ref[groups:rows, :] = layer_two(pl.ds(groups, TAIL), place, cot_tail)
    put_gradient(((here.core, keep_ref), (1 - here.core, send_ref)), [(a1_ref, 0, d2own)])


def forward(
    a0, head, kept, edges, w0, kernel1, kernel2, table, meta, cot, scale, chunks, special
):
    groups = cot.shape[0]
    channels = cot.shape[1]
    rows = groups + TAIL
    taps_all = kernel1.shape[0]
    grad = (2, chunks, taps_all // chunks, BC)
    return pl.pallas_call(
        functools.partial(forward_kernel, special, groups, scale),
        out_shape=[
            sds((rows, 5 * channels), BF16),
            sds((groups, channels), BF16),
            sds(grad, F32),
            sds(grad, BF16),
            sds((2, rows, channels), F32),
            sds((2, rows, channels), F32),
            sds((2, rows, 128), F32),
            sds((rows, channels), BF16),
        ],
        in_specs=[VM] * 11,
        out_specs=[VM] * 8,
        scratch_shapes=[
            pltpu.VMEM((2 * TAIL, 4 * channels), F32),
            pltpu.VMEM((2, rows, channels), F32),
            pltpu.VMEM((rows, channels), F32),
            pltpu.VMEM((rows, 3 * channels), BF16),
            pltpu.VMEM((rows + 8, channels), F32),
            pltpu.VMEM((groups, channels), BF16),
        ],
        compiler_params=params(26),
        cost_estimate=cost(int(8e9), 10 << 20),
        name="forward",
    )(a0, head, kept, *edges, w0, kernel1, kernel2, table, meta, cot)


def window_kernel(special, d2_ref, k2_ref, hat_ref, slope_ref, rstd_ref, a0_ref, d1, keep_ref, dwin, behind):
    groups, channels = dwin.shape[1:]
    rows = groups + TAIL
    d2 = d2_ref[...]
    third = dot_nt(d2, k2_ref[2 * channels : 3 * channels, :])
    behind[8 : 8 + groups, :] = third[0:groups, :]
    behind[7:8, :] = third[rows - 1 : rows, :]
    dwin[0] = dot_nt(d2[0:groups, :], k2_ref[0:channels, :])
    dwin[1] = dot_nt(d2[0:groups, :], k2_ref[channels : 2 * channels, :])

    def step(i, carry):
        start = pl.multiple_of(i * CH3, CH3)
        at = pl.ds(start, CH3)
        for h in range(2):
            d = dwin[h, at, :]
            if h == 0:
                d = d + behind[pl.ds(start, CH3 + 8), :][7 : 7 + CH3, :]
            hat = hat_ref[h, at, :]
            dhat = d * slope_ref[h, at, :]
            mean_d = jnp.mean(dhat, -1, keepdims=True)
            mean_dh = jnp.mean(dhat * hat, -1, keepdims=True)
            rstd = rstd_ref[h, at, 0:1]
            d1[h, at, :] = (rstd * (dhat - mean_d - hat * mean_dh)).astype(BF16)
        return carry

    lax.fori_loop(0, groups // CH3, step, 0, unroll=UN3)
    put_gradient(((Place(special).core, keep_ref),), both_taps(a0_ref, d1))


def both_taps(a0_ref, d1):
    return [(a0_ref, 0, d1.at[0]), (a0_ref, 2 * d1.shape[2], d1.at[1])]


def window(d2, kernel2, hat, slope, rstd, a0, chunks, special):
    rows, channels = d2.shape
    groups = rows - TAIL
    return pl.pallas_call(
        functools.partial(window_kernel, special),
        out_shape=[
            sds((2, groups, channels), BF16),
            sds((2, chunks, kernel2.shape[0] // chunks, BC), F32),
        ],
        in_specs=[VM] * 6,
        out_specs=[VM] * 2,
        scratch_shapes=[
            pltpu.VMEM((2, groups, channels), F32),
            pltpu.VMEM((groups + 8, channels), F32),
        ],
        compiler_params=params(16),
        cost_estimate=cost(int(2.5e9), 3 << 20),
        name="window",
    )(d2, kernel2, hat, slope, rstd, a0)


def backward_kernel(special, d1, a0_ref, order_ref, send_ref):
    put_gradient(((1 - Place(special).core, send_ref),), both_taps(a0_ref, d1))


def backward(d1, a0, order, shape, special):
    return pl.pallas_call(
        functools.partial(backward_kernel, special),
        out_shape=sds(shape, BF16),
        in_specs=[VM] * 2 + [pl.BlockSpec(memory_space=pl.ANY)],
        out_specs=VM,
        compiler_params=params(16),
        cost_estimate=cost(int(2e9), 5 << 20),
        name="backward",
    )(d1, a0, order)


def plane_kernel(keep_ref, recv_ref, *outs):
    here = Place(True)
    x, y = here.x, here.y
    for (dx, dy), out in zip(((0, 0), (1, 0), (0, 1), (1, 1)), outs):
        for zz in range(2):
            at = (x ^ dx, 2 * zz + (y ^ dy))
            out[zz] = (keep_ref[at] + recv_ref[at].astype(F32)).astype(out.dtype)


def plane(keep, recv, flops=1 << 20):
    shape = (2,) + keep.shape[2:]
    return pl.pallas_call(
        plane_kernel,
        out_shape=[sds(shape, F32)] + [sds(shape, BF16)] * 3,
        in_specs=[VM] * 2,
        out_specs=[VM] * 4,
        compiler_params=params(),
        cost_estimate=cost(flops, 5 << 20),
        name="plane",
    )(keep, recv)


def column_kernel(*refs):
    layers, outs = (refs[0:4], refs[4:8]), refs[8:]
    z = Place(True).z
    for dz, out in zip((0, 2, 3, 1), outs):
        zz = z ^ dz
        at = lax.rem(zz, 2)
        for layer, (own, rx, ry, rd) in enumerate(layers):

            @pl.when(lax.div(zz, 2) == layer)
            def _():
                total = own[at] + rx[at].astype(F32) + ry[at].astype(F32) + rd[at].astype(F32)
                out[...] = total.astype(out.dtype)


def column(first, second):
    shape = first[0].shape[1:]
    return pl.pallas_call(
        column_kernel,
        out_shape=[sds(shape, F32)] + [sds(shape, BF16)] * 3,
        in_specs=[VM] * 8,
        out_specs=[VM] * 4,
        compiler_params=params(),
        cost_estimate=cost(1 << 20, 3 << 20),
        name="column",
    )(*first, *second)


def final_kernel(own, a, b, c, out):
    total = own[...] + a[...].astype(F32) + b[...].astype(F32) + c[...].astype(F32)
    out[...] = total.astype(out.dtype)


def final(own, a, b, c):
    return pl.pallas_call(
        final_kernel,
        out_shape=sds(own.shape, BF16),
        in_specs=[VM] * 4,
        out_specs=VM,
        compiler_params=params(),
        cost_estimate=cost(1 << 18, 1 << 19),
        name="final",
    )(own, a, b, c)


def stats_kernel(flips, count, *refs):
    pieces, (lprev, rprev), (left, right, lbuf, rbuf, sems) = refs[:count], refs[count : count + 2], refs[-5:]
    here = Place(True)
    copies = []
    for i, (piece, (dcore, dx)) in enumerate(zip(pieces, flips)):
        v = 2 * (here.core ^ dcore) + (here.x ^ dx)
        for u in range(2):
            slot = 2 * i + u
            q = 4 * u + v
            block = piece[u * BR : (u + 1) * BR, :]
            lbuf[slot] = BETA * lprev[q] + (1.0 - BETA) * dot_nt(block, block)
            rbuf[slot] = BETA * rprev[q] + (1.0 - BETA) * dot_tn(block, block)
            for buf, out, which in ((lbuf, left, 0), (rbuf, right, 1)):
                copy = pltpu.make_async_copy(buf.at[slot], out.at[q], sems.at[which, slot])
                copy.start()
                copies.append(copy)
    for copy in copies:
        copy.wait()


def stats(pieces, flips, lprev, rprev, begun=(), flops=int(1e8)):
    count = len(pieces)
    slots = 2 * count
    hbm = pl.BlockSpec(memory_space=pl.ANY)
    return pl.pallas_call(
        functools.partial(stats_kernel, flips, count),
        out_shape=[sds(lprev.shape, F32), sds(rprev.shape, F32)],
        in_specs=[VM] * (count + 2) + [hbm] * len(begun),
        out_specs=[hbm] * 2,
        input_output_aliases={count + 2 + i: i for i in range(len(begun))},
        scratch_shapes=[
            pltpu.VMEM((slots,) + lprev.shape[1:], F32),
            pltpu.VMEM((slots,) + rprev.shape[1:], F32),
            pltpu.SemaphoreType.DMA((2, slots)),
        ],
        compiler_params=params(),
        cost_estimate=cost(flops, slots << 18),
        name="stats",
    )(*pieces, lprev, rprev, *begun)


def relay_kernel(source, order, out):
    out[...] = source[...]


def relay(source, order):
    return pl.pallas_call(
        relay_kernel,
        out_shape=sds(source.shape, source.dtype),
        in_specs=[VM, pl.BlockSpec(memory_space=pl.ANY)],
        out_specs=VM,
        compiler_params=params(),
        name="relay",
    )(source, order)


def permute(value, route):
    return lax.ppermute(value, AXES, route)


def body(
    audio,
    lengths,
    kernel0,
    kernel1,
    kernel2,
    conv_bias,
    norm_gain,
    norm_shift,
    cotangent,
    left_prev,
    right_prev,
):
    tms, batches = lax.axis_size("tm"), lax.axis_size("batch")
    t, b = lax.axis_index("tm"), lax.axis_index("batch")
    recordings, samples_dev = audio.shape
    piece_rows = samples_dev // 20
    groups = piece_rows * batches
    total = groups * tms
    scale = 1.0 / math.sqrt(total)

    def route(move):
        pairs = []
        for tt in range(tms):
            for bb in range(batches):
                to = move(tt, bb)
                if 0 <= to[0] < tms:
                    pairs.append((tt * batches + bb, to[0] * batches + to[1]))
        return pairs

    pieces = list(pack(audio))
    for k in range(1, batches):
        pieces[k] = permute(pieces[k], route(lambda tt, bb: (tt, bb ^ k)))

    def of_place(place, row, lane):
        chosen = pieces[0][row, lane : lane + 20]
        for k in range(1, batches):
            chosen = jnp.where((b ^ k) == place, pieces[k][row, lane : lane + 20], chosen)
        return chosen[None]

    cot = cotangent[0]
    last_row = cot[groups - 1 :].astype(F32)
    lengths_row = jnp.pad(lengths.astype(F32), (0, cot.shape[1] - recordings))[None]
    table, at = 0.0, 0
    for part in (kernel0, conv_bias, norm_gain, norm_shift, last_row, lengths_row):
        table += jnp.pad(part, ((at, 24 - at - part.shape[0]), (0, 0)))
        at += part.shape[0]
    w0, meta = prep(table)
    first_group = jnp.pad(of_place(0, 0, 0), ((0, 0), (0, 108 + cot.shape[1])))
    last_group = jnp.concatenate(
        [
            jnp.pad(of_place(batches - 1, -1, 20 * (PACK - 1)), ((0, 0), (0, 108))),
            table[19:20],
        ],
        1,
    )
    odd = t % 2 == 1
    edge_a = permute(jnp.where(odd, first_group, last_group), route(lambda tt, bb: (tt ^ 1, bb)))
    edge_b = permute(
        jnp.where(odd, last_group, first_group), route(lambda tt, bb: (tt + 2 * (tt % 2) - 1, bb))
    )

    special = tms == 8 and batches == 4
    chunks = 4
    a0, head, kept = audio_layer(pieces, w0, table, meta, special)
    a0, frames, keep2, send2, hat, slope, rstd, d2 = forward(
        a0,
        head,
        kept,
        (edge_a, edge_b),
        w0,
        kernel1,
        kernel2,
        table,
        meta,
        cot,
        scale,
        chunks,
        special,
    )
    d1, keep1 = window(d2, kernel2, hat, slope, rstd, a0, chunks, special)

    if not special:
        send1 = backward(d1, a0, keep2, keep1.shape, special)

        def blocks_of(keep, send):
            both = jnp.stack([keep, send.astype(F32)])
            both = both.reshape(2, 2, -1, BR, BC)
            return jnp.transpose(both, (2, 0, 1, 3, 4)).reshape(-1, BR, BC)

        stacked = jnp.concatenate([blocks_of(keep1, send1), blocks_of(keep2, send2)], 0)
        owned = lax.psum_scatter(stacked, "tm", scatter_dimension=0, tiled=True)
        owned = lax.psum(owned, "batch")
        left = BETA * left_prev + (1.0 - BETA) * jnp.einsum(
            "bik,bjk->bij", owned, owned, precision=lax.Precision.HIGHEST
        )
        right = BETA * right_prev + (1.0 - BETA) * jnp.einsum(
            "bki,bkj->bij", owned, owned, precision=lax.Precision.HIGHEST
        )
        return frames[None], left, right

    by_core = route(lambda tt, bb: (tt, bb ^ 1))
    by_x = route(lambda tt, bb: (tt, bb ^ 2))
    by_y = route(lambda tt, bb: (tt ^ 1, bb))
    by_xy = route(lambda tt, bb: (tt ^ 1, bb ^ 2))
    by_z = [route(lambda tt, bb: (tt ^ (2 * k), bb)) for k in (2, 3, 1)]

    def to_plane(tox, toy, tod):
        return permute(tox, by_x), permute(toy, by_y), permute(tod, by_xy)

    own2, *out = plane(keep2, permute(send2, by_core), int(1e10))
    second = (own2, *to_plane(*out))
    send1 = backward(d1, a0, own2, keep1.shape, special)
    own1, *out = plane(keep1, permute(send1, by_core))
    tox, toy, tod = out
    first = (own1, permute(toy, by_y), permute(tod, by_xy), permute(tox, by_x))
    own, *out = column(first, second)
    arrived = [permute(value, way) for value, way in zip(out, by_z)]
    owned = final(own, *arrived)
    other = permute(owned, by_x)
    near = permute(owned, by_core)
    begun = stats((owned, near), ((0, 0), (1, 0)), left_prev, right_prev, flops=int(2e9))
    other = relay(other, begun[0])
    far = permute(other, by_core)
    begun = stats((other,), ((0, 1),), left_prev, right_prev, begun, int(1e10))
    left, right = stats((far,), ((1, 1),), left_prev, right_prev, begun)
    return frames[None], left, right


def solution(mesh):
    return jax.shard_map(
        body,
        mesh=mesh,
        in_specs=(
            P(None, AXES),
            P(),
            P(),
            P(),
            P(),
            P(),
            P(),
            P(),
            P("batch", "tm", None),
            P("tm", None, None),
            P("tm", None, None),
        ),
        out_specs=(P("batch", "tm", None), P("tm", None, None), P("tm", None, None)),
        check_vma=False,
    )
```
